32 devices in a mesh: gz: 16 (over z, y, core), gx: 2 (over x).
Axes of the slice: x: 2, y: 2, z: 4, core: 2. Of those that a mesh axis runs over, the one named last changes fastest.
Arguments:
- electric_x: float32 [128, 128, 128], P('gz', 'gx'), may hold values from -6 to 6
- electric_y: float32 [128, 128, 128], P('gz', 'gx'), may hold values from -6 to 6
- electric_s: float32 [128, 128, 128], P('gz', 'gx'), may hold values from -6 to 6
- magnetic_x: float32 [128, 128, 128], P('gz', 'gx'), may hold values from -6 to 6
- magnetic_y: float32 [128, 128, 128], P('gz', 'gx'), may hold values from -6 to 6
- magnetic_s: float32 [128, 128, 128], P('gz', 'gx'), may hold values from -6 to 6
- bunch_profile: int32 [128, 128, 128], P('gz', 'gx'), may hold values from 0 to 7
- cell_codes: int32 [128, 128, 128], P('gz', 'gx'), may hold values from 0 to 7
- shift_counts: int32 [3], replicated, may hold values from 0 to 1, as said below
Outputs:
- out_electric_x: float32 [128, 128, 128], P('gz', 'gx')
- out_electric_y: float32 [128, 128, 128], P('gz', 'gx')
- out_electric_s: float32 [128, 128, 128], P('gz', 'gx')
- out_magnetic_x: float32 [128, 128, 128], P('gz', 'gx')
- out_magnetic_y: float32 [128, 128, 128], P('gz', 'gx')
- out_magnetic_s: float32 [128, 128, 128], P('gz', 'gx')
The draws below stay inside these ranges and needn't reach their ends.
Inputs may be any that keep to these rules, and one draw needn't show every extreme that they name: `shift_counts`: each entry is 0 or 1; some entry is 1 and some entry is 0.
All inputs are finite; a program needn't handle non-finite values.
Results may differ from the reference program's by a relative error of at most 0.00002.
Values sent between devices are 32-bit elements; how exact they have to be, the bound alone decides.
No kernel may reach another device: no remote copies, remote signals or barrier semaphores. Data moves between devices by JAX's collectives and lax.ppermute only.
A program may use at most 64 MiB of HBM per device.

```python
import jax
import jax.numpy as jnp
from jax import lax

NY = 128
STEPS = 3
NZ = 128
NX = 128
RADIUS = 256


def draw_shift_counts(key, part):
    key = jax.random.fold_in(key, 7)
    key_flags, key_first, key_offset = jax.random.split(key, 3)
    flags_drawn = jax.random.randint(key_flags, (STEPS,), 0, 2)
    first_place = jax.random.randint(key_first, (), 0, STEPS)
    offset_drawn = jax.random.randint(key_offset, (), 1, STEPS)
    second_place = (first_place + offset_drawn) % STEPS
    places = jnp.arange(STEPS)
    flags_drawn = jnp.where(places == first_place, 1, flags_drawn)
    flags_drawn = jnp.where(places == second_place, 0, flags_drawn)
    return flags_drawn.astype(jnp.int32)


def set_ends(drawn, rng, least, high):
    extent = drawn.shape
    spot = [jax.random.randint(jax.random.fold_in(rng, axis), (), 0, extent[axis]) for axis in range(len(extent))]
    drawn = drawn.at[tuple(spot)].set(least)
    longest = extent.index(max(extent))
    spot[longest] = (spot[longest] + 1) % extent[longest]
    return drawn.at[tuple(spot)].set(high)


def block_levels(own_key, shape, cuts, least, largest):
    level, own = 1.0, jax.random.fold_in(own_key, 6)
    for position, parts in cuts:
        draws = jnp.exp(jax.random.uniform(jax.random.fold_in(own, position), (parts,), jnp.float32, least / len(cuts), largest / len(cuts)))
        level = level * jnp.repeat(draws, shape[position] // parts).reshape([-1 if axis == position else 1 for axis in range(len(shape))])
    return level


def gaussian(key, dims, width, bound, cuts=(), kind=jnp.bfloat16):
    level = block_levels(key, dims, cuts, -0.22, 0.18) if cuts else 1.0
    result = jax.random.normal(key, dims, jnp.float32) * width * level
    return jnp.minimum(jnp.maximum(result, -bound), bound).astype(kind)


def setup_inputs(seed: int = 0) -> dict:
    arg_keys = jax.random.split(jax.random.key(seed), 10)
    return {
        "electric_x": gaussian(arg_keys[0], (NZ, NX, NY), 1.0, 6.0, ((0, 16), (1, 2)), jnp.float32),
        "electric_y": gaussian(arg_keys[1], (NZ, NX, NY), 1.0, 6.0, ((0, 16), (1, 2)), jnp.float32),
        "electric_s": gaussian(arg_keys[2], (NZ, NX, NY), 1.0, 6.0, ((0, 16), (1, 2)), jnp.float32),
        "magnetic_x": gaussian(arg_keys[3], (NZ, NX, NY), 1.0, 6.0, ((0, 16), (1, 2)), jnp.float32),
        "magnetic_y": gaussian(arg_keys[4], (NZ, NX, NY), 1.0, 6.0, ((0, 16), (1, 2)), jnp.float32),
        "magnetic_s": gaussian(arg_keys[5], (NZ, NX, NY), 1.0, 6.0, ((0, 16), (1, 2)), jnp.float32),
        "bunch_profile": set_ends(jax.random.randint(arg_keys[6], (NZ, NX, NY), 0, 8), jax.random.fold_in(arg_keys[6], 1), 0, 7).astype(jnp.int32),
        "cell_codes": set_ends(jax.random.randint(arg_keys[7], (NZ, NX, NY), 0, 8), jax.random.fold_in(arg_keys[7], 1), 0, 7).astype(jnp.int32),
        "shift_counts": draw_shift_counts(jax.random.fold_in(arg_keys[9], 71), 0),
    }


time_step = 0.5
current_scale = 0.1


def forward_diff(values, along):
    size = values.shape[along]
    nxt = lax.slice_in_dim(values, 1, size, axis=along)
    zero_shape = list(values.shape)
    zero_shape[along] = 1
    nxt = jnp.concatenate([nxt, jnp.zeros(zero_shape, values.dtype)], along)
    return nxt - values


def backward_diff(values, along):
    size = values.shape[along]
    prev = lax.slice_in_dim(values, 0, size - 1, axis=along)
    zero_shape = list(values.shape)
    zero_shape[along] = 1
    prev = jnp.concatenate([jnp.zeros(zero_shape, values.dtype), prev], along)
    return values - prev


def move_window(values, shift_now):
    moved = jnp.concatenate([values[1:], jnp.zeros_like(values[:1])], 0)
    return jnp.where(shift_now == 1, moved, values)


def coefficients(cell_codes):
    keep = jnp.where(cell_codes == 5, 0.0, jnp.where(cell_codes == 6, 0.8 / 1.2, jnp.where(cell_codes == 7, 0.4 / 1.6, 1.0)))
    gain = jnp.where(cell_codes == 5, 0.0, jnp.where(cell_codes == 6, time_step / 1.2, jnp.where(cell_codes == 7, time_step / 1.6, time_step)))
    return keep.astype(jnp.float32), gain.astype(jnp.float32)


def reference(electric_x, electric_y, electric_s, magnetic_x, magnetic_y, magnetic_s, bunch_profile, cell_codes, shift_counts):
    places = jnp.arange(NX).astype(jnp.float32)
    scale_whole = (1.0 + (places - NX / 2) / RADIUS)[None, :, None]
    scale_half = (1.0 + (places + 0.5 - NX / 2) / RADIUS)[None, :, None]
    keep, gain = coefficients(cell_codes)
    current = current_scale * bunch_profile.astype(jnp.float32)
    for step_index in range(STEPS):
        shift_now = shift_counts[step_index]
        electric_x = move_window(electric_x, shift_now)
        electric_y = move_window(electric_y, shift_now)
        electric_s = move_window(electric_s, shift_now)
        magnetic_x = move_window(magnetic_x, shift_now)
        magnetic_y = move_window(magnetic_y, shift_now)
        magnetic_s = move_window(magnetic_s, shift_now)
        magnetic_x = magnetic_x - time_step * (forward_diff(electric_s, 2) - forward_diff(electric_y, 0) / scale_whole)
        magnetic_y = magnetic_y - time_step * (forward_diff(electric_x, 0) - forward_diff(scale_whole * electric_s, 1)) / scale_half
        magnetic_s = magnetic_s - time_step * (forward_diff(electric_y, 1) - forward_diff(electric_x, 2))
        electric_x = keep * electric_x + gain * (backward_diff(magnetic_s, 2) - backward_diff(magnetic_y, 0) / scale_half)
        electric_y = keep * electric_y + gain * (backward_diff(magnetic_x, 0) - backward_diff(scale_half * magnetic_s, 1)) / scale_whole
        electric_s = keep * electric_s + gain * (backward_diff(magnetic_y, 1) - backward_diff(magnetic_x, 2) - current)
    return electric_x, electric_y, electric_s, magnetic_x, magnetic_y, magnetic_s
```

```python
import functools

import jax
import jax.numpy as jnp
from jax import lax
from jax.experimental import pallas as pl
from jax.experimental.pallas import tpu as pltpu
from jax.sharding import PartitionSpec as P

STEPS = 3
TILE = 8
HALF = 4
TIME_STEP = 0.5
CURRENT_SCALE = 0.1
VMEM = pl.BlockSpec(memory_space=pltpu.VMEM)
ANY = pl.BlockSpec(memory_space=pl.ANY)
SMEM = pl.BlockSpec(memory_space=pltpu.SMEM)
CODES, BUNCH = 6, 7


def down_counts(moves):
    return (moves + 3, moves + 3) + (moves + 2,) * 5 + (moves + 1,)


def up_counts(moves):
    below = 3 - moves
    return (below,) * 5 + (below - 1, below, below)


def offsets(counts):
    starts = [0]
    for count in counts:
        starts.append(starts[-1] + count)
    return starts


def pack_kernel(moves, sides, *refs):
    fields, bunch, codes = refs[:6], refs[6], refs[7]
    outs = refs[8 : 8 + 2 + 3 * len(sides)]
    down_int, up_int, side_int, sems = refs[8 + 2 + 3 * len(sides) :]
    down, up = outs[:2]
    planes, width = codes.shape[:2]
    downs, ups = down_counts(moves), up_counts(moves)
    down_at, up_at = offsets(downs), offsets(ups)
    arrays = list(fields) + [codes, bunch]
    copies = []

    def copy(source, target):
        item = pltpu.make_async_copy(source, target, sems.at[len(copies)])
        item.start()
        copies.append(item)

    gx = lax.axis_index("gx")
    for a, array in enumerate(arrays):
        whole = a < 6
        if downs[a]:
            goal = down.at[pl.ds(down_at[a], downs[a])] if whole else down_int.at[a - 6, pl.ds(0, downs[a])]
            copy(array.at[pl.ds(0, downs[a])], goal)
        if ups[a]:
            goal = up.at[pl.ds(up_at[a], ups[a])] if whole else up_int.at[a - 6, pl.ds(0, ups[a])]
            copy(array.at[pl.ds(planes - ups[a], ups[a])], goal)
        for n, side in enumerate(sides):
            if side == "swap":
                row = pl.multiple_of(jnp.where(gx == 0, width - TILE, 0), TILE)
            else:
                row = width - TILE if side == "right" else 0
            goal = outs[2 + 3 * n].at[pl.ds(a * planes, planes)] if whole else side_int.at[n, a - 6]
            copy(array.at[:, pl.ds(row, TILE)], goal)
    for item in copies:
        item.wait()
    for a in (CODES, BUNCH):
        if downs[a]:
            down[pl.ds(down_at[a], downs[a])] = down_int[a - 6, pl.ds(0, downs[a])].astype(jnp.float32)
        if ups[a]:
            up[pl.ds(up_at[a], ups[a])] = up_int[a - 6, pl.ds(0, ups[a])].astype(jnp.float32)
    for n in range(len(sides)):
        block, block_down, block_up = outs[2 + 3 * n : 5 + 3 * n]
        for a in (CODES, BUNCH):
            block[pl.ds(a * planes, planes)] = side_int[n, a - 6].astype(jnp.float32)
        for a in range(8):
            if downs[a]:
                block_down[pl.ds(down_at[a], downs[a])] = block[pl.ds(a * planes, downs[a])]
            if ups[a]:
                block_up[pl.ds(up_at[a], ups[a])] = block[pl.ds((a + 1) * planes - ups[a], ups[a])]


def pack(moves, sides, arrays):
    planes, width, depth = arrays[0].shape
    n_down, n_up = sum(down_counts(moves)), sum(up_counts(moves))
    f32 = lambda *shape: jax.ShapeDtypeStruct(shape, jnp.float32)
    shapes = [f32(n_down, width, depth), f32(n_up, width, depth)]
    for _ in sides:
        shapes += [f32(8 * planes, TILE, depth), f32(n_down, TILE, depth), f32(n_up, TILE, depth)]
    return pl.pallas_call(
        functools.partial(pack_kernel, moves, sides),
        out_shape=shapes,
        in_specs=[ANY] * 8,
        out_specs=[VMEM] * len(shapes),
        scratch_shapes=[
            pltpu.VMEM((2, moves + 2, width, depth), jnp.int32),
            pltpu.VMEM((2, 3 - moves, width, depth), jnp.int32),
            pltpu.VMEM((len(sides), 2, planes, TILE, depth), jnp.int32),
            pltpu.SemaphoreType.DMA((8 * (2 + len(sides)),)),
        ],
        compiler_params=pltpu.CompilerParams(vmem_limit_bytes=24 * 2**20),
        name="pack",
    )(*arrays)


def coefficients(code):
    kind = code.dtype.type
    five, six, seven = code == kind(5), code == kind(6), code == kind(7)
    keep = jnp.where(five, 0.0, jnp.where(six, 0.8 / 1.2, jnp.where(seven, 0.4 / 1.6, 1.0)))
    gain = jnp.where(
        five,
        0.0,
        jnp.where(six, TIME_STEP / 1.2, jnp.where(seven, TIME_STEP / 1.6, TIME_STEP)),
    )
    return keep, gain


def steps_kernel(moves, moved, *refs):
    local, bunch, codes = refs[:6], refs[6], refs[7]
    down, up, side, side_down, side_up = refs[8:13]
    outs = refs[13:19]
    ext, keep, gain, current, rows = refs[19:]
    planes, width, depth = codes.shape
    tall = width + TILE
    gz, gx = lax.axis_index("gz"), lax.axis_index("gx")
    first = gz == 0
    last = gz == lax.axis_size("gz") - 1
    total = width * lax.axis_size("gx")
    start = gx * width
    downs, ups = down_counts(moves), up_counts(moves)
    down_at, up_at = offsets(downs), offsets(ups)
    base = 3 - moves

    row = lax.broadcasted_iota(jnp.int32, (tall, depth), 0)
    place = start + jnp.where(row < width + HALF, row, row - tall)
    inside = (place >= 0) & (place < total)
    place = place.astype(jnp.float32)
    whole = 1.0 + (place - total / 2) / (2 * total)
    half = 1.0 + (place + 0.5 - total / 2) / (2 * total)
    step = jnp.where(inside, TIME_STEP, 0.0)
    for n, value in enumerate((whole, half, 1.0 / whole, 1.0 / half, step, step / whole, step / half)):
        rows[n] = value
    ghost_in = inside[width:]

    own = pl.ds(0, width)
    edge = pl.ds(width, TILE)

    def spread(a, store):
        n_down, n_up = downs[a], ups[a]
        local_ref = (list(local) + [codes, bunch])[a]
        store(base, planes, own, local_ref[...], None)
        store(base, planes, edge, side[pl.ds(a * planes, planes)], ghost_in)
        if n_down:
            store(base + planes, n_down, own, down[pl.ds(down_at[a], n_down)], None)
            store(base + planes, n_down, edge, side_down[pl.ds(down_at[a], n_down)], ghost_in)
        if n_up:
            store(base - n_up, n_up, own, up[pl.ds(up_at[a], n_up)], None)
            store(base - n_up, n_up, edge, side_up[pl.ds(up_at[a], n_up)], ghost_in)

    for a in range(6):

        def store_field(at, count, where, value, mask):
            if mask is not None:
                value = jnp.where(mask[None], value, 0.0)
            ext[a, pl.ds(at, count), where] = value

        spread(a, store_field)

    def store_codes(at, count, where, value, mask):
        kept, gained = coefficients(value)
        if mask is not None:
            kept, gained = jnp.where(mask[None], kept, 0.0), jnp.where(mask[None], gained, 0.0)
        keep[pl.ds(at, count), where] = kept
        gain[pl.ds(at, count), where] = gained

    def store_bunch(at, count, where, value, mask):
        current[pl.ds(at, count), where] = CURRENT_SCALE * value.astype(jnp.float32)

    spread(CODES, store_codes)
    spread(BUNCH, store_bunch)

    lane = lax.broadcasted_iota(jnp.int32, (tall, depth), 1)
    not_last, not_first = lane < depth - 1, lane > 0

    def forward_y(v):
        return jnp.where(not_last, pltpu.roll(v, depth - 1, 1), 0.0) - v

    def backward_y(v):
        return v - jnp.where(not_first, pltpu.roll(v, 1, 1), 0.0)

    def forward_x(v):
        return pltpu.roll(v, tall - 1, 0) - v

    def backward_x(v):
        return v - pltpu.roll(v, 1, 0)

    def magnetic(e):
        ex, ey, es = ext[0, e], ext[1, e], ext[2, e]
        bx = ext[3, e] - (rows[4] * forward_y(es) - rows[5] * (ext[1, e + 1] - ey))
        by = ext[4, e] - rows[6] * ((ext[0, e + 1] - ex) - forward_x(rows[0] * es))
        bs = ext[5, e] - rows[4] * (forward_x(ey) - forward_y(ex))
        return ex, ey, es, bx, by, bs

    moved_now = 0
    for t in range(STEPS):
        moved_now = moved_now + moved[t]
        begin = jnp.where(first, base + moved_now, t + 1)
        end = jnp.where(last, jnp.minimum(planes + 4 - t, planes + 2 + moved_now - moves), planes + 4 - t) + 1
        _, _, _, bx, by, _ = magnetic(t)
        ext[3, t], ext[4, t] = bx, by

        @pl.when(first)
        def _():
            ext[3, begin - 1] = jnp.zeros((tall, depth), jnp.float32)
            ext[4, begin - 1] = jnp.zeros((tall, depth), jnp.float32)

        def plane(e, carry):
            ex, ey, es, bx, by, bs = magnetic(e)
            kept, gained = keep[e - moved_now], gain[e - moved_now]
            ex = kept * ex + gained * (backward_y(bs) - rows[3] * (by - ext[4, e - 1]))
            ey = kept * ey + gained * (rows[2] * ((bx - ext[3, e - 1]) - backward_x(rows[1] * bs)))
            es = kept * es + gained * (backward_x(by) - backward_y(bx) - current[e - moved_now])
            for a, value in enumerate((ex, ey, es, bx, by, bs)):
                if t < STEPS - 1:
                    ext[a, e] = value
                else:
                    outs[a][e - 3] = value[:width]
                    if a in (3, 4):
                        ext[a, e] = value
            return carry

        lax.fori_loop(begin, end, plane, 0)


def advance(moves, moved, arrays, ghosts):
    planes, width, depth = arrays[0].shape
    tall = width + TILE
    block = jax.ShapeDtypeStruct((planes, width, depth), jnp.float32)
    return pl.pallas_call(
        lambda moved, *refs: steps_kernel(moves, moved, *refs),
        out_shape=[block] * 6,
        in_specs=[SMEM] + [VMEM] * 13,
        out_specs=[VMEM] * 6,
        scratch_shapes=[
            pltpu.VMEM((6, planes + 6, tall, depth), jnp.float32),
            pltpu.VMEM((planes + 5, tall, depth), jnp.float32),
            pltpu.VMEM((planes + 5, tall, depth), jnp.float32),
            pltpu.VMEM((planes + 5, tall, depth), jnp.float32),
            pltpu.VMEM((7, tall, depth), jnp.float32),
        ],
        compiler_params=pltpu.CompilerParams(vmem_limit_bytes=32 * 2**20),
        name="steps",
    )(moved, *arrays, *ghosts)


def exchange(moves, sides, packed):
    size_z, size_x = lax.axis_size("gz"), lax.axis_size("gx")

    def passed(block, dz, side):
        steps_x = {"swap": (1, -1), "right": (1,), "left": (-1,), None: (0,)}[side]
        route = [
            (z * size_x + x, (z + dz) * size_x + x + dx)
            for z in range(size_z)
            for x in range(size_x)
            for dx in steps_x
            if 0 <= z + dz < size_z and 0 <= x + dx < size_x
        ]
        return lax.ppermute(block, ("gz", "gx"), route)

    down, up = passed(packed[0], -1, None), passed(packed[1], 1, None)
    found = []
    for n, side in enumerate(sides):
        block, block_down, block_up = packed[2 + 3 * n : 5 + 3 * n]
        found.append((passed(block, 0, side), passed(block_down, -1, side), passed(block_up, 1, side)))
    if len(sides) == 2:
        from_left, from_right = found
        row = lax.broadcasted_iota(jnp.int32, (1, TILE, 1), 1)
        merged = [jnp.where(row < HALF, r, l) for l, r in zip(from_left, from_right)]
    else:
        merged = list(found[0])
    return [down, up] + merged


def on_device(*args):
    arrays, moved = args[:8], args[8]
    sides = ("swap",) if lax.axis_size("gx") == 2 else ("right", "left")

    def run(moves, arrays, moved):
        packed = pack(moves, sides, arrays)
        ghosts = exchange(moves, sides, packed)
        return tuple(advance(moves, moved, arrays, ghosts))

    return lax.cond(
        jnp.sum(moved) == 2,
        functools.partial(run, 2),
        functools.partial(run, 1),
        arrays,
        moved,
    )


def solution(mesh):
    block = P("gz", "gx", None)
    return jax.shard_map(
        on_device,
        mesh=mesh,
        in_specs=(block,) * 8 + (P(),),
        out_specs=(block,) * 6,
        check_vma=False,
    )
```

```python
import functools

import jax
import jax.numpy as jnp
from jax import lax
from jax.experimental import pallas as pl
from jax.experimental.pallas import tpu as pltpu
from jax.sharding import PartitionSpec as P

STEPS = 3
TILE = 8
HALF = 4
TIME_STEP = 0.5
CURRENT_SCALE = 0.1
VMEM = pl.BlockSpec(memory_space=pltpu.VMEM)
SMEM = pl.BlockSpec(memory_space=pltpu.SMEM)
ANY = pl.BlockSpec(memory_space=pl.ANY)
EX, EY, ES, BX, BY, BS, CODES, BUNCH = range(8)
CASES = ((1, 1), (1, 0), (2, 1), (2, 0))


def down_counts(case):
    moves, now = case
    later = moves - now
    return (moves + 2,) * 6 + (later + 2, later + 1)


def up_counts(case):
    moves, now = case
    below = 3 - moves
    later = moves - now
    return (below - 1, below - 1, below, below, below, below - 1, 2 - later, 2 - later)


def offsets(counts):
    starts = [0]
    for count in counts:
        starts.append(starts[-1] + count)
    return starts


def half_up(count):
    return (count + 1) // 2


def column_scales(place, total):
    place = place.astype(jnp.float32)
    whole = 1.0 + (place - total / 2) / (2 * total)
    half = 1.0 + (place + 0.5 - total / 2) / (2 * total)
    return whole, half


def turned(tiles):
    return pltpu.roll(tiles, HALF, 1)


def pack_kernel(sides, *refs):
    sources, moved = refs[:8], refs[8]
    own = refs[9:17]
    which = refs[17]
    across = refs[18 : 18 + len(sides)]
    sent = refs[18 + len(sides) : -3]
    moved_here, sems, moved_sem = refs[-3:]
    per_case = 2 + 2 * len(sides)
    planes, width, depth = own[0].shape
    gx = lax.axis_index("gx")
    total = width * lax.axis_size("gx")

    get_moved = pltpu.make_async_copy(moved, moved_here, moved_sem)
    get_moved.start()
    copies = [pltpu.make_async_copy(sources[a], own[a], sems.at[a]) for a in range(8)]
    for item in copies:
        item.start()
    get_moved.wait()
    now = moved_here[0]
    later = moved_here[1] + moved_here[2]
    case_index = jnp.where(now + later == 1, 1 - now, 3 - now)
    which[0] = case_index

    row = lax.broadcasted_iota(jnp.int32, (width, depth), 0)
    whole, half = column_scales(gx * width + row, total)
    step_whole, step_half = TIME_STEP / whole, TIME_STEP / half
    low = lax.broadcasted_iota(jnp.int32, (1, TILE, depth), 1) < HALF

    def edge_of(side):
        if side == "swap":
            return pl.multiple_of(jnp.where(gx == 0, width - TILE, 0), TILE), gx == 0
        return (width - TILE, True) if side == "right" else (0, False)

    def paired(first, second, high):
        if high is True:
            return jnp.where(low, turned(first), second)
        if high is False:
            return jnp.where(low, first, turned(second))
        return jnp.where(
            low,
            jnp.where(high, turned(first), first),
            jnp.where(high, second, turned(second)),
        )

    for item in copies:
        item.wait()

    for n, side in enumerate(sides):
        at, high = edge_of(side)
        for a in range(4):
            first = own[a][:, pl.ds(at, TILE)]
            second = own[a + 4][:, pl.ds(at, TILE)].astype(jnp.float32)
            across[n][pl.ds(a * planes, planes)] = paired(first, second, high)

    for c, case in enumerate(CASES):
        down, up = sent[c * per_case : c * per_case + 2]
        corners = sent[c * per_case + 2 : (c + 1) * per_case]
        downs, ups = down_counts(case), up_counts(case)
        down_at, up_at = offsets(downs), offsets(ups)
        moves = case[0]

        @pl.when(case_index == c)
        def _():
            for a in range(8):
                if downs[a]:
                    down[pl.ds(down_at[a], downs[a])] = own[a][: downs[a]].astype(jnp.float32)
                if ups[a]:
                    up[pl.ds(up_at[a], ups[a])] = own[a][planes - ups[a] :].astype(jnp.float32)
            far = moves + 2
            down[down_at[BX] + far - 1] = own[BX][far - 1] + step_whole * own[EY][far]
            down[down_at[BY] + far - 1] = own[BY][far - 1] - step_half * own[EX][far]
            far = planes - (3 - moves)
            up[up_at[BX]] = own[BX][far] - step_whole * own[EY][far]
            up[up_at[BY]] = own[BY][far] + step_half * own[EX][far]
            for n, side in enumerate(sides):
                at, high = edge_of(side)
                for block, corner, count in (
                    (down, corners[2 * n], down_at[-1]),
                    (up, corners[2 * n + 1], up_at[-1]),
                ):
                    middle = half_up(count)
                    rest = count - middle
                    first = block[pl.ds(0, middle), pl.ds(at, TILE)]
                    second = block[pl.ds(middle, rest), pl.ds(at, TILE)]
                    corner[pl.ds(0, rest)] = paired(first[:rest], second, high)
                    if rest < middle:
                        corner[pl.ds(rest, 1)] = paired(first[rest:], first[rest:], high)


def pack(sides, arrays, moved):
    planes, width, depth = arrays[0].shape
    vmem = lambda *shape: pltpu.VMEM(shape, jnp.float32)
    shapes = [pltpu.VMEM(a.shape, a.dtype) for a in arrays] + [pltpu.SMEM((1,), jnp.int32)]
    shapes += [vmem(4 * planes, TILE, depth)] * len(sides)
    for case in CASES:
        n_down, n_up = sum(down_counts(case)), sum(up_counts(case))
        shapes += [vmem(n_down, width, depth), vmem(n_up, width, depth)]
        shapes += [vmem(half_up(n_down), TILE, depth), vmem(half_up(n_up), TILE, depth)] * len(sides)
    found = pl.pallas_call(
        functools.partial(pack_kernel, sides),
        out_shape=shapes,
        in_specs=[ANY] * 9,
        out_specs=[VMEM] * 8 + [SMEM] + [VMEM] * (len(shapes) - 9),
        scratch_shapes=[
            pltpu.SMEM((STEPS,), jnp.int32),
            pltpu.SemaphoreType.DMA((8,)),
            pltpu.SemaphoreType.DMA,
        ],
        compiler_params=pltpu.CompilerParams(vmem_limit_bytes=32 * 2**20),
        name="pack",
    )(*arrays, moved)
    own, which, rest = found[:8], found[8], found[9:]
    across, sent = rest[: len(sides)], rest[len(sides) :]
    per_case = 2 + 2 * len(sides)
    return own, which, across, [sent[c * per_case : (c + 1) * per_case] for c in range(len(CASES))]


def coefficients(code):
    kind = code.dtype.type
    five, six, seven = code == kind(5), code == kind(6), code == kind(7)
    keep = jnp.where(five, 0.0, jnp.where(six, 0.8 / 1.2, jnp.where(seven, 0.4 / 1.6, 1.0)))
    gain = jnp.where(
        five,
        0.0,
        jnp.where(six, TIME_STEP / 1.2, jnp.where(seven, TIME_STEP / 1.6, TIME_STEP)),
    )
    return keep, gain


def ghost_inside(width, depth):
    gx = lax.axis_index("gx")
    row = lax.broadcasted_iota(jnp.int32, (1, TILE, depth), 1)
    right = gx < lax.axis_size("gx") - 1
    return jnp.where(row < HALF, right.astype(jnp.int32), (gx > 0).astype(jnp.int32)) == 1


def prepare_kernel(moves, *refs):
    own, (ext, keep, gain, current, rows) = refs[:8], refs[8:]
    planes, width, depth = own[0].shape
    tall = width + TILE
    base = 3 - moves
    total = width * lax.axis_size("gx")

    row = lax.broadcasted_iota(jnp.int32, (tall, depth), 0)
    place = lax.axis_index("gx") * width + jnp.where(row < width + HALF, row, row - tall)
    inside = (place >= 0) & (place < total)
    whole, half = column_scales(place, total)
    step = jnp.where(inside, TIME_STEP, 0.0)
    for n, value in enumerate((whole, half, 1.0 / whole, 1.0 / half, step, step / whole, step / half)):
        rows[n] = value
    here, mine = pl.ds(base, planes), pl.ds(0, width)
    for a in range(6):
        ext[a, here, mine] = own[a][...]
    keep[here, mine], gain[here, mine] = coefficients(own[CODES][...])
    current[here, mine] = CURRENT_SCALE * own[BUNCH][...].astype(jnp.float32)
    for a in (EX, EY):
        ext[a, 0] = jnp.zeros((tall, depth), jnp.float32)
        ext[a, planes + 5] = jnp.zeros((tall, depth), jnp.float32)


def prepare(moves, own):
    planes, width, depth = own[0].shape
    tall = width + TILE
    vmem = lambda *shape: pltpu.VMEM(shape, jnp.float32)
    cells = vmem(planes + 5, tall, depth)
    return pl.pallas_call(
        functools.partial(prepare_kernel, moves),
        out_shape=[vmem(6, planes + 6, tall, depth), cells, cells, cells, vmem(7, tall, depth)],
        in_specs=[VMEM] * 8,
        out_specs=[VMEM] * 5,
        compiler_params=pltpu.CompilerParams(vmem_limit_bytes=32 * 2**20),
        cost_estimate=pl.CostEstimate(flops=10**7, bytes_accessed=10**7, transcendentals=0),
        name="prepare",
    )(*own)


def steps_kernel(case, n_sides, moved, *refs):
    rows = refs[4]
    down, up = refs[5:7]
    beside = [refs[7 + 3 * n : 10 + 3 * n] for n in range(n_sides)]
    outs = refs[7 + 3 * n_sides : 13 + 3 * n_sides]
    ext, keep, gain, current = refs[13 + 3 * n_sides : 17 + 3 * n_sides]
    final, sems = refs[17 + 3 * n_sides :]
    moves = case[0]
    base = 3 - moves
    _, planes, width, depth = final.shape
    tall = width + TILE
    gz, gx = lax.axis_index("gz"), lax.axis_index("gx")
    first = gz == 0
    last = gz == lax.axis_size("gz") - 1
    downs, ups = down_counts(case), up_counts(case)
    down_at, up_at = offsets(downs), offsets(ups)
    ghost_in = ghost_inside(width, depth)
    low = lax.broadcasted_iota(jnp.int32, (1, TILE, depth), 1) < HALF

    def spread_tiles(kind, at, count, upper):
        tiles = [side[kind][pl.ds(at, count)] for side in beside]
        if n_sides == 1:
            same = (gx > 0) if upper else (gx == 0)
            found = jnp.where(same, tiles[0], turned(tiles[0]))
        else:
            from_left, from_right = tiles
            if upper:
                from_right = turned(from_right)
            else:
                from_left = turned(from_left)
            found = jnp.where(low, from_right, from_left)
        return jnp.where(ghost_in, found, 0.0)

    def pieces(kind, at, count, middle):
        cut = min(max(middle - at, 0), count)
        if cut:
            yield 0, cut, spread_tiles(kind, at, cut, False)
        if cut < count:
            yield cut, count - cut, spread_tiles(kind, at + cut - middle, count - cut, True)

    def put(a, at, count, where, value):
        span = pl.ds(at, count)
        if a < 6:
            ext[a, span, where] = value
        elif a == CODES:
            kept, gained = coefficients(value)
            if where.start:
                kept, gained = jnp.where(ghost_in, kept, 0.0), jnp.where(ghost_in, gained, 0.0)
            keep[span, where] = kept
            gain[span, where] = gained
        else:
            current[span, where] = CURRENT_SCALE * value

    mine, edge = pl.ds(0, width), pl.ds(width, TILE)
    for a in range(8):
        for at, count, value in pieces(0, a * planes, planes, 4 * planes):
            put(a, base + at, count, edge, value)
        for block, kind, counts, starts, to in (
            (down, 1, downs, down_at, base + planes),
            (up, 2, ups, up_at, base - ups[a]),
        ):
            if counts[a]:
                put(a, to, counts[a], mine, block[pl.ds(starts[a], counts[a])])
                for at, count, value in pieces(kind, starts[a], counts[a], half_up(starts[-1])):
                    put(a, to + at, count, edge, value)

    lane = lax.broadcasted_iota(jnp.int32, (tall, depth), 1)
    not_last, not_first = lane < depth - 1, lane > 0

    def forward_y(v):
        return jnp.where(not_last, pltpu.roll(v, depth - 1, 1), 0.0) - v

    def backward_y(v):
        return v - jnp.where(not_first, pltpu.roll(v, 1, 1), 0.0)

    def forward_x(v):
        return pltpu.roll(v, tall - 1, 0) - v

    def backward_x(v):
        return v - pltpu.roll(v, 1, 0)

    def magnetic(e):
        ex, ey, es = ext[EX, e], ext[EY, e], ext[ES, e]
        bx = ext[BX, e] - (rows[4] * forward_y(es) - rows[5] * (ext[EY, e + 1] - ey))
        by = ext[BY, e] - rows[6] * ((ext[EX, e + 1] - ex) - forward_x(rows[0] * es))
        bs = ext[BS, e] - rows[4] * (forward_x(ey) - forward_y(ex))
        return ex, ey, es, bx, by, bs

    def out_copy(a, plane):
        return pltpu.make_async_copy(final.at[a, plane], outs[a].at[plane], sems.at[a, plane])

    moved_now = 0
    for t in range(STEPS):
        moved_now = moved_now + moved[t]
        begin = jnp.where(first, base + moved_now, t + 1)
        end = jnp.where(last, jnp.minimum(planes + 4 - t, planes + 2 + moved_now - moves), planes + 4 - t) + 1
        _, _, _, bx, by, _ = magnetic(t)
        ext[BX, t], ext[BY, t] = bx, by

        @pl.when(first)
        def _():
            ext[BX, begin - 1] = jnp.zeros((tall, depth), jnp.float32)
            ext[BY, begin - 1] = jnp.zeros((tall, depth), jnp.float32)

        def plane(e, carry):
            ex, ey, es, bx, by, bs = magnetic(e)
            kept, gained = keep[e - moved_now], gain[e - moved_now]
            ex = kept * ex + gained * (backward_y(bs) - rows[3] * (by - ext[BY, e - 1]))
            ey = kept * ey + gained * (rows[2] * ((bx - ext[BX, e - 1]) - backward_x(rows[1] * bs)))
            es = kept * es + gained * (backward_x(by) - backward_y(bx) - current[e - moved_now])
            for a, value in enumerate((ex, ey, es, bx, by, bs)):
                if t < STEPS - 1:
                    ext[a, e] = value
                else:
                    final[a, e - 3] = value[:width]
                    if a in (BX, BY):
                        ext[a, e] = value
            if t == STEPS - 1:
                for a in range(6):
                    out_copy(a, e - 3).start()
            return carry

        lax.fori_loop(begin, end, plane, 0)

    def finish(plane, carry):
        for a in range(6):
            out_copy(a, plane).wait()
        return carry

    lax.fori_loop(0, planes, finish, 0)


def advance(case, moved, shape, ready, ghosts):
    planes, width, depth = shape
    block = jax.ShapeDtypeStruct(shape, jnp.float32)
    n_in = 6 + len(ghosts)
    like = lambda x: pltpu.VMEM(x.shape, x.dtype)
    found = pl.pallas_call(
        functools.partial(steps_kernel, case, (len(ghosts) - 2) // 3),
        out_shape=[block] * 6 + [like(x) for x in ready[:4]],
        in_specs=[SMEM] + [VMEM] * (n_in - 1),
        out_specs=[ANY] * 6 + [VMEM] * 4,
        input_output_aliases={1: 6, 2: 7, 3: 8, 4: 9},
        scratch_shapes=[
            pltpu.VMEM((6, planes, width, depth), jnp.float32),
            pltpu.SemaphoreType.DMA((6, planes)),
        ],
        compiler_params=pltpu.CompilerParams(vmem_limit_bytes=32 * 2**20),
        name="steps",
    )(moved, *ready, *ghosts)
    return tuple(found[:6])


def passed(block, dz, side):
    size_z, size_x = lax.axis_size("gz"), lax.axis_size("gx")
    steps_x = {"swap": (1, -1), "right": (1,), "left": (-1,), None: (0,)}[side]
    route = [
        (z * size_x + x, (z + dz) * size_x + x + dx)
        for z in range(size_z)
        for x in range(size_x)
        for dx in steps_x
        if 0 <= z + dz < size_z and 0 <= x + dx < size_x
    ]
    return lax.ppermute(block, ("gz", "gx"), route)


def on_device(*args):
    arrays, moved = args[:8], args[8]
    arrays = arrays[:6] + (arrays[7], arrays[6])
    sides = ("swap",) if lax.axis_size("gx") == 2 else ("right", "left")
    own, which, across, sent = pack(sides, arrays, moved)

    def run(c, own, across, sent, moved):
        case = CASES[c]
        blocks = sent[c]
        ghosts = [passed(blocks[0], -1, None), passed(blocks[1], 1, None)]
        for n, side in enumerate(sides):
            ghosts.append(passed(across[n], 0, side))
            ghosts.append(passed(blocks[2 + 2 * n], -1, side))
            ghosts.append(passed(blocks[3 + 2 * n], 1, side))
        ready = prepare(case[0], own)
        return advance(case, moved, own[0].shape, ready, ghosts)

    return lax.switch(
        which[0],
        [functools.partial(run, c) for c in range(len(CASES))],
        own,
        across,
        sent,
        moved,
    )


def solution(mesh):
    block = P("gz", "gx", None)
    return jax.shard_map(
        on_device,
        mesh=mesh,
        in_specs=(block,) * 8 + (P(),),
        out_specs=(block,) * 6,
        check_vma=False,
    )
```

```python
import functools

import jax
import jax.numpy as jnp
from jax import lax
from jax.experimental import pallas as pl
from jax.experimental.pallas import tpu as pltpu
from jax.sharding import PartitionSpec as P

STEPS = 3
TILE = 8
HALF = 4
GROUP = 4
TIME_STEP = 0.5
CURRENT_SCALE = 0.1
VMEM = pl.BlockSpec(memory_space=pltpu.VMEM)
SMEM = pl.BlockSpec(memory_space=pltpu.SMEM)
ANY = pl.BlockSpec(memory_space=pl.ANY)
EX, EY, ES, BX, BY, BS, CODES, BUNCH = range(8)
CASES = ((1, 1), (1, 0), (2, 1), (2, 0))


def down_counts(case):
    moves, now = case
    later = moves - now
    return (moves + 2,) * 6 + (later + 2, later + 1)


def up_counts(case):
    moves, now = case
    below = 3 - moves
    later = moves - now
    return (below - 1, below - 1, below, below, below, below - 1, 2 - later, 2 - later)


def offsets(counts):
    starts = [0]
    for count in counts:
        starts.append(starts[-1] + count)
    return starts


def half_up(count):
    return (count + 1) // 2


def column_scales(place, total):
    place = place.astype(jnp.float32)
    whole = 1.0 + (place - total / 2) / (2 * total)
    half = 1.0 + (place + 0.5 - total / 2) / (2 * total)
    return whole, half


def turned(tiles):
    return pltpu.roll(tiles, HALF, 1)


def pack_kernel(sides, *refs):
    sources, moved = refs[:8], refs[8]
    own = refs[9:17]
    which = refs[17]
    across = refs[18 : 18 + len(sides)]
    sent = refs[18 + len(sides) : -3]
    moved_here, sems, moved_sem = refs[-3:]
    per_case = 2 + 2 * len(sides)
    planes, width, depth = own[0].shape
    gx = lax.axis_index("gx")
    total = width * lax.axis_size("gx")

    get_moved = pltpu.make_async_copy(moved, moved_here, moved_sem)
    get_moved.start()
    copies = [pltpu.make_async_copy(sources[a], own[a], sems.at[a]) for a in range(8)]
    for item in copies:
        item.start()
    get_moved.wait()
    now = moved_here[0]
    later = moved_here[1] + moved_here[2]
    case_index = jnp.where(now + later == 1, 1 - now, 3 - now)
    which[0] = case_index

    row = lax.broadcasted_iota(jnp.int32, (width, depth), 0)
    whole, half = column_scales(gx * width + row, total)
    step_whole, step_half = TIME_STEP / whole, TIME_STEP / half
    low = lax.broadcasted_iota(jnp.int32, (1, TILE, depth), 1) < HALF

    def edge_of(side):
        if side == "swap":
            return pl.multiple_of(jnp.where(gx == 0, width - TILE, 0), TILE), gx == 0
        return (width - TILE, True) if side == "right" else (0, False)

    def paired(first, second, high):
        if high is True:
            return jnp.where(low, turned(first), second)
        if high is False:
            return jnp.where(low, first, turned(second))
        return jnp.where(
            low,
            jnp.where(high, turned(first), first),
            jnp.where(high, second, turned(second)),
        )

    for item in copies:
        item.wait()

    for n, side in enumerate(sides):
        at, high = edge_of(side)
        for a in range(4):
            first = own[a][:, pl.ds(at, TILE)]
            second = own[a + 4][:, pl.ds(at, TILE)].astype(jnp.float32)
            across[n][pl.ds(a * planes, planes)] = paired(first, second, high)

    for c, case in enumerate(CASES):
        down, up = sent[c * per_case : c * per_case + 2]
        corners = sent[c * per_case + 2 : (c + 1) * per_case]
        downs, ups = down_counts(case), up_counts(case)
        down_at, up_at = offsets(downs), offsets(ups)
        moves = case[0]

        @pl.when(case_index == c)
        def _():
            for a in range(8):
                if downs[a]:
                    down[pl.ds(down_at[a], downs[a])] = own[a][: downs[a]].astype(jnp.float32)
                if ups[a]:
                    up[pl.ds(up_at[a], ups[a])] = own[a][planes - ups[a] :].astype(jnp.float32)
            far = moves + 2
            down[down_at[BX] + far - 1] = own[BX][far - 1] + step_whole * own[EY][far]
            down[down_at[BY] + far - 1] = own[BY][far - 1] - step_half * own[EX][far]
            far = planes - (3 - moves)
            up[up_at[BX]] = own[BX][far] - step_whole * own[EY][far]
            up[up_at[BY]] = own[BY][far] + step_half * own[EX][far]
            for n, side in enumerate(sides):
                at, high = edge_of(side)
                for block, corner, count in (
                    (down, corners[2 * n], down_at[-1]),
                    (up, corners[2 * n + 1], up_at[-1]),
                ):
                    middle = half_up(count)
                    rest = count - middle
                    first = block[pl.ds(0, middle), pl.ds(at, TILE)]
                    second = block[pl.ds(middle, rest), pl.ds(at, TILE)]
                    corner[pl.ds(0, rest)] = paired(first[:rest], second, high)
                    if rest < middle:
                        corner[pl.ds(rest, 1)] = paired(first[rest:], first[rest:], high)


def pack(sides, arrays, moved):
    planes, width, depth = arrays[0].shape
    vmem = lambda *shape: pltpu.VMEM(shape, jnp.float32)
    shapes = [pltpu.VMEM(a.shape, a.dtype) for a in arrays] + [pltpu.SMEM((1,), jnp.int32)]
    shapes += [vmem(4 * planes, TILE, depth)] * len(sides)
    for case in CASES:
        n_down, n_up = sum(down_counts(case)), sum(up_counts(case))
        shapes += [vmem(n_down, width, depth), vmem(n_up, width, depth)]
        shapes += [vmem(half_up(n_down), TILE, depth), vmem(half_up(n_up), TILE, depth)] * len(sides)
    found = pl.pallas_call(
        functools.partial(pack_kernel, sides),
        out_shape=shapes,
        in_specs=[ANY] * 9,
        out_specs=[VMEM] * 8 + [SMEM] + [VMEM] * (len(shapes) - 9),
        scratch_shapes=[
            pltpu.SMEM((STEPS,), jnp.int32),
            pltpu.SemaphoreType.DMA((8,)),
            pltpu.SemaphoreType.DMA,
        ],
        compiler_params=pltpu.CompilerParams(vmem_limit_bytes=32 * 2**20),
        name="pack",
    )(*(pltpu.with_memory_space_constraint(a, pltpu.HBM) for a in (*arrays, moved)))
    own, which, rest = found[:8], found[8], found[9:]
    across, sent = rest[: len(sides)], rest[len(sides) :]
    per_case = 2 + 2 * len(sides)
    return own, which, across, [sent[c * per_case : (c + 1) * per_case] for c in range(len(CASES))]


def coefficients(code):
    kind = code.dtype.type
    five, six, seven = code == kind(5), code == kind(6), code == kind(7)
    keep = jnp.where(five, 0.0, jnp.where(six, 0.8 / 1.2, jnp.where(seven, 0.4 / 1.6, 1.0)))
    gain = jnp.where(
        five,
        0.0,
        jnp.where(six, TIME_STEP / 1.2, jnp.where(seven, TIME_STEP / 1.6, TIME_STEP)),
    )
    return keep, gain


def ghost_inside(width, depth):
    gx = lax.axis_index("gx")
    row = lax.broadcasted_iota(jnp.int32, (1, TILE, depth), 1)
    right = gx < lax.axis_size("gx") - 1
    return jnp.where(row < HALF, right.astype(jnp.int32), (gx > 0).astype(jnp.int32)) == 1


def prepare_kernel(moves, *refs):
    own, ext, (keep, gain, current, rows) = refs[:8], refs[8:14], refs[14:]
    planes, width, depth = own[0].shape
    tall = width + TILE
    base = 3 - moves
    total = width * lax.axis_size("gx")

    row = lax.broadcasted_iota(jnp.int32, (tall, depth), 0)
    place = lax.axis_index("gx") * width + jnp.where(row < width + HALF, row, row - tall)
    inside = (place >= 0) & (place < total)
    whole, half = column_scales(place, total)
    step = jnp.where(inside, TIME_STEP, 0.0)
    for n, value in enumerate((whole, half, 1.0 / whole, 1.0 / half, step, step / whole, step / half)):
        rows[n] = value
    here, mine = pl.ds(base, planes), pl.ds(0, width)
    for a in range(6):
        ext[a][here, mine] = own[a][...]
    keep[here, mine], gain[here, mine] = coefficients(own[CODES][...])
    current[here, mine] = CURRENT_SCALE * own[BUNCH][...].astype(jnp.float32)
    for a in (EX, EY):
        ext[a][0] = jnp.zeros((tall, depth), jnp.float32)
        ext[a][planes + 5] = jnp.zeros((tall, depth), jnp.float32)


def prepare(moves, own):
    planes, width, depth = own[0].shape
    tall = width + TILE
    vmem = lambda *shape: pltpu.VMEM(shape, jnp.float32)
    cells = vmem(planes + 5, tall, depth)
    return pl.pallas_call(
        functools.partial(prepare_kernel, moves),
        out_shape=[vmem(planes + 6, tall, depth)] * 6 + [cells] * 3 + [vmem(7, tall, depth)],
        in_specs=[VMEM] * 8,
        out_specs=[VMEM] * 10,
        compiler_params=pltpu.CompilerParams(vmem_limit_bytes=32 * 2**20),
        cost_estimate=pl.CostEstimate(flops=10**7, bytes_accessed=10**7, transcendentals=0),
        name="prepare",
    )(*own)


def steps_kernel(case, n_sides, moved, *refs):
    rows = refs[9]
    down, up = refs[10:12]
    beside = [refs[12 + 3 * n : 15 + 3 * n] for n in range(n_sides)]
    at = 12 + 3 * n_sides
    outs, ext = refs[at : at + 6], refs[at + 6 : at + 12]
    keep, gain, current, final, sems = refs[at + 12 :]
    moves = case[0]
    base = 3 - moves
    _, planes, width, depth = final.shape
    tall = width + TILE
    gz, gx = lax.axis_index("gz"), lax.axis_index("gx")
    first = gz == 0
    last = gz == lax.axis_size("gz") - 1
    downs, ups = down_counts(case), up_counts(case)
    down_at, up_at = offsets(downs), offsets(ups)
    ghost_in = ghost_inside(width, depth)
    low = lax.broadcasted_iota(jnp.int32, (1, TILE, depth), 1) < HALF

    def spread_tiles(kind, at, count, upper):
        tiles = [side[kind][pl.ds(at, count)] for side in beside]
        if n_sides == 1:
            same = (gx > 0) if upper else (gx == 0)
            found = jnp.where(same, tiles[0], turned(tiles[0]))
        else:
            from_left, from_right = tiles
            if upper:
                from_right = turned(from_right)
            else:
                from_left = turned(from_left)
            found = jnp.where(low, from_right, from_left)
        return jnp.where(ghost_in, found, 0.0)

    def pieces(kind, at, count, middle):
        cut = min(max(middle - at, 0), count)
        if cut:
            yield 0, cut, spread_tiles(kind, at, cut, False)
        if cut < count:
            yield cut, count - cut, spread_tiles(kind, at + cut - middle, count - cut, True)

    def put(a, at, count, where, value):
        span = pl.ds(at, count)
        if a < 6:
            ext[a][span, where] = value
        elif a == CODES:
            kept, gained = coefficients(value)
            if where.start:
                kept, gained = jnp.where(ghost_in, kept, 0.0), jnp.where(ghost_in, gained, 0.0)
            keep[span, where] = kept
            gain[span, where] = gained
        else:
            current[span, where] = CURRENT_SCALE * value

    mine, edge = pl.ds(0, width), pl.ds(width, TILE)
    for a in range(8):
        for at, count, value in pieces(0, a * planes, planes, 4 * planes):
            put(a, base + at, count, edge, value)
        for block, kind, counts, starts, to in (
            (down, 1, downs, down_at, base + planes),
            (up, 2, ups, up_at, base - ups[a]),
        ):
            if counts[a]:
                put(a, to, counts[a], mine, block[pl.ds(starts[a], counts[a])])
                for at, count, value in pieces(kind, starts[a], counts[a], half_up(starts[-1])):
                    put(a, to + at, count, edge, value)

    lane = lax.broadcasted_iota(jnp.int32, (tall, depth), 1)
    not_last, not_first = lane < depth - 1, lane > 0

    def forward_y(v):
        return jnp.where(not_last, pltpu.roll(v, depth - 1, 2), 0.0) - v

    def backward_y(v):
        return v - jnp.where(not_first, pltpu.roll(v, 1, 2), 0.0)

    def forward_x(v):
        return pltpu.roll(v, tall - 1, 1) - v

    def backward_x(v):
        return v - pltpu.roll(v, 1, 1)

    def out_copy(a, plane):
        return pltpu.make_async_copy(final.at[a, plane], outs[a].at[plane], sems.at[a, plane])

    def in_groups(start, count, body):
        whole = count // GROUP
        if whole:

            @pl.loop(0, whole)
            def _(i):
                body(start + i * GROUP, GROUP)

        if count % GROUP:
            body(start + whole * GROUP, count % GROUP)

    moved_now = 0
    for t in range(STEPS):
        moved_now = moved_now + moved[t]
        done = t == STEPS - 1

        def magnetic(e, count):
            here, above = pl.ds(e, count), pl.ds(e + 1, count)
            ex, ey, es = ext[EX][here], ext[EY][here], ext[ES][here]
            bx = ext[BX][here] - (rows[4] * forward_y(es) - rows[5] * (ext[EY][above] - ey))
            by = ext[BY][here] - rows[6] * ((ext[EX][above] - ex) - forward_x(rows[0] * es))
            bs = ext[BS][here] - rows[4] * (forward_x(ey) - forward_y(ex))
            ext[BX][here], ext[BY][here], ext[BS][here] = bx, by, bs

        def electric(e, count):
            here, below, cells = pl.ds(e, count), pl.ds(e - 1, count), pl.ds(e - moved_now, count)
            bx, by, bs = ext[BX][here], ext[BY][here], ext[BS][here]
            kept, gained = keep[cells], gain[cells]
            ex = kept * ext[EX][here] + gained * (backward_y(bs) - rows[3] * (by - ext[BY][below]))
            ey = kept * ext[EY][here] + gained * (
                rows[2] * ((bx - ext[BX][below]) - backward_x(rows[1] * bs))
            )
            es = kept * ext[ES][here] + gained * (backward_x(by) - backward_y(bx) - current[cells])
            if not done:
                ext[EX][here], ext[EY][here], ext[ES][here] = ex, ey, es
                return
            for a, value in enumerate((ex, ey, es, bx, by, bs)):
                final[a, pl.ds(e - 3, count)] = value[:, :width]
                for n in range(count):
                    out_copy(a, e - 3 + n).start()

        in_groups(t, planes + 5 - 2 * t, magnetic)

        @pl.when(first)
        def _():
            for a in (BX, BY):
                ext[a][base + moved_now - 1] = jnp.zeros((tall, depth), jnp.float32)

        in_groups(t + 1, planes + 4 - 2 * t, electric)

        if not done:

            @pl.when(last)
            def _():
                for a in (EX, EY, ES):
                    ext[a][planes + base + moved_now] = jnp.zeros((tall, depth), jnp.float32)

    def finish(plane, carry):
        for a in range(6):
            out_copy(a, plane).wait()
        return carry

    lax.fori_loop(0, planes, finish, 0)


def advance(case, moved, shape, ready, ghosts):
    planes, width, depth = shape
    block = jax.ShapeDtypeStruct(shape, jnp.float32)
    n_in = 11 + len(ghosts)
    like = lambda x: pltpu.VMEM(x.shape, x.dtype)
    found = pl.pallas_call(
        functools.partial(steps_kernel, case, (len(ghosts) - 2) // 3),
        out_shape=[block] * 6 + [like(x) for x in ready[:9]],
        in_specs=[SMEM] + [VMEM] * (n_in - 1),
        out_specs=[ANY] * 6 + [VMEM] * 9,
        input_output_aliases={1 + n: 6 + n for n in range(9)},
        scratch_shapes=[
            pltpu.VMEM((6, planes, width, depth), jnp.float32),
            pltpu.SemaphoreType.DMA((6, planes)),
        ],
        compiler_params=pltpu.CompilerParams(vmem_limit_bytes=32 * 2**20),
        name="steps",
    )(moved, *ready, *ghosts)
    return tuple(found[:6])


def passed(block, dz, side):
    size_z, size_x = lax.axis_size("gz"), lax.axis_size("gx")
    steps_x = {"swap": (1, -1), "right": (1,), "left": (-1,), None: (0,)}[side]
    route = [
        (z * size_x + x, (z + dz) * size_x + x + dx)
        for z in range(size_z)
        for x in range(size_x)
        for dx in steps_x
        if 0 <= z + dz < size_z and 0 <= x + dx < size_x
    ]
    return lax.ppermute(block, ("gz", "gx"), route)


def on_device(*args):
    arrays, moved = args[:8], args[8]
    arrays = arrays[:6] + (arrays[7], arrays[6])
    sides = ("swap",) if lax.axis_size("gx") == 2 else ("right", "left")
    own, which, across, sent = pack(sides, arrays, moved)

    def run(c, own, across, sent, moved):
        case = CASES[c]
        blocks = sent[c]
        ghosts = [passed(blocks[0], -1, None), passed(blocks[1], 1, None)]
        for n, side in enumerate(sides):
            ghosts.append(passed(across[n], 0, side))
            ghosts.append(passed(blocks[2 + 2 * n], -1, side))
            ghosts.append(passed(blocks[3 + 2 * n], 1, side))
        ready = prepare(case[0], own)
        return advance(case, moved, own[0].shape, ready, ghosts)

    return lax.switch(
        which[0],
        [functools.partial(run, c) for c in range(len(CASES))],
        own,
        across,
        sent,
        moved,
    )


def solution(mesh):
    block = P("gz", "gx", None)
    return jax.shard_map(
        on_device,
        mesh=mesh,
        in_specs=(block,) * 8 + (P(),),
        out_specs=(block,) * 6,
        check_vma=False,
    )
```

```python
import functools

import jax
import jax.numpy as jnp
from jax import lax
from jax.experimental import pallas as pl
from jax.experimental.pallas import tpu as pltpu
from jax.sharding import PartitionSpec as P

STEPS = 3
TILE = 8
HALF = 4
GROUP = 4
TIME_STEP = 0.5
CURRENT_SCALE = 0.1
VMEM = pl.BlockSpec(memory_space=pltpu.VMEM)
SMEM = pl.BlockSpec(memory_space=pltpu.SMEM)
ANY = pl.BlockSpec(memory_space=pl.ANY)
EX, EY, ES, BX, BY, BS, CODES, BUNCH = range(8)
CASES = ((1, 1), (1, 0), (2, 1), (2, 0))


def down_counts(case):
    moves, now = case
    later = moves - now
    return (moves + 2,) * 6 + (later + 2, later + 1)


def up_counts(case):
    moves, now = case
    below = 3 - moves
    later = moves - now
    return (below - 1, below - 1, below, below, below, below - 1, 2 - later, 2 - later)


def offsets(counts):
    starts = [0]
    for count in counts:
        starts.append(starts[-1] + count)
    return starts


def half_up(count):
    return (count + 1) // 2


def column_scales(place, total):
    place = place.astype(jnp.float32)
    whole = 1.0 + (place - total / 2) / (2 * total)
    half = 1.0 + (place + 0.5 - total / 2) / (2 * total)
    return whole, half


def turned(tiles):
    return pltpu.roll(tiles, HALF, 1)


def pack_kernel(sides, *refs):
    sources, moved = refs[:8], refs[8]
    own = refs[9:17]
    which, moved_here = refs[17:19]
    across = refs[19 : 19 + len(sides)]
    sent = refs[19 + len(sides) : -2]
    sems, moved_sem = refs[-2:]
    per_case = 2 + 2 * len(sides)
    planes, width, depth = own[0].shape
    gx = lax.axis_index("gx")
    total = width * lax.axis_size("gx")

    get_moved = pltpu.make_async_copy(moved, moved_here, moved_sem)
    get_moved.start()
    copies = [pltpu.make_async_copy(sources[a], own[a], sems.at[a]) for a in range(8)]
    for item in copies:
        item.start()
    get_moved.wait()
    now = moved_here[0]
    later = moved_here[1] + moved_here[2]
    case_index = jnp.where(now + later == 1, 1 - now, 3 - now)
    which[0] = case_index

    row = lax.broadcasted_iota(jnp.int32, (width, depth), 0)
    whole, half = column_scales(gx * width + row, total)
    step_whole, step_half = TIME_STEP / whole, TIME_STEP / half
    low = lax.broadcasted_iota(jnp.int32, (1, TILE, depth), 1) < HALF

    def edge_of(side):
        if side == "swap":
            return pl.multiple_of(jnp.where(gx == 0, width - TILE, 0), TILE), gx == 0
        return (width - TILE, True) if side == "right" else (0, False)

    def paired(first, second, high):
        if high is True:
            return jnp.where(low, turned(first), second)
        if high is False:
            return jnp.where(low, first, turned(second))
        return jnp.where(
            low,
            jnp.where(high, turned(first), first),
            jnp.where(high, second, turned(second)),
        )

    for item in copies:
        item.wait()

    for n, side in enumerate(sides):
        at, high = edge_of(side)
        for a in range(4):
            first = own[a][:, pl.ds(at, TILE)]
            second = own[a + 4][:, pl.ds(at, TILE)].astype(jnp.float32)
            across[n][pl.ds(a * planes, planes)] = paired(first, second, high)

    for c, case in enumerate(CASES):
        down, up = sent[c * per_case : c * per_case + 2]
        corners = sent[c * per_case + 2 : (c + 1) * per_case]
        downs, ups = down_counts(case), up_counts(case)
        down_at, up_at = offsets(downs), offsets(ups)
        moves = case[0]

        @pl.when(case_index == c)
        def _():
            for a in range(8):
                if downs[a]:
                    down[pl.ds(down_at[a], downs[a])] = own[a][: downs[a]].astype(jnp.float32)
                if ups[a]:
                    up[pl.ds(up_at[a], ups[a])] = own[a][planes - ups[a] :].astype(jnp.float32)
            far = moves + 2
            down[down_at[BX] + far - 1] = own[BX][far - 1] + step_whole * own[EY][far]
            down[down_at[BY] + far - 1] = own[BY][far - 1] - step_half * own[EX][far]
            far = planes - (3 - moves)
            up[up_at[BX]] = own[BX][far] - step_whole * own[EY][far]
            up[up_at[BY]] = own[BY][far] + step_half * own[EX][far]
            for n, side in enumerate(sides):
                at, high = edge_of(side)
                for block, corner, count in (
                    (down, corners[2 * n], down_at[-1]),
                    (up, corners[2 * n + 1], up_at[-1]),
                ):
                    middle = half_up(count)
                    rest = count - middle
                    first = block[pl.ds(0, middle), pl.ds(at, TILE)]
                    second = block[pl.ds(middle, rest), pl.ds(at, TILE)]
                    corner[pl.ds(0, rest)] = paired(first[:rest], second, high)
                    if rest < middle:
                        corner[pl.ds(rest, 1)] = paired(first[rest:], first[rest:], high)


def pack(sides, arrays, moved):
    planes, width, depth = arrays[0].shape
    vmem = lambda *shape: pltpu.VMEM(shape, jnp.float32)
    shapes = [pltpu.VMEM(a.shape, a.dtype) for a in arrays] + [pltpu.SMEM((1,), jnp.int32), pltpu.SMEM((STEPS,), jnp.int32)]
    shapes += [vmem(4 * planes, TILE, depth)] * len(sides)
    for case in CASES:
        n_down, n_up = sum(down_counts(case)), sum(up_counts(case))
        shapes += [vmem(n_down, width, depth), vmem(n_up, width, depth)]
        shapes += [vmem(half_up(n_down), TILE, depth), vmem(half_up(n_up), TILE, depth)] * len(sides)
    found = pl.pallas_call(
        functools.partial(pack_kernel, sides),
        out_shape=shapes,
        in_specs=[ANY] * 9,
        out_specs=[VMEM] * 8 + [SMEM] * 2 + [VMEM] * (len(shapes) - 10),
        scratch_shapes=[
            pltpu.SemaphoreType.DMA((8,)),
            pltpu.SemaphoreType.DMA,
        ],
        compiler_params=pltpu.CompilerParams(vmem_limit_bytes=32 * 2**20),
        name="pack",
    )(*(pltpu.with_memory_space_constraint(a, pltpu.HBM) for a in (*arrays, moved)))
    own, which, moved_here, rest = found[:8], found[8], found[9], found[10:]
    across, sent = rest[: len(sides)], rest[len(sides) :]
    per_case = 2 + 2 * len(sides)
    return own, which, moved_here, across, [sent[c * per_case : (c + 1) * per_case] for c in range(len(CASES))]


def coefficients(code):
    kind = code.dtype.type
    five, six, seven = code == kind(5), code == kind(6), code == kind(7)
    keep = jnp.where(five, 0.0, jnp.where(six, 0.8 / 1.2, jnp.where(seven, 0.4 / 1.6, 1.0)))
    gain = jnp.where(
        five,
        0.0,
        jnp.where(six, TIME_STEP / 1.2, jnp.where(seven, TIME_STEP / 1.6, TIME_STEP)),
    )
    return keep, gain


def ghost_inside(width, depth):
    gx = lax.axis_index("gx")
    row = lax.broadcasted_iota(jnp.int32, (1, TILE, depth), 1)
    right = gx < lax.axis_size("gx") - 1
    return jnp.where(row < HALF, right.astype(jnp.int32), (gx > 0).astype(jnp.int32)) == 1


def spread_tiles(beside, upper, depth):
    gx = lax.axis_index("gx")
    if len(beside) == 1:
        same = (gx > 0) if upper else (gx == 0)
        found = jnp.where(same, beside[0], turned(beside[0]))
    else:
        from_left, from_right = beside
        if upper:
            from_right = turned(from_right)
        else:
            from_left = turned(from_left)
        low = lax.broadcasted_iota(jnp.int32, (1, TILE, depth), 1) < HALF
        found = jnp.where(low, from_right, from_left)
    return found


def pieces(beside, at, count, middle):
    depth = beside[0].shape[-1]
    cut = min(max(middle - at, 0), count)
    if cut:
        yield 0, cut, spread_tiles([side[pl.ds(at, cut)] for side in beside], False, depth)
    if cut < count:
        span = pl.ds(at + cut - middle, count - cut)
        yield cut, count - cut, spread_tiles([side[span] for side in beside], True, depth)


class Cells:
    def __init__(self, refs, width):
        self.ext, (self.keep, self.gain, self.current, self.rows) = refs[:6], refs[6:]
        self.width = width
        self.tall, self.depth = self.keep.shape[1:]
        self.ghost_in = ghost_inside(width, self.depth)
        lane = lax.broadcasted_iota(jnp.int32, (self.tall, self.depth), 1)
        self.not_last, self.not_first = lane < self.depth - 1, lane > 0

    def put(self, a, at, count, value, ghost):
        here = pl.ds(at, count)
        where = pl.ds(self.width, TILE) if ghost else pl.ds(0, self.width)
        mask = (lambda v: jnp.where(self.ghost_in, v, 0.0)) if ghost else (lambda v: v)
        if a < 6:
            self.ext[a][here, where] = mask(value)
        elif a == CODES:
            kept, gained = coefficients(value)
            self.keep[here, where], self.gain[here, where] = mask(kept), mask(gained)
        else:
            self.current[here, where] = CURRENT_SCALE * mask(value.astype(jnp.float32))

    def forward_y(self, v):
        return jnp.where(self.not_last, pltpu.roll(v, self.depth - 1, 2), 0.0) - v

    def backward_y(self, v):
        return v - jnp.where(self.not_first, pltpu.roll(v, 1, 2), 0.0)

    def forward_x(self, v):
        return pltpu.roll(v, self.tall - 1, 1) - v

    def backward_x(self, v):
        return v - pltpu.roll(v, 1, 1)

    def magnetic(self, e, count):
        ext, rows = self.ext, self.rows
        here, above = pl.ds(e, count), pl.ds(e + 1, count)
        ex, ey, es = ext[EX][here], ext[EY][here], ext[ES][here]
        bx = ext[BX][here] - (rows[4] * self.forward_y(es) - rows[5] * (ext[EY][above] - ey))
        by = ext[BY][here] - rows[6] * ((ext[EX][above] - ex) - self.forward_x(rows[0] * es))
        bs = ext[BS][here] - rows[4] * (self.forward_x(ey) - self.forward_y(ex))
        ext[BX][here], ext[BY][here], ext[BS][here] = bx, by, bs

    def electric(self, e, count, moved_now):
        ext, rows = self.ext, self.rows
        here, below, cells = pl.ds(e, count), pl.ds(e - 1, count), pl.ds(e - moved_now, count)
        bx, by, bs = ext[BX][here], ext[BY][here], ext[BS][here]
        kept, gained = self.keep[cells], self.gain[cells]
        ex = kept * ext[EX][here] + gained * (self.backward_y(bs) - rows[3] * (by - ext[BY][below]))
        ey = kept * ext[EY][here] + gained * (
            rows[2] * ((bx - ext[BX][below]) - self.backward_x(rows[1] * bs))
        )
        es = kept * ext[ES][here] + gained * (
            self.backward_x(by) - self.backward_y(bx) - self.current[cells]
        )
        ext[EX][here], ext[EY][here], ext[ES][here] = ex, ey, es

    def leave(self, plane):
        for a in (BX, BY):
            self.ext[a][plane] = jnp.zeros((self.tall, self.depth), jnp.float32)


def in_groups(start, count, body):
    whole = max(count, 0) // GROUP
    if whole:

        @pl.loop(0, whole)
        def _(i):
            body(start + i * GROUP, GROUP)

    if count > 0 and count % GROUP:
        body(start + whole * GROUP, count % GROUP)


def prepare_kernel(moves, n_sides, moved, *refs):
    own, beside = refs[:8], refs[8 : 8 + n_sides]
    planes, width, depth = own[0].shape
    cells = Cells(refs[8 + n_sides :], width)
    tall, rows = cells.tall, cells.rows
    base = 3 - moves
    top = base + planes - 1
    total = width * lax.axis_size("gx")

    row = lax.broadcasted_iota(jnp.int32, (tall, depth), 0)
    place = lax.axis_index("gx") * width + jnp.where(row < width + HALF, row, row - tall)
    inside = (place >= 0) & (place < total)
    whole, half = column_scales(place, total)
    step = jnp.where(inside, TIME_STEP, 0.0)
    for n, value in enumerate((whole, half, 1.0 / whole, 1.0 / half, step, step / whole, step / half)):
        rows[n] = value
    for a in range(8):
        cells.put(a, base, planes, own[a][...], False)
        for at, count, value in pieces(beside, a * planes, planes, 4 * planes):
            cells.put(a, base + at, count, value, True)
    for a in (EX, EY):
        cells.ext[a][0] = jnp.zeros((tall, depth), jnp.float32)
        cells.ext[a][planes + 5] = jnp.zeros((tall, depth), jnp.float32)

    moved_now = 0
    for t in range(STEPS):
        moved_now = moved_now + moved[t]
        in_groups(base + t, planes - 1 - 2 * t, cells.magnetic)

        @pl.when((lax.axis_index("gz") == 0) & (moved_now == t + 1))
        def _():
            cells.leave(base + t)

        in_groups(base + t + 1, planes - 2 - 2 * t, lambda e, n: cells.electric(e, n, moved_now))


def prepare(moves, moved, own, beside):
    planes, width, depth = own[0].shape
    tall = width + TILE
    vmem = lambda *shape: pltpu.VMEM(shape, jnp.float32)
    shapes = [vmem(planes + 6, tall, depth)] * 6 + [vmem(planes + 5, tall, depth)] * 3
    shapes += [vmem(7, tall, depth)]
    return pl.pallas_call(
        functools.partial(prepare_kernel, moves, len(beside)),
        out_shape=shapes,
        in_specs=[SMEM] + [VMEM] * (8 + len(beside)),
        out_specs=[VMEM] * len(shapes),
        compiler_params=pltpu.CompilerParams(vmem_limit_bytes=32 * 2**20),
        cost_estimate=pl.CostEstimate(flops=10**7, bytes_accessed=10**7, transcendentals=0),
        name="prepare",
    )(moved, *own, *beside)


def steps_kernel(case, n_sides, planes, width, moved, *refs):
    rows, (down, up) = refs[9], refs[10:12]
    side_down, side_up = refs[12 : 12 + n_sides], refs[12 + n_sides : 12 + 2 * n_sides]
    at = 12 + 2 * n_sides
    outs = refs[at : at + 6]
    cells = Cells((*refs[at + 6 : at + 15], rows), width)
    sems = refs[at + 15]
    ext = cells.ext
    moves = case[0]
    base = 3 - moves
    top = base + planes - 1
    first = lax.axis_index("gz") == 0
    last = lax.axis_index("gz") == lax.axis_size("gz") - 1
    downs, ups = down_counts(case), up_counts(case)
    down_at, up_at = offsets(downs), offsets(ups)
    copies = []

    def send(a, start, end):
        if end > start:
            item = pltpu.make_async_copy(
                ext[a].at[pl.ds(start, end - start), pl.ds(0, width)],
                outs[a].at[pl.ds(start - 3, end - start)],
                sems.at[len(copies)],
            )
            item.start()
            copies.append(item)

    for a in range(6):
        send(a, base + (2 if a >= BX else 3), top - 2)

    for block, sides, counts, starts, is_down in (
        (down, side_down, downs, down_at, True),
        (up, side_up, ups, up_at, False),
    ):
        for a in range(8):
            if counts[a]:
                to = top + 1 if is_down else base - counts[a]
                cells.put(a, to, counts[a], block[pl.ds(starts[a], counts[a])], False)
                for at, count, value in pieces(sides, starts[a], counts[a], half_up(starts[-1])):
                    cells.put(a, to + at, count, value, True)

    moved_now = 0
    for t in range(STEPS):
        moved_now = moved_now + moved[t]
        cells.magnetic(t, base)
        cells.magnetic(top - t, moves + 3)

        @pl.when(first)
        def _():
            cells.leave(base + moved_now - 1)

        if t == STEPS - 1:
            for a in (BX, BY, BS):
                send(a, 3, base + 2)
                send(a, top - 2, planes + 3)
        cells.electric(t + 1, base, moved_now)
        if t == STEPS - 1:
            for a in (EX, EY, ES):
                send(a, 3, base + 3)
        cells.electric(top - t, moves + 3, moved_now)
        if t == STEPS - 1:
            for a in (EX, EY, ES):
                send(a, top - 2, planes + 3)
        else:

            @pl.when(last)
            def _():
                for a in (EX, EY, ES):
                    ext[a][top + 1 + moved_now] = jnp.zeros((cells.tall, cells.depth), jnp.float32)

    for item in copies:
        item.wait()


def advance(case, moved, shape, ready, ghosts):
    planes, width, depth = shape
    block = jax.ShapeDtypeStruct(shape, jnp.float32)
    n_in = 11 + len(ghosts)
    found = pl.pallas_call(
        functools.partial(steps_kernel, case, (len(ghosts) - 2) // 2, planes, width),
        out_shape=[block] * 6 + [pltpu.VMEM(x.shape, x.dtype) for x in ready[:9]],
        in_specs=[SMEM] + [VMEM] * (n_in - 1),
        out_specs=[ANY] * 6 + [VMEM] * 9,
        input_output_aliases={1 + n: 6 + n for n in range(9)},
        scratch_shapes=[pltpu.SemaphoreType.DMA((18,))],
        compiler_params=pltpu.CompilerParams(vmem_limit_bytes=32 * 2**20),
        name="steps",
    )(moved, *ready, *ghosts)
    return tuple(found[:6])


def passed(block, dz, side):
    size_z, size_x = lax.axis_size("gz"), lax.axis_size("gx")
    steps_x = {"swap": (1, -1), "right": (1,), "left": (-1,), None: (0,)}[side]
    route = [
        (z * size_x + x, (z + dz) * size_x + x + dx)
        for z in range(size_z)
        for x in range(size_x)
        for dx in steps_x
        if 0 <= z + dz < size_z and 0 <= x + dx < size_x
    ]
    return lax.ppermute(block, ("gz", "gx"), route)


def on_device(*args):
    arrays, moved = args[:8], args[8]
    arrays = arrays[:6] + (arrays[7], arrays[6])
    sides = ("swap",) if lax.axis_size("gx") == 2 else ("right", "left")
    own, which, moved, across, sent = pack(sides, arrays, moved)

    def run(c, own, across, sent, moved):
        case, blocks = CASES[c], sent[c]
        down, up = passed(blocks[0], -1, None), passed(blocks[1], 1, None)
        beside = [passed(across[n], 0, side) for n, side in enumerate(sides)]
        side_down = [passed(blocks[2 + 2 * n], -1, side) for n, side in enumerate(sides)]
        side_up = [passed(blocks[3 + 2 * n], 1, side) for n, side in enumerate(sides)]
        ready = prepare(case[0], moved, own, beside)
        return advance(case, moved, own[0].shape, ready, [down, up] + side_down + side_up)

    return lax.switch(
        which[0],
        [functools.partial(run, c) for c in range(len(CASES))],
        own,
        across,
        sent,
        moved,
    )


def solution(mesh):
    block = P("gz", "gx", None)
    return jax.shard_map(
        on_device,
        mesh=mesh,
        in_specs=(block,) * 8 + (P(),),
        out_specs=(block,) * 6,
        check_vma=False,
    )
```

```python
import functools

import jax
import jax.numpy as jnp
from jax import lax
from jax.experimental import pallas as pl
from jax.experimental.pallas import tpu as pltpu
from jax.sharding import PartitionSpec as P

STEPS = 3
TILE = 8
HALF = 4
GROUP = 4
TIME_STEP = 0.5
CURRENT_SCALE = 0.1
VMEM = pl.BlockSpec(memory_space=pltpu.VMEM)
SMEM = pl.BlockSpec(memory_space=pltpu.SMEM)
ANY = pl.BlockSpec(memory_space=pl.ANY)
EX, EY, ES, BX, BY, BS, CODES, BUNCH = range(8)
CASES = ((1, 1), (1, 0), (2, 1), (2, 0))


def down_counts(case):
    moves, now = case
    later = moves - now
    return (moves + 1,) * 6 + (later + 1, later + 1)


def up_counts(case):
    moves, now = case
    below = 3 - moves
    later = moves - now
    return (below - 1, below - 1, below, below, below, below - 1, 2 - later, 2 - later)


def offsets(counts):
    starts = [0]
    for count in counts:
        starts.append(starts[-1] + count)
    return starts


def tile_planes(count, width):
    return -(-count // (width // TILE))


def tile_of(ref, start, n, width):
    per_plane = width // TILE
    return start + n // per_plane, pl.ds(n % per_plane * TILE, TILE)


def column_scales(place, total):
    place = place.astype(jnp.float32)
    whole = 1.0 + (place - total / 2) / (2 * total)
    half = 1.0 + (place + 0.5 - total / 2) / (2 * total)
    return whole, half


def turned(tiles):
    return pltpu.roll(tiles, HALF, tiles.ndim - 2)


def next_y(v):
    depth = v.shape[-1]
    lane = lax.broadcasted_iota(jnp.int32, v.shape[-2:], 1)
    return jnp.where(lane < depth - 1, pltpu.roll(v, depth - 1, v.ndim - 1), 0.0)


def last_y(v):
    lane = lax.broadcasted_iota(jnp.int32, v.shape[-2:], 1)
    return jnp.where(lane > 0, pltpu.roll(v, 1, v.ndim - 1), 0.0)


def next_x(v):
    return pltpu.roll(v, v.shape[-2] - 1, v.ndim - 2)


def last_x(v):
    return pltpu.roll(v, 1, v.ndim - 2)


def low_half(depth):
    return lax.broadcasted_iota(jnp.int32, (TILE, depth), 0) < HALF


def pack_kernel(*refs):
    sources, moved = refs[:8], refs[8]
    which, moved_here = refs[9:11]
    sent = refs[11 : 11 + len(CASES)]
    near, near_int, sems, moved_sem = refs[11 + len(CASES) :]
    _, count, width, depth = near.shape
    gx = lax.axis_index("gx")
    total = width * lax.axis_size("gx")

    get_moved = pltpu.make_async_copy(moved, moved_here, moved_sem)
    get_moved.start()
    copies = []
    for a in range(8):
        goal = near.at[a] if a < 6 else near_int.at[a - 6]
        copies.append(pltpu.make_async_copy(sources[a].at[pl.ds(0, count)], goal, sems.at[a]))
        copies[-1].start()
    get_moved.wait()
    now = moved_here[0]
    later = moved_here[1] + moved_here[2]
    case_index = jnp.where(now + later == 1, 1 - now, 3 - now)
    which[0] = case_index

    row = lax.broadcasted_iota(jnp.int32, (width, depth), 0)
    whole, half = column_scales(gx * width + row, total)
    one_whole, one_half = 1.0 / whole, 1.0 / half
    step_whole, step_half = TIME_STEP * one_whole, TIME_STEP * one_half
    low = low_half(depth)
    for item in copies:
        item.wait()

    for c, case in enumerate(CASES):
        down = sent[c]
        downs = down_counts(case)
        at = offsets(downs[:6])
        moves = case[0]
        far = moves + 1
        cell = 1 + moves - case[1]

        @pl.when(case_index == c)
        def _():
            field = lambda a, plane: near[a, plane]
            for a in range(6):
                down[pl.ds(at[a], far)] = near[a, :far]
            folded = {}
            for plane in (far - 1, far):
                folded[BX, plane] = field(BX, plane) + step_whole * field(EY, plane + 1)
                folded[BY, plane] = field(BY, plane) - step_half * field(EX, plane + 1)
            down[at[BX] + far - 1] = folded[BX, far - 1]
            down[at[BY] + far - 1] = folded[BY, far - 1]

            def magnetic(plane):
                ex, ey, es = field(EX, plane), field(EY, plane), field(ES, plane)
                weighted = whole * es
                bx = folded[BX, plane] - TIME_STEP * (next_y(es) - es) - step_whole * ey
                by = folded[BY, plane] + step_half * (ex + next_x(weighted) - weighted)
                return bx, by

            bx_below, by_below = magnetic(far - 1)
            bx, by = magnetic(far)
            ex, ey = field(EX, far), field(EY, far)
            bs = field(BS, far) - TIME_STEP * ((next_x(ey) - ey) - (next_y(ex) - ex))
            code = near_int[0, cell]
            kept, gained = coefficients(code)
            weighted = half * bs
            place = at[-1]
            down[place] = kept * ex + gained * ((bs - last_y(bs)) - one_half * (by - by_below))
            down[place + 1] = kept * ey + gained * (
                one_whole * ((bx - bx_below) - (weighted - last_x(weighted)))
            )
            place += 2
            for n, a in enumerate((CODES, BUNCH)):
                down[pl.ds(place, cell)] = near_int[n, :cell].astype(jnp.float32)
                place += cell
            edges = [ex, ey, field(ES, far), folded[BX, far], folded[BY, far], field(BS, far)]
            edges.append(code.astype(jnp.float32))
            for n, v in enumerate(edges):
                tile = jnp.where(low, turned(v[width - TILE :]), turned(v[:TILE]))
                plane, rows = tile_of(down, place, n, width)
                down[plane, rows] = tile


def pack(arrays, moved):
    planes, width, depth = arrays[0].shape
    near = max(case[0] for case in CASES) + 3
    shapes = [pltpu.SMEM((1,), jnp.int32), pltpu.SMEM((STEPS,), jnp.int32)]
    for case in CASES:
        count = sum(down_counts(case)) + 2 + tile_planes(7, width)
        shapes.append(pltpu.VMEM((count, width, depth), jnp.float32))
    found = pl.pallas_call(
        pack_kernel,
        out_shape=shapes,
        in_specs=[ANY] * 9,
        out_specs=[SMEM] * 2 + [VMEM] * len(CASES),
        scratch_shapes=[
            pltpu.VMEM((6, near, width, depth), jnp.float32),
            pltpu.VMEM((2, near, width, depth), jnp.int32),
            pltpu.SemaphoreType.DMA((8,)),
            pltpu.SemaphoreType.DMA,
        ],
        compiler_params=pltpu.CompilerParams(vmem_limit_bytes=32 * 2**20),
        name="pack",
    )(*(pltpu.with_memory_space_constraint(a, pltpu.HBM) for a in (*arrays, moved)))
    return found[0], found[1], found[2:]


def edges_kernel(sides, *refs):
    own, across = refs[:8], refs[8:]
    planes, width, depth = own[0].shape
    gx = lax.axis_index("gx")
    low = low_half(depth)
    for n, side in enumerate(sides):
        if side == "swap":
            at, high = pl.multiple_of(jnp.where(gx == 0, width - TILE, 0), TILE), gx == 0
        else:
            at, high = (width - TILE, True) if side == "right" else (0, False)
        for a in range(4):
            first = own[a][:, pl.ds(at, TILE)]
            second = own[a + 4][:, pl.ds(at, TILE)].astype(jnp.float32)
            if side == "swap":
                first = jnp.where(high, turned(first), first)
                second = jnp.where(high, second, turned(second))
            elif high:
                first = turned(first)
            else:
                second = turned(second)
            across[n][pl.ds(a * planes, planes)] = jnp.where(low, first, second)


def edges(sides, own):
    planes, width, depth = own[0].shape
    return pl.pallas_call(
        functools.partial(edges_kernel, sides),
        out_shape=[pltpu.VMEM((4 * planes, TILE, depth), jnp.float32)] * len(sides),
        in_specs=[VMEM] * 8,
        out_specs=[VMEM] * len(sides),
        compiler_params=pltpu.CompilerParams(vmem_limit_bytes=32 * 2**20),
        name="edges",
    )(*own)


def relay_kernel(case, n_sides, *refs):
    own, beside = refs[:8], refs[8 : 8 + n_sides]
    up, corners = refs[8 + n_sides :]
    planes, width, depth = own[0].shape
    moves = case[0]
    gx = lax.axis_index("gx")
    start = gx * width
    total = width * lax.axis_size("gx")
    low = low_half(depth)
    row = lax.broadcasted_iota(jnp.int32, (TILE, depth), 0)
    ups = up_counts(case)
    up_at = offsets(ups)

    column = lax.broadcasted_iota(jnp.int32, (width, depth), 0)
    whole, half = column_scales(start + column, total)
    bottom = planes - (3 - moves)
    for a in range(8):
        if ups[a]:
            up[pl.ds(up_at[a], ups[a])] = own[a][planes - ups[a] :].astype(jnp.float32)
    up[up_at[BX]] = own[BX][bottom] - (TIME_STEP / whole) * own[EY][bottom]
    up[up_at[BY]] = own[BY][bottom] + (TIME_STEP / half) * own[EX][bottom]

    for n in range(n_sides):
        if n_sides == 1:
            left_column = jnp.where(gx == 0, start + width, start - HALF)
        else:
            left_column = start - HALF if n == 0 else start + width
        whole, half = column_scales(left_column + jnp.where(row < HALF, row, row - HALF), total)
        step_whole, step_half = TIME_STEP / whole, TIME_STEP / half
        tile = lambda a, plane: beside[n][a * planes + plane]

        def folded(a, plane, source, sign):
            if a == BX:
                return tile(a, plane) + jnp.where(low, sign * step_whole * tile(EY, source), 0.0)
            if a == BY - 4:
                return tile(a, plane) - jnp.where(low, 0.0, turned(sign * step_half * tile(EX, source)))
            return tile(a, plane)

        count = moves + 2
        for a in range(4):
            to = (n * 4 + a) * count
            corners[pl.ds(to, count)] = beside[n][pl.ds(a * planes, count)]
            if a in (BX, BY - 4):
                for plane in (moves, moves + 1):
                    corners[to + plane] = folded(a, plane, plane + 1, 1.0)
            for i in range(3 - moves):
                plane, rows = tile_of(up, up_at[-1], (n * 4 + a) * (3 - moves) + i, width)
                value = folded(a, bottom, bottom, -1.0) if i == 0 else tile(a, bottom + i)
                up[plane, rows] = value


def relay(case, own, beside):
    planes, width, depth = own[0].shape
    moves = case[0]
    tiles = len(beside) * 4
    n_up = sum(up_counts(case)) + tile_planes(tiles * (3 - moves), width)
    return pl.pallas_call(
        functools.partial(relay_kernel, case, len(beside)),
        out_shape=[
            pltpu.VMEM((n_up, width, depth), jnp.float32),
            pltpu.VMEM((tiles * (moves + 2), TILE, depth), jnp.float32),
        ],
        in_specs=[VMEM] * (8 + len(beside)),
        out_specs=[VMEM] * 2,
        compiler_params=pltpu.CompilerParams(vmem_limit_bytes=32 * 2**20),
        name="relay",
    )(*own, *beside)


def coefficients(code):
    kind = code.dtype.type
    five, six, seven = code == kind(5), code == kind(6), code == kind(7)
    keep = jnp.where(five, 0.0, jnp.where(six, 0.8 / 1.2, jnp.where(seven, 0.4 / 1.6, 1.0)))
    gain = jnp.where(
        five,
        0.0,
        jnp.where(six, TIME_STEP / 1.2, jnp.where(seven, TIME_STEP / 1.6, TIME_STEP)),
    )
    return keep, gain


def ghost_inside(width, depth):
    gx = lax.axis_index("gx")
    row = lax.broadcasted_iota(jnp.int32, (1, TILE, depth), 1)
    right = gx < lax.axis_size("gx") - 1
    return jnp.where(row < HALF, right.astype(jnp.int32), (gx > 0).astype(jnp.int32)) == 1


def spread_tiles(beside, upper):
    gx = lax.axis_index("gx")
    if len(beside) == 1:
        same = (gx > 0) if upper else (gx == 0)
        return jnp.where(same, beside[0], turned(beside[0]))
    from_left, from_right = beside
    if upper:
        from_right = turned(from_right)
    else:
        from_left = turned(from_left)
    return jnp.where(low_half(from_left.shape[-1]), from_right, from_left)


class Cells:
    def __init__(self, refs, width):
        self.ext, (self.keep, self.gain, self.current, self.rows) = refs[:6], refs[6:]
        self.width = width
        self.tall, self.depth = self.keep.shape[1:]
        self.ghost_in = ghost_inside(width, self.depth)

    def put(self, a, at, count, value, ghost):
        here = pl.ds(at, count)
        where = pl.ds(self.width, TILE) if ghost else pl.ds(0, self.width)
        mask = (lambda v: jnp.where(self.ghost_in, v, 0.0)) if ghost else (lambda v: v)
        if a < 6:
            self.ext[a][here, where] = mask(value)
        elif a == CODES:
            kept, gained = coefficients(value)
            self.keep[here, where], self.gain[here, where] = mask(kept), mask(gained)
        else:
            self.current[here, where] = CURRENT_SCALE * mask(value.astype(jnp.float32))

    def magnetic(self, e, count):
        ext, rows = self.ext, self.rows
        here, above = pl.ds(e, count), pl.ds(e + 1, count)
        ex, ey, es = ext[EX][here], ext[EY][here], ext[ES][here]
        bx = ext[BX][here] - (rows[4] * (next_y(es) - es) - rows[5] * (ext[EY][above] - ey))
        by = ext[BY][here] - rows[6] * ((ext[EX][above] - ex) - (next_x(rows[0] * es) - rows[0] * es))
        bs = ext[BS][here] - rows[4] * ((next_x(ey) - ey) - (next_y(ex) - ex))
        ext[BX][here], ext[BY][here], ext[BS][here] = bx, by, bs

    def electric(self, e, count, moved_now):
        ext, rows = self.ext, self.rows
        here, below, cells = pl.ds(e, count), pl.ds(e - 1, count), pl.ds(e - moved_now, count)
        bx, by, bs = ext[BX][here], ext[BY][here], ext[BS][here]
        kept, gained = self.keep[cells], self.gain[cells]
        ex = kept * ext[EX][here] + gained * ((bs - last_y(bs)) - rows[3] * (by - ext[BY][below]))
        ey = kept * ext[EY][here] + gained * (
            rows[2] * ((bx - ext[BX][below]) - (rows[1] * bs - last_x(rows[1] * bs)))
        )
        es = kept * ext[ES][here] + gained * (
            (by - last_x(by)) - (bx - last_y(bx)) - self.current[cells]
        )
        ext[EX][here], ext[EY][here], ext[ES][here] = ex, ey, es

    def leave(self, plane):
        for a in (BX, BY):
            self.ext[a][plane] = jnp.zeros((self.tall, self.depth), jnp.float32)


def in_groups(start, count, body):
    whole = max(count, 0) // GROUP
    if whole:

        @pl.loop(0, whole)
        def _(i):
            body(start + i * GROUP, GROUP)

    if count > 0 and count % GROUP:
        body(start + whole * GROUP, count % GROUP)


def prepare_kernel(moves, n_sides, moved, *refs):
    own, beside = refs[:8], refs[8 : 8 + n_sides]
    planes, width, depth = own[0].shape
    cells = Cells(refs[8 + n_sides :], width)
    tall, rows = cells.tall, cells.rows
    base = 3 - moves
    top = base + planes - 1
    total = width * lax.axis_size("gx")

    row = lax.broadcasted_iota(jnp.int32, (tall, depth), 0)
    place = lax.axis_index("gx") * width + jnp.where(row < width + HALF, row, row - tall)
    inside = (place >= 0) & (place < total)
    whole, half = column_scales(place, total)
    step = jnp.where(inside, TIME_STEP, 0.0)
    for n, value in enumerate((whole, half, 1.0 / whole, 1.0 / half, step, step / whole, step / half)):
        rows[n] = value
    for a in range(8):
        cells.put(a, base, planes, own[a][...], False)
        tiles = [side[pl.ds(a % 4 * planes, planes)] for side in beside]
        cells.put(a, base, planes, spread_tiles(tiles, a >= 4), True)
    for a in (EX, EY):
        cells.ext[a][0] = jnp.zeros((tall, depth), jnp.float32)
        cells.ext[a][planes + 4] = jnp.zeros((tall, depth), jnp.float32)

    moved_now = 0
    for t in range(STEPS):
        moved_now = moved_now + moved[t]
        in_groups(base + t, planes - 1 - 2 * t, cells.magnetic)

        @pl.when((lax.axis_index("gz") == 0) & (moved_now == t + 1))
        def _():
            cells.leave(base + t)

        in_groups(base + t + 1, planes - 2 - 2 * t, lambda e, n: cells.electric(e, n, moved_now))


def prepare(moves, moved, own, beside):
    planes, width, depth = own[0].shape
    tall = width + TILE
    vmem = lambda *shape: pltpu.VMEM(shape, jnp.float32)
    shapes = [vmem(planes + 5, tall, depth)] * 9
    shapes += [vmem(7, tall, depth)]
    return pl.pallas_call(
        functools.partial(prepare_kernel, moves, len(beside)),
        out_shape=shapes,
        in_specs=[SMEM] + [VMEM] * (8 + len(beside)),
        out_specs=[VMEM] * len(shapes),
        compiler_params=pltpu.CompilerParams(vmem_limit_bytes=32 * 2**20),
        cost_estimate=pl.CostEstimate(flops=10**7, bytes_accessed=10**7, transcendentals=0),
        name="prepare",
    )(moved, *own, *beside)


def steps_kernel(case, n_sides, planes, width, moved, *refs):
    rows, down, up, corners = refs[9:13]
    outs = refs[13:19]
    cells = Cells((*refs[19:28], rows), width)
    sems = refs[28]
    ext = cells.ext
    moves = case[0]
    base = 3 - moves
    top = base + planes - 1
    far = planes + 4
    first = lax.axis_index("gz") == 0
    last = lax.axis_index("gz") == lax.axis_size("gz") - 1
    downs, ups = down_counts(case), up_counts(case)
    at, up_at = offsets(downs[:6]), offsets(ups)
    far_at = at[-1]
    at = at[:6] + [far_at + 2, far_at + 2 + downs[CODES]]
    tiles_at = at[BUNCH] + downs[BUNCH]
    copies = []

    def send(a, start, end):
        if end > start:
            item = pltpu.make_async_copy(
                ext[a].at[pl.ds(start, end - start), pl.ds(0, width)],
                outs[a].at[pl.ds(start - 3, end - start)],
                sems.at[len(copies)],
            )
            item.start()
            copies.append(item)

    for a in range(6):
        send(a, base + (2 if a >= BX else 3), top - 2)

    def corner(a, plane, count):
        first_tile = [(n * 4 + a % 4) * (moves + 2) + plane for n in range(n_sides)]
        return spread_tiles([corners[pl.ds(t, count)] for t in first_tile], a >= 4)

    for a in range(8):
        cells.put(a, top + 1, downs[a], down[pl.ds(at[a], downs[a])], False)
        cells.put(a, top + 1, downs[a], corner(a, 0, downs[a]), True)
        if ups[a]:
            cells.put(a, base - ups[a], ups[a], up[pl.ds(up_at[a], ups[a])], False)
            for i in range(base - ups[a], base):
                tiles = []
                for n in range(n_sides):
                    plane, here = tile_of(up, up_at[-1], (n * 4 + a % 4) * base + i, width)
                    tiles.append(up[plane, here])
                cells.put(a, i, 1, spread_tiles(tiles, a >= 4)[None], True)

    low = low_half(cells.depth)
    left, right, ghost = pl.ds(0, TILE), pl.ds(width - TILE, TILE), pl.ds(width, TILE)

    def blocks(right_tile, ghost_tile, left_tile):
        return jnp.where(low, right_tile, ghost_tile), jnp.where(low, ghost_tile, left_tile)

    def far_plane():
        def kept_blocks(ref, *plane):
            return blocks(*(turned(ref[(*plane, where)]) for where in (right, ghost, left)))

        def sent_blocks(a, ghost_tile):
            plane, here = tile_of(down, tiles_at, min(a, 6), width)
            tile = down[plane, here]
            return tile, jnp.where(cells.ghost_in[0], ghost_tile, 0.0)

        raw = []
        for a in range(6):
            tile, beyond = sent_blocks(a, corner(a, moves + 1, 1)[0])
            raw.append(blocks(tile, turned(beyond), tile))
        tile, beyond = sent_blocks(CODES, corner(CODES, downs[CODES], 1)[0])
        factors = [
            blocks(mine, turned(jnp.where(cells.ghost_in[0], theirs, 0.0)), mine)
            for mine, theirs in zip(coefficients(tile), coefficients(beyond))
        ]
        const = [kept_blocks(rows, n) for n in range(7)]
        below = [kept_blocks(ext[a], far - 1) for a in (BX, BY)]
        found = []
        for b in range(2):
            ex, ey, es, bx, by, bs = (v[b] for v in raw)
            kept, gained = (v[b] for v in factors)
            row = [v[b] for v in const]
            weighted = row[0] * es
            bx = bx - row[4] * (next_y(es) - es) - row[5] * ey
            by = by + row[6] * (ex + next_x(weighted) - weighted)
            bs = bs - row[4] * ((next_x(ey) - ey) - (next_y(ex) - ex))
            weighted = row[1] * bs
            ex = kept * ex + gained * ((bs - last_y(bs)) - row[3] * (by - below[1][b]))
            ey = kept * ey + gained * (
                row[2] * ((bx - below[0][b]) - (weighted - last_x(weighted)))
            )
            found.append((ex, ey))
        n_row = lax.broadcasted_iota(jnp.int32, (TILE, cells.depth), 0)
        for a in (EX, EY):
            right_block, left_block = found[0][a], found[1][a]
            ext[a][far, pl.ds(0, width)] = down[far_at + a]
            ext[a][far, right] = jnp.where(
                n_row == TILE - 1, turned(right_block), down[far_at + a, right]
            )
            ext[a][far, left] = jnp.where(n_row == 0, turned(left_block), down[far_at + a, left])
            ext[a][far, ghost] = turned(jnp.where(low, left_block, right_block))

    moved_now = 0
    for t in range(STEPS):
        moved_now = moved_now + moved[t]
        above = moves + (2 if t == 0 else 3)
        cells.magnetic(t, base)
        cells.magnetic(top - t, above)

        @pl.when(first)
        def _():
            cells.leave(base + moved_now - 1)

        if t == STEPS - 1:
            for a in (BX, BY, BS):
                send(a, 3, base + 2)
                send(a, top - 2, planes + 3)
        cells.electric(t + 1, base, moved_now)
        if t == STEPS - 1:
            for a in (EX, EY, ES):
                send(a, 3, base + 3)
        cells.electric(top - t, above, moved_now)
        if t == 0:
            far_plane()
        if t == STEPS - 1:
            for a in (EX, EY, ES):
                send(a, top - 2, planes + 3)
        else:

            @pl.when(last)
            def _():
                for a in (EX, EY, ES):
                    ext[a][top + 1 + moved_now] = jnp.zeros((cells.tall, cells.depth), jnp.float32)

    for item in copies:
        item.wait()


def advance(case, n_sides, moved, shape, ready, ghosts):
    planes, width, depth = shape
    block = jax.ShapeDtypeStruct(shape, jnp.float32)
    n_in = 11 + len(ghosts)
    found = pl.pallas_call(
        functools.partial(steps_kernel, case, n_sides, planes, width),
        out_shape=[block] * 6 + [pltpu.VMEM(x.shape, x.dtype) for x in ready[:9]],
        in_specs=[SMEM] + [VMEM] * (n_in - 1),
        out_specs=[ANY] * 6 + [VMEM] * 9,
        input_output_aliases={1 + n: 6 + n for n in range(9)},
        scratch_shapes=[pltpu.SemaphoreType.DMA((18,))],
        compiler_params=pltpu.CompilerParams(vmem_limit_bytes=32 * 2**20),
        name="steps",
    )(moved, *ready, *ghosts)
    return tuple(found[:6])


def passed(block, dz, side):
    size_z, size_x = lax.axis_size("gz"), lax.axis_size("gx")
    steps_x = {"swap": (1, -1), "right": (1,), "left": (-1,), None: (0,)}[side]
    route = [
        (z * size_x + x, (z + dz) * size_x + x + dx)
        for z in range(size_z)
        for x in range(size_x)
        for dx in steps_x
        if 0 <= z + dz < size_z and 0 <= x + dx < size_x
    ]
    return lax.ppermute(block, ("gz", "gx"), route)


def on_device(*args):
    arrays, moved = args[:8], args[8]
    arrays = arrays[:6] + (arrays[7], arrays[6])
    sides = ("swap",) if lax.axis_size("gx") == 2 else ("right", "left")
    which, moved, sent = pack(arrays, moved)

    def run(c, own, sent, moved):
        case = CASES[c]
        down = passed(sent[c], -1, None)
        across = edges(sides, own)
        beside = [passed(block, 0, side) for block, side in zip(across, sides)]
        up, corners = relay(case, own, beside)
        up, corners = passed(up, 1, None), passed(corners, -1, None)
        ready = prepare(case[0], moved, own, beside)
        return advance(case, len(sides), moved, own[0].shape, ready, [down, up, corners])

    return lax.switch(
        which[0],
        [functools.partial(run, c) for c in range(len(CASES))],
        arrays,
        sent,
        moved,
    )


def solution(mesh):
    block = P("gz", "gx", None)
    return jax.shard_map(
        on_device,
        mesh=mesh,
        in_specs=(block,) * 8 + (P(),),
        out_specs=(block,) * 6,
        check_vma=False,
    )
```

```python
import functools

import jax
import jax.numpy as jnp
from jax import lax
from jax.experimental import pallas as pl
from jax.experimental.pallas import tpu as pltpu
from jax.sharding import PartitionSpec as P

STEPS = 3
TILE = 8
HALF = 4
GROUP = 4
TIME_STEP = 0.5
CURRENT_SCALE = 0.1
VMEM = pl.BlockSpec(memory_space=pltpu.VMEM)
SMEM = pl.BlockSpec(memory_space=pltpu.SMEM)
ANY = pl.BlockSpec(memory_space=pl.ANY)
EX, EY, ES, BX, BY, BS, CODES, BUNCH = range(8)
CASES = ((1, 1), (1, 0), (2, 1), (2, 0))


def down_counts(case):
    moves, now = case
    later = moves - now
    return (moves + 1,) * 6 + (later + 1, later + 1)


def up_counts(case):
    moves, now = case
    below = 3 - moves
    later = moves - now
    return (below - 1, below - 1, below, below, below, below - 1, 2 - later, 2 - later)


def offsets(counts):
    starts = [0]
    for count in counts:
        starts.append(starts[-1] + count)
    return starts


def tile_planes(count, width):
    return -(-count // (width // TILE))


def tile_of(ref, start, n, width):
    per_plane = width // TILE
    return start + n // per_plane, pl.ds(n % per_plane * TILE, TILE)


def column_scales(place, total):
    place = place.astype(jnp.float32)
    whole = 1.0 + (place - total / 2) / (2 * total)
    half = 1.0 + (place + 0.5 - total / 2) / (2 * total)
    return whole, half


def turned(tiles):
    return pltpu.roll(tiles, HALF, tiles.ndim - 2)


def next_y(v):
    depth = v.shape[-1]
    lane = lax.broadcasted_iota(jnp.int32, v.shape[-2:], 1)
    return jnp.where(lane < depth - 1, pltpu.roll(v, depth - 1, v.ndim - 1), 0.0)


def last_y(v):
    lane = lax.broadcasted_iota(jnp.int32, v.shape[-2:], 1)
    return jnp.where(lane > 0, pltpu.roll(v, 1, v.ndim - 1), 0.0)


def next_x(v):
    return pltpu.roll(v, v.shape[-2] - 1, v.ndim - 2)


def last_x(v):
    return pltpu.roll(v, 1, v.ndim - 2)


def low_half(depth):
    return lax.broadcasted_iota(jnp.int32, (TILE, depth), 0) < HALF


def pack_kernel(*refs):
    sources, moved = refs[:8], refs[8]
    which, moved_here = refs[9:11]
    sent = refs[11 : 11 + len(CASES)]
    near, near_int, sems, moved_sem = refs[11 + len(CASES) :]
    _, count, width, depth = near.shape
    gx = lax.axis_index("gx")
    total = width * lax.axis_size("gx")

    get_moved = pltpu.make_async_copy(moved, moved_here, moved_sem)
    get_moved.start()
    copies = []
    for a in range(8):
        goal = near.at[a] if a < 6 else near_int.at[a - 6]
        copies.append(pltpu.make_async_copy(sources[a].at[pl.ds(0, count)], goal, sems.at[a]))
        copies[-1].start()
    get_moved.wait()
    now = moved_here[0]
    later = moved_here[1] + moved_here[2]
    case_index = jnp.where(now + later == 1, 1 - now, 3 - now)
    which[0] = case_index

    row = lax.broadcasted_iota(jnp.int32, (width, depth), 0)
    whole, half = column_scales(gx * width + row, total)
    one_whole, one_half = 1.0 / whole, 1.0 / half
    step_whole, step_half = TIME_STEP * one_whole, TIME_STEP * one_half
    low = low_half(depth)
    for item in copies:
        item.wait()

    for c, case in enumerate(CASES):
        down = sent[c]
        downs = down_counts(case)
        at = offsets(downs[:6])
        moves = case[0]
        far = moves + 1
        cell = 1 + moves - case[1]

        @pl.when(case_index == c)
        def _():
            field = lambda a, plane: near[a, plane]
            for a in range(6):
                down[pl.ds(at[a], far)] = near[a, :far]
            folded = {}
            for plane in (far - 1, far):
                folded[BX, plane] = field(BX, plane) + step_whole * field(EY, plane + 1)
                folded[BY, plane] = field(BY, plane) - step_half * field(EX, plane + 1)
            down[at[BX] + far - 1] = folded[BX, far - 1]
            down[at[BY] + far - 1] = folded[BY, far - 1]

            def magnetic(plane):
                ex, ey, es = field(EX, plane), field(EY, plane), field(ES, plane)
                weighted = whole * es
                bx = folded[BX, plane] - TIME_STEP * (next_y(es) - es) - step_whole * ey
                by = folded[BY, plane] + step_half * (ex + next_x(weighted) - weighted)
                return bx, by

            bx_below, by_below = magnetic(far - 1)
            bx, by = magnetic(far)
            ex, ey = field(EX, far), field(EY, far)
            bs = field(BS, far) - TIME_STEP * ((next_x(ey) - ey) - (next_y(ex) - ex))
            code = near_int[0, cell]
            kept, gained = coefficients(code)
            weighted = half * bs
            place = at[-1]
            down[place] = kept * ex + gained * ((bs - last_y(bs)) - one_half * (by - by_below))
            down[place + 1] = kept * ey + gained * (
                one_whole * ((bx - bx_below) - (weighted - last_x(weighted)))
            )
            place += 2
            for n, a in enumerate((CODES, BUNCH)):
                down[pl.ds(place, cell)] = near_int[n, :cell].astype(jnp.float32)
                place += cell
            edges = [ex, ey, field(ES, far), folded[BX, far], folded[BY, far], field(BS, far)]
            edges.append(code.astype(jnp.float32))
            for n, v in enumerate(edges):
                tile = jnp.where(low, turned(v[width - TILE :]), turned(v[:TILE]))
                plane, rows = tile_of(down, place, n, width)
                down[plane, rows] = tile


def pack(arrays, moved):
    planes, width, depth = arrays[0].shape
    near = max(case[0] for case in CASES) + 3
    shapes = [pltpu.SMEM((1,), jnp.int32), pltpu.SMEM((STEPS,), jnp.int32)]
    for case in CASES:
        count = sum(down_counts(case)) + 2 + tile_planes(7, width)
        shapes.append(pltpu.VMEM((count, width, depth), jnp.float32))
    found = pl.pallas_call(
        pack_kernel,
        out_shape=shapes,
        in_specs=[ANY] * 9,
        out_specs=[SMEM] * 2 + [VMEM] * len(CASES),
        scratch_shapes=[
            pltpu.VMEM((6, near, width, depth), jnp.float32),
            pltpu.VMEM((2, near, width, depth), jnp.int32),
            pltpu.SemaphoreType.DMA((8,)),
            pltpu.SemaphoreType.DMA,
        ],
        compiler_params=pltpu.CompilerParams(vmem_limit_bytes=32 * 2**20),
        name="pack",
    )(*(pltpu.with_memory_space_constraint(a, pltpu.HBM) for a in (*arrays, moved)))
    return found[0], found[1], found[2:]


def edges_kernel(sides, *refs):
    own, across = refs[:8], refs[8:]
    planes, width, depth = own[0].shape
    gx = lax.axis_index("gx")
    low = low_half(depth)
    for n, side in enumerate(sides):
        if side == "swap":
            at, high = pl.multiple_of(jnp.where(gx == 0, width - TILE, 0), TILE), gx == 0
        else:
            at, high = (width - TILE, True) if side == "right" else (0, False)
        for a in range(4):
            first = own[a][:, pl.ds(at, TILE)]
            second = own[a + 4][:, pl.ds(at, TILE)].astype(jnp.float32)
            if side == "swap":
                first = jnp.where(high, turned(first), first)
                second = jnp.where(high, second, turned(second))
            elif high:
                first = turned(first)
            else:
                second = turned(second)
            across[n][pl.ds(a * planes, planes)] = jnp.where(low, first, second)


def edges(sides, own):
    planes, width, depth = own[0].shape
    return pl.pallas_call(
        functools.partial(edges_kernel, sides),
        out_shape=[pltpu.VMEM((4 * planes, TILE, depth), jnp.float32)] * len(sides),
        in_specs=[VMEM] * 8,
        out_specs=[VMEM] * len(sides),
        compiler_params=pltpu.CompilerParams(vmem_limit_bytes=32 * 2**20),
        name="edges",
    )(*own)


def lift_kernel(case, *refs):
    own, up = refs[:8], refs[-1]
    planes, width, depth = own[0].shape
    ups = up_counts(case)
    up_at = offsets(ups)
    column = lax.broadcasted_iota(jnp.int32, (width, depth), 0)
    whole, half = column_scales(lax.axis_index("gx") * width + column, width * lax.axis_size("gx"))
    bottom = planes - (3 - case[0])
    for a in range(8):
        if ups[a]:
            up[pl.ds(up_at[a], ups[a])] = own[a][planes - ups[a] :].astype(jnp.float32)
    up[up_at[BX]] = own[BX][bottom] - (TIME_STEP / whole) * own[EY][bottom]
    up[up_at[BY]] = own[BY][bottom] + (TIME_STEP / half) * own[EX][bottom]


def lift(case, own, after):
    planes, width, depth = own[0].shape
    return pl.pallas_call(
        functools.partial(lift_kernel, case),
        out_shape=pltpu.VMEM((sum(up_counts(case)), width, depth), jnp.float32),
        in_specs=[VMEM] * 8 + [ANY] * len(after),
        out_specs=VMEM,
        compiler_params=pltpu.CompilerParams(vmem_limit_bytes=32 * 2**20),
        cost_estimate=pl.CostEstimate(flops=10**7, bytes_accessed=10**7, transcendentals=0),
        name="lift",
    )(*own, *after)


def relay_kernel(case, planes, width, n_sides, *refs):
    beside, (on, off) = refs[:n_sides], refs[n_sides:]
    depth = on.shape[-1]
    moves = case[0]
    gx = lax.axis_index("gx")
    even = lax.axis_index("gz") % 2 == 0
    start = gx * width
    total = width * lax.axis_size("gx")
    low = low_half(depth)
    row = lax.broadcasted_iota(jnp.int32, (TILE, depth), 0)
    bottom = planes - (3 - moves)

    def fill(to_before, to_after):
        for n in range(n_sides):
            if n_sides == 1:
                left_column = jnp.where(gx == 0, start + width, start - HALF)
            else:
                left_column = start - HALF if n == 0 else start + width
            whole, half = column_scales(left_column + jnp.where(row < HALF, row, row - HALF), total)
            step_whole, step_half = TIME_STEP / whole, TIME_STEP / half
            tile = lambda a, plane: beside[n][a * planes + plane]

            def folded(a, plane, source, sign):
                if a == BX:
                    return tile(a, plane) + jnp.where(low, sign * step_whole * tile(EY, source), 0.0)
                return tile(a, plane) - jnp.where(
                    low, 0.0, turned(sign * step_half * tile(EX, source))
                )

            for a in range(4):
                for ref, first, count, folds in (
                    (to_before, 0, moves + 2, ((moves, 1), (moves + 1, 1))),
                    (to_after, bottom, 3 - moves, ((0, 0),)),
                ):
                    to = (n * 4 + a) * count
                    ref[pl.ds(to, count)] = beside[n][pl.ds(a * planes + first, count)]
                    if a in (BX, BY - 4):
                        for plane, above in folds:
                            at = first + plane
                            ref[to + plane] = folded(a, at, at + above, 1.0 if above else -1.0)

    @pl.when(even)
    def _():
        fill(off, on)

    @pl.when(jnp.logical_not(even))
    def _():
        fill(on, off)


def relay(case, shape, beside):
    planes, width, depth = shape
    tiles = pltpu.VMEM((len(beside) * 4 * (case[0] + 2), TILE, depth), jnp.float32)
    return pl.pallas_call(
        functools.partial(relay_kernel, case, planes, width, len(beside)),
        out_shape=[tiles] * 2,
        in_specs=[VMEM] * len(beside),
        out_specs=[VMEM] * 2,
        compiler_params=pltpu.CompilerParams(vmem_limit_bytes=32 * 2**20),
        name="relay",
    )(*beside)


def coefficients(code):
    kind = code.dtype.type
    five, six, seven = code == kind(5), code == kind(6), code == kind(7)
    keep = jnp.where(five, 0.0, jnp.where(six, 0.8 / 1.2, jnp.where(seven, 0.4 / 1.6, 1.0)))
    gain = jnp.where(
        five,
        0.0,
        jnp.where(six, TIME_STEP / 1.2, jnp.where(seven, TIME_STEP / 1.6, TIME_STEP)),
    )
    return keep, gain


def ghost_inside(width, depth):
    gx = lax.axis_index("gx")
    row = lax.broadcasted_iota(jnp.int32, (1, TILE, depth), 1)
    right = gx < lax.axis_size("gx") - 1
    return jnp.where(row < HALF, right.astype(jnp.int32), (gx > 0).astype(jnp.int32)) == 1


def spread_tiles(beside, upper):
    gx = lax.axis_index("gx")
    if len(beside) == 1:
        same = (gx > 0) if upper else (gx == 0)
        return jnp.where(same, beside[0], turned(beside[0]))
    from_left, from_right = beside
    if upper:
        from_right = turned(from_right)
    else:
        from_left = turned(from_left)
    return jnp.where(low_half(from_left.shape[-1]), from_right, from_left)


class Cells:
    def __init__(self, refs, width):
        self.ext, (self.keep, self.gain, self.current, self.rows) = refs[:6], refs[6:]
        self.width = width
        self.tall, self.depth = self.keep.shape[1:]
        self.ghost_in = ghost_inside(width, self.depth)

    def put(self, a, at, count, value, ghost):
        here = pl.ds(at, count)
        where = pl.ds(self.width, TILE) if ghost else pl.ds(0, self.width)
        mask = (lambda v: jnp.where(self.ghost_in, v, 0.0)) if ghost else (lambda v: v)
        if a < 6:
            self.ext[a][here, where] = mask(value)
        elif a == CODES:
            kept, gained = coefficients(value)
            self.keep[here, where], self.gain[here, where] = mask(kept), mask(gained)
        else:
            self.current[here, where] = CURRENT_SCALE * mask(value.astype(jnp.float32))

    def magnetic(self, e, count):
        ext, rows = self.ext, self.rows
        here, above = pl.ds(e, count), pl.ds(e + 1, count)
        ex, ey, es = ext[EX][here], ext[EY][here], ext[ES][here]
        bx = ext[BX][here] - (rows[4] * (next_y(es) - es) - rows[5] * (ext[EY][above] - ey))
        by = ext[BY][here] - rows[6] * ((ext[EX][above] - ex) - (next_x(rows[0] * es) - rows[0] * es))
        bs = ext[BS][here] - rows[4] * ((next_x(ey) - ey) - (next_y(ex) - ex))
        ext[BX][here], ext[BY][here], ext[BS][here] = bx, by, bs

    def electric(self, e, count, moved_now):
        ext, rows = self.ext, self.rows
        here, below, cells = pl.ds(e, count), pl.ds(e - 1, count), pl.ds(e - moved_now, count)
        bx, by, bs = ext[BX][here], ext[BY][here], ext[BS][here]
        kept, gained = self.keep[cells], self.gain[cells]
        ex = kept * ext[EX][here] + gained * ((bs - last_y(bs)) - rows[3] * (by - ext[BY][below]))
        ey = kept * ext[EY][here] + gained * (
            rows[2] * ((bx - ext[BX][below]) - (rows[1] * bs - last_x(rows[1] * bs)))
        )
        es = kept * ext[ES][here] + gained * (
            (by - last_x(by)) - (bx - last_y(bx)) - self.current[cells]
        )
        ext[EX][here], ext[EY][here], ext[ES][here] = ex, ey, es

    def leave(self, plane):
        for a in (BX, BY):
            self.ext[a][plane] = jnp.zeros((self.tall, self.depth), jnp.float32)


def in_groups(start, count, body):
    whole = max(count, 0) // GROUP
    if whole:

        @pl.loop(0, whole)
        def _(i):
            body(start + i * GROUP, GROUP)

    if count > 0 and count % GROUP:
        body(start + whole * GROUP, count % GROUP)


def prepare_kernel(moves, n_sides, moved, *refs):
    own, beside = refs[:8], refs[8 : 8 + n_sides]
    planes, width, depth = own[0].shape
    cells = Cells(refs[8 + n_sides :], width)
    tall, rows = cells.tall, cells.rows
    base = 3 - moves
    top = base + planes - 1
    total = width * lax.axis_size("gx")

    row = lax.broadcasted_iota(jnp.int32, (tall, depth), 0)
    place = lax.axis_index("gx") * width + jnp.where(row < width + HALF, row, row - tall)
    inside = (place >= 0) & (place < total)
    whole, half = column_scales(place, total)
    step = jnp.where(inside, TIME_STEP, 0.0)
    for n, value in enumerate((whole, half, 1.0 / whole, 1.0 / half, step, step / whole, step / half)):
        rows[n] = value
    for a in range(8):
        cells.put(a, base, planes, own[a][...], False)
        tiles = [side[pl.ds(a % 4 * planes, planes)] for side in beside]
        cells.put(a, base, planes, spread_tiles(tiles, a >= 4), True)
    for a in (EX, EY):
        cells.ext[a][0] = jnp.zeros((tall, depth), jnp.float32)
        cells.ext[a][planes + 4] = jnp.zeros((tall, depth), jnp.float32)

    moved_now = 0
    for t in range(STEPS):
        moved_now = moved_now + moved[t]
        in_groups(base + t, planes - 1 - 2 * t, cells.magnetic)

        @pl.when((lax.axis_index("gz") == 0) & (moved_now == t + 1))
        def _():
            cells.leave(base + t)

        in_groups(base + t + 1, planes - 2 - 2 * t, lambda e, n: cells.electric(e, n, moved_now))


def prepare(moves, moved, own, beside):
    planes, width, depth = own[0].shape
    tall = width + TILE
    vmem = lambda *shape: pltpu.VMEM(shape, jnp.float32)
    shapes = [vmem(planes + 5, tall, depth)] * 9
    shapes += [vmem(7, tall, depth)]
    return pl.pallas_call(
        functools.partial(prepare_kernel, moves, len(beside)),
        out_shape=shapes,
        in_specs=[SMEM] + [VMEM] * (8 + len(beside)),
        out_specs=[VMEM] * len(shapes),
        compiler_params=pltpu.CompilerParams(vmem_limit_bytes=32 * 2**20),
        cost_estimate=pl.CostEstimate(flops=10**7, bytes_accessed=10**7, transcendentals=0),
        name="prepare",
    )(moved, *own, *beside)


def steps_kernel(case, n_sides, planes, width, moved, *refs):
    rows, down, up, on, off = refs[9:14]
    outs = refs[14:20]
    cells = Cells((*refs[20:29], rows), width)
    sems = refs[29]
    ext = cells.ext
    moves = case[0]
    base = 3 - moves
    top = base + planes - 1
    far = planes + 4
    first = lax.axis_index("gz") == 0
    last = lax.axis_index("gz") == lax.axis_size("gz") - 1
    even = lax.axis_index("gz") % 2 == 0
    downs, ups = down_counts(case), up_counts(case)
    at, up_at = offsets(downs[:6]), offsets(ups)
    far_at = at[-1]
    at = at[:6] + [far_at + 2, far_at + 2 + downs[CODES]]
    tiles_at = at[BUNCH] + downs[BUNCH]
    copies = []

    def send(a, start, end):
        if end > start:
            item = pltpu.make_async_copy(
                ext[a].at[pl.ds(start, end - start), pl.ds(0, width)],
                outs[a].at[pl.ds(start - 3, end - start)],
                sems.at[len(copies)],
            )
            item.start()
            copies.append(item)

    for a in range(6):
        send(a, base + (2 if a >= BX else 3), top - 2)

    def corner(a, plane, count, stack, above):
        tiles = []
        for n in range(n_sides):
            span = pl.ds((n * 4 + a % 4) * stack + plane, count)
            tiles.append(jnp.where(even, on[span], off[span]) if above else jnp.where(even, off[span], on[span]))
        return spread_tiles(tiles, a >= 4)

    from_above = lambda a, plane, count: corner(a, plane, count, moves + 2, True)
    for a in range(8):
        cells.put(a, top + 1, downs[a], down[pl.ds(at[a], downs[a])], False)
        cells.put(a, top + 1, downs[a], from_above(a, 0, downs[a]), True)
        if ups[a]:
            cells.put(a, base - ups[a], ups[a], up[pl.ds(up_at[a], ups[a])], False)
            cells.put(a, base - ups[a], ups[a], corner(a, base - ups[a], ups[a], base, False), True)

    low = low_half(cells.depth)
    left, right, ghost = pl.ds(0, TILE), pl.ds(width - TILE, TILE), pl.ds(width, TILE)

    def blocks(right_tile, ghost_tile, left_tile):
        return jnp.where(low, right_tile, ghost_tile), jnp.where(low, ghost_tile, left_tile)

    def far_plane():
        def kept_blocks(ref, *plane):
            return blocks(*(turned(ref[(*plane, where)]) for where in (right, ghost, left)))

        def sent_blocks(a, ghost_tile):
            plane, here = tile_of(down, tiles_at, min(a, 6), width)
            tile = down[plane, here]
            return tile, jnp.where(cells.ghost_in[0], ghost_tile, 0.0)

        raw = []
        for a in range(6):
            tile, beyond = sent_blocks(a, from_above(a, moves + 1, 1)[0])
            raw.append(blocks(tile, turned(beyond), tile))
        tile, beyond = sent_blocks(CODES, from_above(CODES, downs[CODES], 1)[0])
        factors = [
            blocks(mine, turned(jnp.where(cells.ghost_in[0], theirs, 0.0)), mine)
            for mine, theirs in zip(coefficients(tile), coefficients(beyond))
        ]
        const = [kept_blocks(rows, n) for n in range(7)]
        below = [kept_blocks(ext[a], far - 1) for a in (BX, BY)]
        found = []
        for b in range(2):
            ex, ey, es, bx, by, bs = (v[b] for v in raw)
            kept, gained = (v[b] for v in factors)
            row = [v[b] for v in const]
            weighted = row[0] * es
            bx = bx - row[4] * (next_y(es) - es) - row[5] * ey
            by = by + row[6] * (ex + next_x(weighted) - weighted)
            bs = bs - row[4] * ((next_x(ey) - ey) - (next_y(ex) - ex))
            weighted = row[1] * bs
            ex = kept * ex + gained * ((bs - last_y(bs)) - row[3] * (by - below[1][b]))
            ey = kept * ey + gained * (
                row[2] * ((bx - below[0][b]) - (weighted - last_x(weighted)))
            )
            found.append((ex, ey))
        n_row = lax.broadcasted_iota(jnp.int32, (TILE, cells.depth), 0)
        for a in (EX, EY):
            right_block, left_block = found[0][a], found[1][a]
            ext[a][far, pl.ds(0, width)] = down[far_at + a]
            ext[a][far, right] = jnp.where(
                n_row == TILE - 1, turned(right_block), down[far_at + a, right]
            )
            ext[a][far, left] = jnp.where(n_row == 0, turned(left_block), down[far_at + a, left])
            ext[a][far, ghost] = turned(jnp.where(low, left_block, right_block))

    moved_now = 0
    for t in range(STEPS):
        moved_now = moved_now + moved[t]
        above = moves + (2 if t == 0 else 3)
        cells.magnetic(t, base)
        cells.magnetic(top - t, above)

        @pl.when(first)
        def _():
            cells.leave(base + moved_now - 1)

        if t == STEPS - 1:
            for a in (BX, BY, BS):
                send(a, 3, base + 2)
                send(a, top - 2, planes + 3)
        cells.electric(t + 1, base, moved_now)
        if t == STEPS - 1:
            for a in (EX, EY, ES):
                send(a, 3, base + 3)
        cells.electric(top - t, above, moved_now)
        if t == 0:
            far_plane()
        if t == STEPS - 1:
            for a in (EX, EY, ES):
                send(a, top - 2, planes + 3)
        else:

            @pl.when(last)
            def _():
                for a in (EX, EY, ES):
                    ext[a][top + 1 + moved_now] = jnp.zeros((cells.tall, cells.depth), jnp.float32)

    for item in copies:
        item.wait()


def advance(case, n_sides, moved, shape, ready, ghosts):
    planes, width, depth = shape
    block = jax.ShapeDtypeStruct(shape, jnp.float32)
    n_in = 11 + len(ghosts)
    found = pl.pallas_call(
        functools.partial(steps_kernel, case, n_sides, planes, width),
        out_shape=[block] * 6 + [pltpu.VMEM(x.shape, x.dtype) for x in ready[:9]],
        in_specs=[SMEM] + [VMEM] * (n_in - 1),
        out_specs=[ANY] * 6 + [VMEM] * 9,
        input_output_aliases={1 + n: 6 + n for n in range(9)},
        scratch_shapes=[pltpu.SemaphoreType.DMA((18,))],
        compiler_params=pltpu.CompilerParams(vmem_limit_bytes=32 * 2**20),
        name="steps",
    )(moved, *ready, *ghosts)
    return tuple(found[:6])


def passed(block, to, sides=(0,)):
    size_z, size_x = lax.axis_size("gz"), lax.axis_size("gx")
    route = [
        (z * size_x + x, to(z) * size_x + x + dx)
        for z in range(size_z)
        for x in range(size_x)
        for dx in sides
        if 0 <= to(z) < size_z and 0 <= x + dx < size_x
    ]
    return lax.ppermute(block, ("gz", "gx"), route)


def on_device(*args):
    arrays, moved = args[:8], args[8]
    arrays = arrays[:6] + (arrays[7], arrays[6])
    sides = ("swap",) if lax.axis_size("gx") == 2 else ("right", "left")
    which, moved, sent = pack(arrays, moved)

    def run(c, own, sent, moved):
        case = CASES[c]
        down = passed(sent[c], lambda z: z - 1)
        across = edges(sides, own)
        ways = {"swap": (1, -1), "right": (1,), "left": (-1,)}
        beside = [passed(block, lambda z: z, ways[side]) for block, side in zip(across, sides)]
        up = passed(lift(case, own, across), lambda z: z + 1)
        on, off = relay(case, own[0].shape, beside)
        on, off = passed(on, lambda z: z ^ 1), passed(off, lambda z: z + 1 if z % 2 else z - 1)
        ready = prepare(case[0], moved, own, beside)
        return advance(case, len(sides), moved, own[0].shape, ready, [down, up, on, off])

    return lax.switch(
        which[0],
        [functools.partial(run, c) for c in range(len(CASES))],
        arrays,
        sent,
        moved,
    )


def solution(mesh):
    block = P("gz", "gx", None)
    return jax.shard_map(
        on_device,
        mesh=mesh,
        in_specs=(block,) * 8 + (P(),),
        out_specs=(block,) * 6,
        check_vma=False,
    )
```

```python
import functools

import jax
import jax.numpy as jnp
from jax import lax
from jax.experimental import pallas as pl
from jax.experimental.pallas import tpu as pltpu
from jax.sharding import PartitionSpec as P

STEPS = 3
TILE = 8
HALF = 4
GROUP = 4
TIME_STEP = 0.5
CURRENT_SCALE = 0.1
VMEM = pl.BlockSpec(memory_space=pltpu.VMEM)
SMEM = pl.BlockSpec(memory_space=pltpu.SMEM)
ANY = pl.BlockSpec(memory_space=pl.ANY)
EX, EY, ES, BX, BY, BS, CODES, BUNCH = range(8)
CASES = ((1, 1), (1, 0), (2, 1), (2, 0))


def down_counts(case):
    moves, now = case
    later = moves - now
    return (moves,) * 6 + (later + 1, later)


def up_counts(case):
    moves, now = case
    below = 3 - moves
    later = moves - now
    return (below - 1, below - 1, below, below, below, below - 1, 2 - later, 2 - later)


def offsets(counts):
    starts = [0]
    for count in counts:
        starts.append(starts[-1] + count)
    return starts


def tile_planes(count, width):
    return -(-count // (width // TILE))


def tile_of(ref, start, n, width):
    per_plane = width // TILE
    return start + n // per_plane, pl.ds(n % per_plane * TILE, TILE)


def column_scales(place, total):
    place = place.astype(jnp.float32)
    whole = 1.0 + (place - total / 2) / (2 * total)
    half = 1.0 + (place + 0.5 - total / 2) / (2 * total)
    return whole, half


def turned(tiles):
    return pltpu.roll(tiles, HALF, tiles.ndim - 2)


def next_y(v):
    depth = v.shape[-1]
    lane = lax.broadcasted_iota(jnp.int32, v.shape[-2:], 1)
    return jnp.where(lane < depth - 1, pltpu.roll(v, depth - 1, v.ndim - 1), 0.0)


def last_y(v):
    lane = lax.broadcasted_iota(jnp.int32, v.shape[-2:], 1)
    return jnp.where(lane > 0, pltpu.roll(v, 1, v.ndim - 1), 0.0)


def next_x(v):
    return pltpu.roll(v, v.shape[-2] - 1, v.ndim - 2)


def last_x(v):
    return pltpu.roll(v, 1, v.ndim - 2)


def low_half(depth):
    return lax.broadcasted_iota(jnp.int32, (TILE, depth), 0) < HALF


def pack_kernel(*refs):
    sources, moved = refs[:8], refs[8]
    which, moved_here = refs[9:11]
    sent = refs[11 : 11 + len(CASES)]
    near, near_int, sems, moved_sem = refs[11 + len(CASES) :]
    _, count, width, depth = near.shape
    gx = lax.axis_index("gx")
    total = width * lax.axis_size("gx")

    get_moved = pltpu.make_async_copy(moved, moved_here, moved_sem)
    get_moved.start()
    copies = []
    for a in range(8):
        goal = near.at[a] if a < 6 else near_int.at[a - 6]
        copies.append(pltpu.make_async_copy(sources[a].at[pl.ds(0, count)], goal, sems.at[a]))
        copies[-1].start()
    get_moved.wait()
    now = moved_here[0]
    later = moved_here[1] + moved_here[2]
    case_index = jnp.where(now + later == 1, 1 - now, 3 - now)
    which[0] = case_index

    row = lax.broadcasted_iota(jnp.int32, (width, depth), 0)
    whole, half = column_scales(gx * width + row, total)
    one_whole, one_half = 1.0 / whole, 1.0 / half
    step_whole, step_half = TIME_STEP * one_whole, TIME_STEP * one_half
    low = low_half(depth)
    for item in copies:
        item.wait()

    for c, case in enumerate(CASES):
        down = sent[c]
        downs = down_counts(case)
        at = offsets(downs[:6])
        far, first_move = case

        @pl.when(case_index == c)
        def _():
            field = lambda a, plane: near[a, plane]
            for a in range(6):
                down[pl.ds(at[a], far)] = near[a, :far]

            folded = {}
            for plane in range(far - 1, far + 2):
                folded[BX, plane] = field(BX, plane) + step_whole * field(EY, plane + 1)
                folded[BY, plane] = field(BY, plane) - step_half * field(EX, plane + 1)
            down[at[BX] + far - 1] = folded[BX, far - 1]
            down[at[BY] + far - 1] = folded[BY, far - 1]

            def radial_vertical(bx, by, ex, ey, es):
                weighted = whole * es
                bx = bx - TIME_STEP * (next_y(es) - es) - step_whole * ey
                by = by + step_half * (ex + next_x(weighted) - weighted)
                return bx, by

            def longitudinal(bs, ex, ey):
                return bs - TIME_STEP * ((next_x(ey) - ey) - (next_y(ex) - ex))

            def electric(ex, ey, bs, over_x, over_y, factors):
                kept, gained = factors
                weighted = half * bs
                ex = kept * ex + gained * ((bs - last_y(bs)) - one_half * over_y)
                ey = kept * ey + gained * (one_whole * (over_x - (weighted - last_x(weighted))))
                return ex, ey

            now_b = {}
            for plane in range(far - 1, far + 2):
                now_b[plane] = radial_vertical(
                    folded[BX, plane],
                    folded[BY, plane],
                    field(EX, plane),
                    field(EY, plane),
                    field(ES, plane),
                )
            now_e, now_s = {}, {}
            for plane in (far, far + 1):
                ex, ey = field(EX, plane), field(EY, plane)
                now_s[plane] = longitudinal(field(BS, plane), ex, ey)
                factors = coefficients(near_int[0, plane - first_move])
                over = [up - under for up, under in zip(now_b[plane], now_b[plane - 1])]
                now_e[plane] = electric(ex, ey, now_s[plane], *over, factors)
                if plane == far:
                    bx, by = now_b[far]
                    current = CURRENT_SCALE * near_int[1, far - first_move].astype(jnp.float32)
                    es = factors[0] * field(ES, far) + factors[1] * (
                        (by - last_x(by)) - (bx - last_y(bx)) - current
                    )
            place = at[-1]
            down[place], down[place + 1] = now_e[far]

            ex, ey = now_e[far]
            bx, by = now_b[far]
            bx, by = radial_vertical(
                bx + step_whole * now_e[far + 1][1], by - step_half * now_e[far + 1][0], ex, ey, es
            )
            bs = longitudinal(now_s[far], ex, ey)
            factors = coefficients(near_int[0, far - (first_move + moved_here[1])])
            down[place + 2], down[place + 3] = electric(ex, ey, bs, bx, by, factors)

            place += 4
            for n, a in enumerate((CODES, BUNCH)):
                if downs[a]:
                    down[pl.ds(place, downs[a])] = near_int[n, : downs[a]].astype(jnp.float32)
                place += downs[a]
            tiles = [field(a, far) for a in range(6)]
            tiles.append(near_int[1, far - first_move].astype(jnp.float32))
            tiles += [field(EX, far + 1), field(EY, far + 1), field(ES, far + 1)]
            tiles += [folded[BX, far + 1], folded[BY, far + 1], field(BS, far + 1)]
            tiles.append(near_int[0, far + 1 - first_move].astype(jnp.float32))
            for n, v in enumerate(tiles):
                tile = jnp.where(low, turned(v[width - TILE :]), turned(v[:TILE]))
                plane, rows = tile_of(down, place, n, width)
                down[plane, rows] = tile


def pack(arrays, moved):
    planes, width, depth = arrays[0].shape
    near = max(case[0] for case in CASES) + 3
    shapes = [pltpu.SMEM((1,), jnp.int32), pltpu.SMEM((STEPS,), jnp.int32)]
    for case in CASES:
        count = sum(down_counts(case)) + 4 + tile_planes(14, width)
        count += case == (1, 1)
        shapes.append(pltpu.VMEM((count, width, depth), jnp.float32))
    found = pl.pallas_call(
        pack_kernel,
        out_shape=shapes,
        in_specs=[ANY] * 9,
        out_specs=[SMEM] * 2 + [VMEM] * len(CASES),
        scratch_shapes=[
            pltpu.VMEM((6, near, width, depth), jnp.float32),
            pltpu.VMEM((2, near, width, depth), jnp.int32),
            pltpu.SemaphoreType.DMA((8,)),
            pltpu.SemaphoreType.DMA,
        ],
        compiler_params=pltpu.CompilerParams(vmem_limit_bytes=32 * 2**20),
        name="pack",
    )(*(pltpu.with_memory_space_constraint(a, pltpu.HBM) for a in (*arrays, moved)))
    return found[0], found[1], found[2:]


def edges_kernel(sides, *refs):
    own, across = refs[:8], refs[8:]
    planes, width, depth = own[0].shape
    gx = lax.axis_index("gx")
    low = low_half(depth)
    for n, side in enumerate(sides):
        if side == "swap":
            at, high = pl.multiple_of(jnp.where(gx == 0, width - TILE, 0), TILE), gx == 0
        else:
            at, high = (width - TILE, True) if side == "right" else (0, False)
        for a in range(4):
            first = own[a][:, pl.ds(at, TILE)]
            second = own[a + 4][:, pl.ds(at, TILE)].astype(jnp.float32)
            if side == "swap":
                first = jnp.where(high, turned(first), first)
                second = jnp.where(high, second, turned(second))
            elif high:
                first = turned(first)
            else:
                second = turned(second)
            across[n][pl.ds(a * planes, planes)] = jnp.where(low, first, second)


def edges(sides, own):
    planes, width, depth = own[0].shape
    return pl.pallas_call(
        functools.partial(edges_kernel, sides),
        out_shape=[pltpu.VMEM((4 * planes, TILE, depth), jnp.float32)] * len(sides),
        in_specs=[VMEM] * 8,
        out_specs=[VMEM] * len(sides),
        compiler_params=pltpu.CompilerParams(vmem_limit_bytes=32 * 2**20),
        name="edges",
    )(*own)


def lift_kernel(case, *refs):
    own, up = refs[:8], refs[-1]
    planes, width, depth = own[0].shape
    ups = up_counts(case)
    up_at = offsets(ups)
    column = lax.broadcasted_iota(jnp.int32, (width, depth), 0)
    whole, half = column_scales(lax.axis_index("gx") * width + column, width * lax.axis_size("gx"))
    bottom = planes - (3 - case[0])
    for a in range(8):
        if ups[a]:
            up[pl.ds(up_at[a], ups[a])] = own[a][planes - ups[a] :].astype(jnp.float32)
    up[up_at[BX]] = own[BX][bottom] - (TIME_STEP / whole) * own[EY][bottom]
    up[up_at[BY]] = own[BY][bottom] + (TIME_STEP / half) * own[EX][bottom]


def lift(case, own, after):
    planes, width, depth = own[0].shape
    return pl.pallas_call(
        functools.partial(lift_kernel, case),
        out_shape=pltpu.VMEM((sum(up_counts(case)), width, depth), jnp.float32),
        in_specs=[VMEM] * 8 + [ANY] * len(after),
        out_specs=VMEM,
        compiler_params=pltpu.CompilerParams(vmem_limit_bytes=32 * 2**20),
        cost_estimate=pl.CostEstimate(flops=10**7, bytes_accessed=10**7, transcendentals=0),
        name="lift",
    )(*own, *after)


def relay_kernel(case, planes, width, n_sides, *refs):
    beside, (on, off) = refs[:n_sides], refs[n_sides:]
    depth = on.shape[-1]
    moves = case[0]
    gx = lax.axis_index("gx")
    even = lax.axis_index("gz") % 2 == 0
    start = gx * width
    total = width * lax.axis_size("gx")
    low = low_half(depth)
    row = lax.broadcasted_iota(jnp.int32, (TILE, depth), 0)
    bottom = planes - (3 - moves)

    def fill(to_before, to_after):
        for n in range(n_sides):
            if n_sides == 1:
                left_column = jnp.where(gx == 0, start + width, start - HALF)
            else:
                left_column = start - HALF if n == 0 else start + width
            whole, half = column_scales(left_column + jnp.where(row < HALF, row, row - HALF), total)
            step_whole, step_half = TIME_STEP / whole, TIME_STEP / half
            tile = lambda a, plane: beside[n][a * planes + plane]

            def folded(a, plane, source, sign):
                if a == BX:
                    return tile(a, plane) + jnp.where(low, sign * step_whole * tile(EY, source), 0.0)
                return tile(a, plane) - jnp.where(
                    low, 0.0, turned(sign * step_half * tile(EX, source))
                )

            for a in range(4):
                for ref, first, count, folds in (
                    (to_before, 0, moves + 2, ((moves - 1, 1), (moves + 1, 1))),
                    (to_after, bottom, 3 - moves, ((0, 0),)),
                ):
                    to = (n * 4 + a) * count
                    ref[pl.ds(to, count)] = beside[n][pl.ds(a * planes + first, count)]
                    if a in (BX, BY - 4):
                        for plane, above in folds:
                            at = first + plane
                            ref[to + plane] = folded(a, at, at + above, 1.0 if above else -1.0)

    @pl.when(even)
    def _():
        fill(off, on)

    @pl.when(jnp.logical_not(even))
    def _():
        fill(on, off)


def relay(case, shape, beside):
    planes, width, depth = shape
    tiles = pltpu.VMEM((len(beside) * 4 * (case[0] + 2), TILE, depth), jnp.float32)
    return pl.pallas_call(
        functools.partial(relay_kernel, case, planes, width, len(beside)),
        out_shape=[tiles] * 2,
        in_specs=[VMEM] * len(beside),
        out_specs=[VMEM] * 2,
        compiler_params=pltpu.CompilerParams(vmem_limit_bytes=32 * 2**20),
        name="relay",
    )(*beside)


def coefficients(code):
    kind = code.dtype.type
    five, six, seven = code == kind(5), code == kind(6), code == kind(7)
    keep = jnp.where(five, 0.0, jnp.where(six, 0.8 / 1.2, jnp.where(seven, 0.4 / 1.6, 1.0)))
    gain = jnp.where(
        five,
        0.0,
        jnp.where(six, TIME_STEP / 1.2, jnp.where(seven, TIME_STEP / 1.6, TIME_STEP)),
    )
    return keep, gain


def ghost_inside(width, depth):
    gx = lax.axis_index("gx")
    row = lax.broadcasted_iota(jnp.int32, (1, TILE, depth), 1)
    right = gx < lax.axis_size("gx") - 1
    return jnp.where(row < HALF, right.astype(jnp.int32), (gx > 0).astype(jnp.int32)) == 1


def spread_tiles(beside, upper):
    gx = lax.axis_index("gx")
    if len(beside) == 1:
        same = (gx > 0) if upper else (gx == 0)
        return jnp.where(same, beside[0], turned(beside[0]))
    from_left, from_right = beside
    if upper:
        from_right = turned(from_right)
    else:
        from_left = turned(from_left)
    return jnp.where(low_half(from_left.shape[-1]), from_right, from_left)


class Cells:
    def __init__(self, refs, width):
        self.ext, (self.keep, self.gain, self.current, self.rows) = refs[:6], refs[6:]
        self.width = width
        self.tall, self.depth = self.keep.shape[1:]
        self.ghost_in = ghost_inside(width, self.depth)

    def put(self, a, at, count, value, ghost):
        here = pl.ds(at, count)
        where = pl.ds(self.width, TILE) if ghost else pl.ds(0, self.width)
        mask = (lambda v: jnp.where(self.ghost_in, v, 0.0)) if ghost else (lambda v: v)
        if a < 6:
            self.ext[a][here, where] = mask(value)
        elif a == CODES:
            kept, gained = coefficients(value)
            self.keep[here, where], self.gain[here, where] = mask(kept), mask(gained)
        else:
            self.current[here, where] = CURRENT_SCALE * mask(value.astype(jnp.float32))

    def magnetic(self, e, count):
        ext, rows = self.ext, self.rows
        here, above = pl.ds(e, count), pl.ds(e + 1, count)
        ex, ey, es = ext[EX][here], ext[EY][here], ext[ES][here]
        bx = ext[BX][here] - (rows[4] * (next_y(es) - es) - rows[5] * (ext[EY][above] - ey))
        by = ext[BY][here] - rows[6] * ((ext[EX][above] - ex) - (next_x(rows[0] * es) - rows[0] * es))
        bs = ext[BS][here] - rows[4] * ((next_x(ey) - ey) - (next_y(ex) - ex))
        ext[BX][here], ext[BY][here], ext[BS][here] = bx, by, bs

    def electric(self, e, count, moved_now):
        ext, rows = self.ext, self.rows
        here, below, cells = pl.ds(e, count), pl.ds(e - 1, count), pl.ds(e - moved_now, count)
        bx, by, bs = ext[BX][here], ext[BY][here], ext[BS][here]
        kept, gained = self.keep[cells], self.gain[cells]
        ex = kept * ext[EX][here] + gained * ((bs - last_y(bs)) - rows[3] * (by - ext[BY][below]))
        ey = kept * ext[EY][here] + gained * (
            rows[2] * ((bx - ext[BX][below]) - (rows[1] * bs - last_x(rows[1] * bs)))
        )
        es = kept * ext[ES][here] + gained * (
            (by - last_x(by)) - (bx - last_y(bx)) - self.current[cells]
        )
        ext[EX][here], ext[EY][here], ext[ES][here] = ex, ey, es

    def leave(self, plane):
        for a in (BX, BY):
            self.ext[a][plane] = jnp.zeros((self.tall, self.depth), jnp.float32)


def in_groups(start, count, body):
    whole = max(count, 0) // GROUP
    if whole:

        @pl.loop(0, whole)
        def _(i):
            body(start + i * GROUP, GROUP)

    if count > 0 and count % GROUP:
        body(start + whole * GROUP, count % GROUP)


def prepare_kernel(moves, n_sides, moved, *refs):
    own, beside = refs[:8], refs[8 : 8 + n_sides]
    planes, width, depth = own[0].shape
    cells = Cells(refs[8 + n_sides :], width)
    tall, rows = cells.tall, cells.rows
    base = 3 - moves
    top = base + planes - 1
    total = width * lax.axis_size("gx")

    row = lax.broadcasted_iota(jnp.int32, (tall, depth), 0)
    place = lax.axis_index("gx") * width + jnp.where(row < width + HALF, row, row - tall)
    inside = (place >= 0) & (place < total)
    whole, half = column_scales(place, total)
    step = jnp.where(inside, TIME_STEP, 0.0)
    for n, value in enumerate((whole, half, 1.0 / whole, 1.0 / half, step, step / whole, step / half)):
        rows[n] = value
    for a in range(8):
        cells.put(a, base, planes, own[a][...], False)
        tiles = [side[pl.ds(a % 4 * planes, planes)] for side in beside]
        cells.put(a, base, planes, spread_tiles(tiles, a >= 4), True)
    for a in (EX, EY):
        cells.ext[a][0] = jnp.zeros((tall, depth), jnp.float32)
        cells.ext[a][planes + 3] = jnp.zeros((tall, depth), jnp.float32)

    moved_now = 0
    for t in range(STEPS):
        moved_now = moved_now + moved[t]
        in_groups(base + t, planes - 1 - 2 * t, cells.magnetic)

        @pl.when((lax.axis_index("gz") == 0) & (moved_now == t + 1))
        def _():
            cells.leave(base + t)

        in_groups(base + t + 1, planes - 2 - 2 * t, lambda e, n: cells.electric(e, n, moved_now))


def prepare(moves, moved, own, beside):
    planes, width, depth = own[0].shape
    tall = width + TILE
    vmem = lambda *shape: pltpu.VMEM(shape, jnp.float32)
    shapes = [vmem(planes + 4, tall, depth)] * 9
    shapes += [vmem(7, tall, depth)]
    return pl.pallas_call(
        functools.partial(prepare_kernel, moves, len(beside)),
        out_shape=shapes,
        in_specs=[SMEM] + [VMEM] * (8 + len(beside)),
        out_specs=[VMEM] * len(shapes),
        compiler_params=pltpu.CompilerParams(vmem_limit_bytes=32 * 2**20),
        cost_estimate=pl.CostEstimate(flops=32 * 10**8, bytes_accessed=10**7, transcendentals=0),
        name="prepare",
    )(moved, *own, *beside)


def steps_kernel(case, n_sides, planes, width, moved, *refs):
    rows, down, up, on, off = refs[9:14]
    outs = refs[14:20]
    cells = Cells((*refs[20:29], rows), width)
    sems = refs[29]
    ext = cells.ext
    moves = case[0]
    base = 3 - moves
    top = base + planes - 1
    far = planes + 3
    first = lax.axis_index("gz") == 0
    last = lax.axis_index("gz") == lax.axis_size("gz") - 1
    even = lax.axis_index("gz") % 2 == 0
    downs, ups = down_counts(case), up_counts(case)
    at, up_at = offsets(downs[:6]), offsets(ups)
    far_at = at[-1]
    at = at[:6] + [far_at + 4, far_at + 4 + downs[CODES]]
    tiles_at = at[BUNCH] + downs[BUNCH]
    copies = []

    def send(a, start, end):
        if end > start:
            item = pltpu.make_async_copy(
                ext[a].at[pl.ds(start, end - start), pl.ds(0, width)],
                outs[a].at[pl.ds(start - 3, end - start)],
                sems.at[len(copies)],
            )
            item.start()
            copies.append(item)

    for a in range(6):
        send(a, base + (2 if a >= BX else 3), top - 2)

    def corner(a, plane, count, stack, above):
        tiles = []
        for n in range(n_sides):
            span = pl.ds((n * 4 + a % 4) * stack + plane, count)
            tiles.append(jnp.where(even, on[span], off[span]) if above else jnp.where(even, off[span], on[span]))
        return spread_tiles(tiles, a >= 4)

    from_above = lambda a, plane, count: corner(a, plane, count, moves + 2, True)
    for a in range(8):
        if downs[a]:
            cells.put(a, top + 1, downs[a], down[pl.ds(at[a], downs[a])], False)
            cells.put(a, top + 1, downs[a], from_above(a, 0, downs[a]), True)
        if ups[a]:
            cells.put(a, base - ups[a], ups[a], up[pl.ds(up_at[a], ups[a])], False)
            cells.put(a, base - ups[a], ups[a], corner(a, base - ups[a], ups[a], base, False), True)

    low = low_half(cells.depth)
    left, right, ghost = pl.ds(0, TILE), pl.ds(width - TILE, TILE), pl.ds(width, TILE)

    def blocks(right_tile, ghost_tile, left_tile):
        return jnp.where(low, right_tile, ghost_tile), jnp.where(low, ghost_tile, left_tile)

    def kept_blocks(ref, *plane):
        return blocks(*(turned(ref[(*plane, where)]) for where in (right, ghost, left)))

    def sent_blocks(a, n, plane):
        where, here = tile_of(down, tiles_at, n, width)
        tile = down[where, here]
        beyond = jnp.where(cells.ghost_in[0], from_above(a, plane, 1)[0], 0.0)
        return tile, beyond

    def both(tiles):
        return blocks(tiles[0], turned(tiles[1]), tiles[0])

    const = [kept_blocks(rows, n) for n in range(7)]

    def block_magnetic(fields, next_e, b):
        ex, ey, es, bx, by, bs = fields
        row = [v[b] for v in const]
        weighted = row[0] * es
        above_x, above_y = next_e if next_e else (0.0, 0.0)
        bx = bx - row[4] * (next_y(es) - es) + row[5] * (above_y - ey)
        by = by - row[6] * ((above_x - ex) - (next_x(weighted) - weighted))
        bs = bs - row[4] * ((next_x(ey) - ey) - (next_y(ex) - ex))
        return ex, ey, es, bx, by, bs

    def block_electric(fields, below, factors, b):
        ex, ey, _, bx, by, bs = fields
        row = [v[b] for v in const]
        kept, gained = factors
        weighted = row[1] * bs
        ex = kept * ex + gained * ((bs - last_y(bs)) - row[3] * (by - below[1]))
        ey = kept * ey + gained * (row[2] * ((bx - below[0]) - (weighted - last_x(weighted))))
        return ex, ey

    tile_row = lax.broadcasted_iota(jnp.int32, (TILE, cells.depth), 0)

    def set_far(values, found, edge):
        for a in (EX, EY):
            right_block, left_block = found[0][a], found[1][a]
            ext[a][far, pl.ds(0, width)] = jnp.where(last, 0.0, values[a])
            at_right = jnp.where(tile_row >= TILE - edge, turned(right_block), values[a][width - TILE :])
            at_left = jnp.where(tile_row < edge, turned(left_block), values[a][:TILE])
            ext[a][far, right] = jnp.where(last, 0.0, at_right)
            ext[a][far, left] = jnp.where(last, 0.0, at_left)
            beyond = turned(jnp.where(low, left_block, right_block))
            ext[a][far, ghost] = jnp.where(last, 0.0, beyond)

    def far_first(moved_now):
        planes_raw = [[both(sent_blocks(a, n * 7 + a, moves + n)) for a in range(6)] for n in range(2)]
        bunch = both(sent_blocks(BUNCH, 6, moves - case[1]))
        tile, beyond = sent_blocks(CODES, 13, moves + 1 - case[1])
        over = [both(pair) for pair in zip(coefficients(tile), coefficients(beyond))]
        own = [kept_blocks(ref, far - moved_now) for ref in (cells.keep, cells.gain)]
        below = [kept_blocks(ext[a], far - 1) for a in (BX, BY)]
        state = []
        for b in range(2):
            raw, raw_over = ([v[b] for v in plane] for plane in planes_raw)
            mine = block_magnetic(raw, raw_over[:2], b)
            theirs = block_magnetic(raw_over, None, b)
            factors = [v[b] for v in own]
            ex, ey = block_electric(mine, [v[b] for v in below], factors, b)
            ex_over, ey_over = block_electric(theirs, mine[3:5], [v[b] for v in over], b)
            bx, by = mine[3:5]
            es = factors[0] * mine[2] + factors[1] * (
                (by - last_x(by)) - (bx - last_y(bx)) - CURRENT_SCALE * bunch[b]
            )
            state.append(((ex, ey, es, *mine[3:]), (ex_over, ey_over)))
        set_far([down[far_at], down[far_at + 1]], [fields[:2] for fields, _ in state], 1)
        return state

    def far_second(state, moved_now):
        own = [kept_blocks(ref, far - moved_now) for ref in (cells.keep, cells.gain)]
        below = [kept_blocks(ext[a], far - 1) for a in (BX, BY)]
        found = []
        for b in range(2):
            fields = block_magnetic(*state[b], b)
            found.append(block_electric(fields, [v[b] for v in below], [v[b] for v in own], b))
        gained = cells.gain[far - moved_now, mine]
        ex = down[far_at + 2] + gained * (rows[3, mine] * ext[BY][far - 1, mine])
        ey = down[far_at + 3] - gained * (rows[2, mine] * ext[BX][far - 1, mine])
        set_far([ex, ey], found, 2)

    mine = pl.ds(0, width)
    moved_now = 0
    for t in range(STEPS):
        moved_now = moved_now + moved[t]
        above = moves + 1 + t
        cells.magnetic(t, base)
        cells.magnetic(top - t, above)

        @pl.when(first)
        def _():
            cells.leave(base + moved_now - 1)

        if t == STEPS - 1:
            for a in (BX, BY, BS):
                send(a, 3, base + 2)
                send(a, top - 2, planes + 3)
        cells.electric(t + 1, base, moved_now)
        if t == STEPS - 1:
            for a in (EX, EY, ES):
                send(a, 3, base + 3)
        cells.electric(top - t, above, moved_now)
        if t == 0:
            edge_state = far_first(moved_now)
        elif t == 1:
            far_second(edge_state, moved_now)
        if t == STEPS - 1:
            for a in (EX, EY, ES):
                send(a, top - 2, planes + 3)
        else:

            @pl.when(last)
            def _():
                for a in (EX, EY, ES):
                    ext[a][top + 1 + moved_now] = jnp.zeros((cells.tall, cells.depth), jnp.float32)

    for item in copies:
        item.wait()


def advance(case, n_sides, moved, shape, ready, ghosts):
    planes, width, depth = shape
    block = jax.ShapeDtypeStruct(shape, jnp.float32)
    n_in = 11 + len(ghosts)
    found = pl.pallas_call(
        functools.partial(steps_kernel, case, n_sides, planes, width),
        out_shape=[block] * 6 + [pltpu.VMEM(x.shape, x.dtype) for x in ready[:9]],
        in_specs=[SMEM] + [VMEM] * (n_in - 1),
        out_specs=[ANY] * 6 + [VMEM] * 9,
        input_output_aliases={1 + n: 6 + n for n in range(9)},
        scratch_shapes=[pltpu.SemaphoreType.DMA((18,))],
        compiler_params=pltpu.CompilerParams(vmem_limit_bytes=32 * 2**20),
        name="steps",
    )(moved, *ready, *ghosts)
    return tuple(found[:6])


def passed(block, to, sides=(0,)):
    size_z, size_x = lax.axis_size("gz"), lax.axis_size("gx")
    route = [
        (z * size_x + x, to(z) * size_x + x + dx)
        for z in range(size_z)
        for x in range(size_x)
        for dx in sides
        if 0 <= to(z) < size_z and 0 <= x + dx < size_x
    ]
    return lax.ppermute(block, ("gz", "gx"), route)


def on_device(*args):
    arrays, moved = args[:8], args[8]
    arrays = arrays[:6] + (arrays[7], arrays[6])
    sides = ("swap",) if lax.axis_size("gx") == 2 else ("right", "left")
    which, moved, sent = pack(arrays, moved)

    def run(c, own, sent, moved):
        case = CASES[c]
        down = passed(sent[c], lambda z: z - 1)
        across = edges(sides, own)
        ways = {"swap": (1, -1), "right": (1,), "left": (-1,)}
        beside = [passed(block, lambda z: z, ways[side]) for block, side in zip(across, sides)]
        up = passed(lift(case, own, across), lambda z: z + 1)
        on, off = relay(case, own[0].shape, beside)
        on, off = passed(on, lambda z: z ^ 1), passed(off, lambda z: z + 1 if z % 2 else z - 1)
        ready = prepare(case[0], moved, own, beside)
        return advance(case, len(sides), moved, own[0].shape, ready, [down, up, on, off])

    return lax.switch(
        which[0],
        [functools.partial(run, c) for c in range(len(CASES))],
        arrays,
        sent,
        moved,
    )


def solution(mesh):
    block = P("gz", "gx", None)
    return jax.shard_map(
        on_device,
        mesh=mesh,
        in_specs=(block,) * 8 + (P(),),
        out_specs=(block,) * 6,
        check_vma=False,
    )
```

```python
import functools

import jax
import jax.numpy as jnp
from jax import lax
from jax.experimental import pallas as pl
from jax.experimental.pallas import tpu as pltpu
from jax.sharding import PartitionSpec as P

STEPS = 3
TILE = 8
HALF = 4
GROUP = 4
TIME_STEP = 0.5
CURRENT_SCALE = 0.1
VMEM = pl.BlockSpec(memory_space=pltpu.VMEM)
SMEM = pl.BlockSpec(memory_space=pltpu.SMEM)
ANY = pl.BlockSpec(memory_space=pl.ANY)
EX, EY, ES, BX, BY, BS, CODES, BUNCH = range(8)
CASES = ((1, 1), (1, 0), (2, 1), (2, 0))


def down_counts(case):
    moves, now = case
    later = moves - now
    return (moves,) * 6 + (later + 1, later)


def up_counts(case):
    moves, now = case
    later = moves - now
    if moves == 1:
        return (0,) * 6 + (2 - later, 1)
    return (0, 0, 1, 1, 1, 0, 2 - later, 2 - later)


def up_traces(case):
    return (4, 10) if case[0] == 1 else (0, 0)


def offsets(counts):
    starts = [0]
    for count in counts:
        starts.append(starts[-1] + count)
    return starts


def tile_planes(count, width):
    return -(-count // (width // TILE))


def tile_of(ref, start, n, width):
    per_plane = width // TILE
    return start + n // per_plane, pl.ds(n % per_plane * TILE, TILE)


def column_scales(place, total):
    place = place.astype(jnp.float32)
    whole = 1.0 + (place - total / 2) / (2 * total)
    half = 1.0 + (place + 0.5 - total / 2) / (2 * total)
    return whole, half


def turned(tiles):
    return pltpu.roll(tiles, HALF, tiles.ndim - 2)


def next_y(v):
    depth = v.shape[-1]
    lane = lax.broadcasted_iota(jnp.int32, v.shape[-2:], 1)
    return jnp.where(lane < depth - 1, pltpu.roll(v, depth - 1, v.ndim - 1), 0.0)


def last_y(v):
    lane = lax.broadcasted_iota(jnp.int32, v.shape[-2:], 1)
    return jnp.where(lane > 0, pltpu.roll(v, 1, v.ndim - 1), 0.0)


def next_x(v):
    return pltpu.roll(v, v.shape[-2] - 1, v.ndim - 2)


def last_x(v):
    return pltpu.roll(v, 1, v.ndim - 2)


def low_half(depth):
    return lax.broadcasted_iota(jnp.int32, (TILE, depth), 0) < HALF


def tile_of_edges(v):
    return jnp.where(low_half(v.shape[-1]), turned(v[-TILE:]), turned(v[:TILE]))


class Plane:
    def __init__(self, start, width, depth, total):
        row = lax.broadcasted_iota(jnp.int32, (width, depth), 0)
        self.whole, self.half = column_scales(start + row, total)
        self.one_whole, self.one_half = 1.0 / self.whole, 1.0 / self.half
        self.step_whole, self.step_half = TIME_STEP * self.one_whole, TIME_STEP * self.one_half

    def add_above(self, bx, by, ex, ey):
        return bx + self.step_whole * ey, by - self.step_half * ex

    def radial_vertical(self, bx, by, ex, ey, es):
        weighted = self.whole * es
        bx = bx - TIME_STEP * (next_y(es) - es) - self.step_whole * ey
        by = by + self.step_half * (ex + next_x(weighted) - weighted)
        return bx, by

    def longitudinal(self, bs, ex, ey):
        return bs - TIME_STEP * ((next_x(ey) - ey) - (next_y(ex) - ex))

    def electric(self, ex, ey, bs, over_x, over_y, factors):
        kept, gained = factors
        weighted = self.half * bs
        ex = kept * ex + gained * ((bs - last_y(bs)) - self.one_half * over_y)
        ey = kept * ey + gained * (self.one_whole * (over_x - (weighted - last_x(weighted))))
        return ex, ey

    def electric_s(self, es, bx, by, bunch, factors):
        current = CURRENT_SCALE * bunch.astype(jnp.float32)
        return factors[0] * es + factors[1] * ((by - last_x(by)) - (bx - last_y(bx)) - current)


def pack_kernel(*refs):
    sources, moved = refs[:8], refs[8]
    which, moved_here = refs[9:11]
    sent = refs[11 : 11 + len(CASES)]
    near, near_int, sems, moved_sem = refs[11 + len(CASES) :]
    _, _, width, depth = near.shape
    most = max(case[0] for case in CASES)
    fetched = (most + 3,) * 2 + (most + 2,) * 5 + (most + 1,)
    gx = lax.axis_index("gx")
    total = width * lax.axis_size("gx")

    get_moved = pltpu.make_async_copy(moved, moved_here, moved_sem)
    get_moved.start()
    copies = []
    for a in range(8):
        span = pl.ds(0, fetched[a])
        goal = near.at[a, span] if a < 6 else near_int.at[a - 6, span]
        copies.append(pltpu.make_async_copy(sources[a].at[span], goal, sems.at[a]))
        copies[-1].start()
    get_moved.wait()
    now = moved_here[0]
    later = moved_here[1] + moved_here[2]
    case_index = jnp.where(now + later == 1, 1 - now, 3 - now)
    which[0] = case_index

    flat = Plane(gx * width, width, depth, total)
    for item in copies[:6]:
        item.wait()

    for c, case in enumerate(CASES):
        down = sent[c]
        downs = down_counts(case)
        at = offsets(downs[:6])
        far, first_move = case

        @pl.when(case_index == c)
        def _():
            field = lambda a, plane: near[a, plane]
            for a in range(6):
                down[pl.ds(at[a], far)] = near[a, :far]

            folded, now_b = {}, {}
            for plane in range(far - 1, far + 2):
                above = field(EX, plane + 1), field(EY, plane + 1)
                folded[plane] = flat.add_above(field(BX, plane), field(BY, plane), *above)
                fields = field(EX, plane), field(EY, plane), field(ES, plane)
                now_b[plane] = flat.radial_vertical(*folded[plane], *fields)
            down[at[BX] + far - 1], down[at[BY] + far - 1] = folded[far - 1]
            for item in copies[6:]:
                item.wait()
            now_e, now_s = {}, {}
            for plane in (far, far + 1):
                ex, ey = field(EX, plane), field(EY, plane)
                now_s[plane] = flat.longitudinal(field(BS, plane), ex, ey)
                factors = coefficients(near_int[0, plane - first_move])
                over = [up - under for up, under in zip(now_b[plane], now_b[plane - 1])]
                now_e[plane] = flat.electric(ex, ey, now_s[plane], *over, factors)
                if plane == far:
                    bunch = near_int[1, far - first_move]
                    es = flat.electric_s(field(ES, far), *now_b[far], bunch, factors)
            place = at[-1]
            down[place], down[place + 1] = now_e[far]

            bx, by = flat.add_above(*now_b[far], *now_e[far + 1])
            bx, by = flat.radial_vertical(bx, by, *now_e[far], es)
            bs = flat.longitudinal(now_s[far], *now_e[far])
            factors = coefficients(near_int[0, far - (first_move + moved_here[1])])
            down[place + 2], down[place + 3] = flat.electric(*now_e[far], bs, bx, by, factors)

            place += 4
            for n, a in enumerate((CODES, BUNCH)):
                if downs[a]:
                    down[pl.ds(place, downs[a])] = near_int[n, : downs[a]].astype(jnp.float32)
                place += downs[a]
            tiles = [field(a, far) for a in range(6)]
            tiles.append(near_int[1, far - first_move].astype(jnp.float32))
            tiles += [field(EX, far + 1), field(EY, far + 1), field(ES, far + 1)]
            tiles += [*folded[far + 1], field(BS, far + 1)]
            tiles.append(near_int[0, far + 1 - first_move].astype(jnp.float32))
            for n, v in enumerate(tiles):
                plane, rows = tile_of(down, place, n, width)
                down[plane, rows] = tile_of_edges(v)


def pack(arrays, moved):
    planes, width, depth = arrays[0].shape
    near = max(case[0] for case in CASES) + 3
    shapes = [pltpu.SMEM((1,), jnp.int32), pltpu.SMEM((STEPS,), jnp.int32)]
    for case in CASES:
        count = sum(down_counts(case)) + 4 + tile_planes(14, width)
        shapes.append(pltpu.VMEM((count, width, depth), jnp.float32))
    found = pl.pallas_call(
        pack_kernel,
        out_shape=shapes,
        in_specs=[ANY] * 9,
        out_specs=[SMEM] * 2 + [VMEM] * len(CASES),
        scratch_shapes=[
            pltpu.VMEM((6, near, width, depth), jnp.float32),
            pltpu.VMEM((2, near, width, depth), jnp.int32),
            pltpu.SemaphoreType.DMA((8,)),
            pltpu.SemaphoreType.DMA,
        ],
        compiler_params=pltpu.CompilerParams(vmem_limit_bytes=32 * 2**20),
        name="pack",
    )(*(pltpu.with_memory_space_constraint(a, pltpu.HBM) for a in (*arrays, moved)))
    return found[0], found[1], found[2:]


def edges_kernel(sides, *refs):
    own, across = refs[:8], refs[8:]
    planes, width, depth = own[0].shape
    gx = lax.axis_index("gx")
    low = low_half(depth)
    for n, side in enumerate(sides):
        if side == "swap":
            at, high = pl.multiple_of(jnp.where(gx == 0, width - TILE, 0), TILE), gx == 0
        else:
            at, high = (width - TILE, True) if side == "right" else (0, False)
        for a in range(4):
            first = own[a][:, pl.ds(at, TILE)]
            second = own[a + 4][:, pl.ds(at, TILE)].astype(jnp.float32)
            if side == "swap":
                first = jnp.where(high, turned(first), first)
                second = jnp.where(high, second, turned(second))
            elif high:
                first = turned(first)
            else:
                second = turned(second)
            across[n][pl.ds(a * planes, planes)] = jnp.where(low, first, second)


def edges(sides, own):
    planes, width, depth = own[0].shape
    return pl.pallas_call(
        functools.partial(edges_kernel, sides),
        out_shape=[pltpu.VMEM((4 * planes, TILE, depth), jnp.float32)] * len(sides),
        in_specs=[VMEM] * 8,
        out_specs=[VMEM] * len(sides),
        compiler_params=pltpu.CompilerParams(vmem_limit_bytes=32 * 2**20),
        name="edges",
    )(*own)


def lift_kernel(case, *refs):
    own, up = refs[:8], refs[-1]
    planes, width, depth = own[0].shape
    ups = up_counts(case)
    traces, n_tiles = up_traces(case)
    at = [traces + n for n in offsets(ups)]
    flat = Plane(lax.axis_index("gx") * width, width, depth, width * lax.axis_size("gx"))
    for a in range(8):
        if ups[a]:
            up[pl.ds(at[a], ups[a])] = own[a][planes - ups[a] :].astype(jnp.float32)
    bottom = planes - (3 - case[0])
    ex, ey, es, bx, by, bs = (own[a][bottom] for a in range(6))
    under = flat.add_above(bx, by, -ex, -ey)
    if not traces:
        up[at[BX]], up[at[BY]] = under
        return
    edge = [es, *under]
    fields = [own[a][bottom + 1] for a in range(6)]
    edge += fields
    below_x, below_y = flat.radial_vertical(*flat.add_above(bx, by, *fields[:2]), ex, ey, es)
    ex, ey, es, bx, by, bs = fields
    bx, by = flat.radial_vertical(bx, by, ex, ey, es)
    bs = flat.longitudinal(bs, ex, ey)
    up[0], up[1] = bx, by
    factors = coefficients(own[CODES][planes - 1 - case[1]])
    bunch = own[BUNCH][planes - 1 - case[1]]
    ex, ey = flat.electric(ex, ey, bs, bx - below_x, by - below_y, factors)
    es = flat.electric_s(es, bx, by, bunch, factors)
    up[2], up[3] = flat.radial_vertical(bx, by, ex, ey, es)
    edge.append(bunch.astype(jnp.float32))
    for n, v in enumerate(edge):
        plane, rows = tile_of(up, at[-1], n, width)
        up[plane, rows] = tile_of_edges(v)


def lift(case, own, after):
    planes, width, depth = own[0].shape
    traces, n_tiles = up_traces(case)
    count = sum(up_counts(case)) + traces + tile_planes(n_tiles, width)
    return pl.pallas_call(
        functools.partial(lift_kernel, case),
        out_shape=pltpu.VMEM((count, width, depth), jnp.float32),
        in_specs=[VMEM] * 8 + [ANY] * len(after),
        out_specs=VMEM,
        compiler_params=pltpu.CompilerParams(vmem_limit_bytes=32 * 2**20),
        cost_estimate=pl.CostEstimate(flops=10**7, bytes_accessed=10**7, transcendentals=0),
        name="lift",
    )(*own, *after)


def relay_kernel(case, planes, width, n_sides, *refs):
    beside, (on, off) = refs[:n_sides], refs[n_sides:]
    depth = on.shape[-1]
    moves = case[0]
    gx = lax.axis_index("gx")
    even = lax.axis_index("gz") % 2 == 0
    start = gx * width
    total = width * lax.axis_size("gx")
    low = low_half(depth)
    row = lax.broadcasted_iota(jnp.int32, (TILE, depth), 0)
    bottom = planes - (3 - moves)

    def fill(to_before, to_after):
        for n in range(n_sides):
            if n_sides == 1:
                left_column = jnp.where(gx == 0, start + width, start - HALF)
            else:
                left_column = start - HALF if n == 0 else start + width
            whole, half = column_scales(left_column + jnp.where(row < HALF, row, row - HALF), total)
            step_whole, step_half = TIME_STEP / whole, TIME_STEP / half
            tile = lambda a, plane: beside[n][a * planes + plane]

            def folded(a, plane, source, sign):
                if a == BX:
                    return tile(a, plane) + jnp.where(low, sign * step_whole * tile(EY, source), 0.0)
                return tile(a, plane) - jnp.where(
                    low, 0.0, turned(sign * step_half * tile(EX, source))
                )

            for a in range(4):
                for ref, first, count, folds in (
                    (to_before, 0, moves + 2, ((moves - 1, 1), (moves + 1, 1))),
                    (to_after, bottom, 3 - moves, ((0, 0),)),
                ):
                    to = (n * 4 + a) * count
                    ref[pl.ds(to, count)] = beside[n][pl.ds(a * planes + first, count)]
                    if a in (BX, BY - 4):
                        for plane, above in folds:
                            at = first + plane
                            ref[to + plane] = folded(a, at, at + above, 1.0 if above else -1.0)

    @pl.when(even)
    def _():
        fill(off, on)

    @pl.when(jnp.logical_not(even))
    def _():
        fill(on, off)


def relay(case, shape, beside):
    planes, width, depth = shape
    tiles = pltpu.VMEM((len(beside) * 4 * (case[0] + 2), TILE, depth), jnp.float32)
    return pl.pallas_call(
        functools.partial(relay_kernel, case, planes, width, len(beside)),
        out_shape=[tiles] * 2,
        in_specs=[VMEM] * len(beside),
        out_specs=[VMEM] * 2,
        compiler_params=pltpu.CompilerParams(vmem_limit_bytes=32 * 2**20),
        name="relay",
    )(*beside)


def coefficients(code):
    kind = code.dtype.type
    five, six, seven = code == kind(5), code == kind(6), code == kind(7)
    keep = jnp.where(five, 0.0, jnp.where(six, 0.8 / 1.2, jnp.where(seven, 0.4 / 1.6, 1.0)))
    gain = jnp.where(
        five,
        0.0,
        jnp.where(six, TIME_STEP / 1.2, jnp.where(seven, TIME_STEP / 1.6, TIME_STEP)),
    )
    return keep, gain


def ghost_inside(width, depth):
    gx = lax.axis_index("gx")
    row = lax.broadcasted_iota(jnp.int32, (1, TILE, depth), 1)
    right = gx < lax.axis_size("gx") - 1
    return jnp.where(row < HALF, right.astype(jnp.int32), (gx > 0).astype(jnp.int32)) == 1


def spread_tiles(beside, upper):
    gx = lax.axis_index("gx")
    if len(beside) == 1:
        same = (gx > 0) if upper else (gx == 0)
        return jnp.where(same, beside[0], turned(beside[0]))
    from_left, from_right = beside
    if upper:
        from_right = turned(from_right)
    else:
        from_left = turned(from_left)
    return jnp.where(low_half(from_left.shape[-1]), from_right, from_left)


class Cells:
    def __init__(self, refs, width):
        self.ext, (self.keep, self.gain, self.current, self.rows) = refs[:6], refs[6:]
        self.width = width
        self.tall, self.depth = self.keep.shape[1:]
        self.ghost_in = ghost_inside(width, self.depth)

    def put(self, a, at, count, value, ghost):
        here = pl.ds(at, count)
        where = pl.ds(self.width, TILE) if ghost else pl.ds(0, self.width)
        mask = (lambda v: jnp.where(self.ghost_in, v, 0.0)) if ghost else (lambda v: v)
        if a < 6:
            self.ext[a][here, where] = mask(value)
        elif a == CODES:
            kept, gained = coefficients(value)
            self.keep[here, where], self.gain[here, where] = mask(kept), mask(gained)
        else:
            self.current[here, where] = CURRENT_SCALE * mask(value.astype(jnp.float32))

    def magnetic(self, e, count):
        ext, rows = self.ext, self.rows
        here, above = pl.ds(e, count), pl.ds(e + 1, count)
        ex, ey, es = ext[EX][here], ext[EY][here], ext[ES][here]
        bx = ext[BX][here] - (rows[4] * (next_y(es) - es) - rows[5] * (ext[EY][above] - ey))
        by = ext[BY][here] - rows[6] * ((ext[EX][above] - ex) - (next_x(rows[0] * es) - rows[0] * es))
        bs = ext[BS][here] - rows[4] * ((next_x(ey) - ey) - (next_y(ex) - ex))
        ext[BX][here], ext[BY][here], ext[BS][here] = bx, by, bs

    def electric(self, e, count, moved_now):
        ext, rows = self.ext, self.rows
        here, below, cells = pl.ds(e, count), pl.ds(e - 1, count), pl.ds(e - moved_now, count)
        bx, by, bs = ext[BX][here], ext[BY][here], ext[BS][here]
        kept, gained = self.keep[cells], self.gain[cells]
        ex = kept * ext[EX][here] + gained * ((bs - last_y(bs)) - rows[3] * (by - ext[BY][below]))
        ey = kept * ext[EY][here] + gained * (
            rows[2] * ((bx - ext[BX][below]) - (rows[1] * bs - last_x(rows[1] * bs)))
        )
        es = kept * ext[ES][here] + gained * (
            (by - last_x(by)) - (bx - last_y(bx)) - self.current[cells]
        )
        ext[EX][here], ext[EY][here], ext[ES][here] = ex, ey, es

    def leave(self, plane):
        for a in (BX, BY):
            self.ext[a][plane] = jnp.zeros((self.tall, self.depth), jnp.float32)


def in_groups(start, count, body):
    whole = max(count, 0) // GROUP
    if whole:

        @pl.loop(0, whole)
        def _(i):
            body(start + i * GROUP, GROUP)

    if count > 0 and count % GROUP:
        body(start + whole * GROUP, count % GROUP)


def prepare_kernel(moves, n_sides, moved, *refs):
    own, beside = refs[:8], refs[8 : 8 + n_sides]
    planes, width, depth = own[0].shape
    cells = Cells(refs[8 + n_sides :], width)
    tall, rows = cells.tall, cells.rows
    base = 3 - moves
    top = base + planes - 1
    total = width * lax.axis_size("gx")

    row = lax.broadcasted_iota(jnp.int32, (tall, depth), 0)
    place = lax.axis_index("gx") * width + jnp.where(row < width + HALF, row, row - tall)
    inside = (place >= 0) & (place < total)
    whole, half = column_scales(place, total)
    step = jnp.where(inside, TIME_STEP, 0.0)
    for n, value in enumerate((whole, half, 1.0 / whole, 1.0 / half, step, step / whole, step / half)):
        rows[n] = value
    for a in range(8):
        cells.put(a, base, planes, own[a][...], False)
        tiles = [side[pl.ds(a % 4 * planes, planes)] for side in beside]
        cells.put(a, base, planes, spread_tiles(tiles, a >= 4), True)
    for a in (EX, EY):
        cells.ext[a][0] = jnp.zeros((tall, depth), jnp.float32)
        cells.ext[a][planes + 3] = jnp.zeros((tall, depth), jnp.float32)

    moved_now = 0
    for t in range(STEPS):
        moved_now = moved_now + moved[t]
        in_groups(base + t, planes - 1 - 2 * t, cells.magnetic)

        @pl.when((lax.axis_index("gz") == 0) & (moved_now == t + 1))
        def _():
            cells.leave(base + t)

        in_groups(base + t + 1, planes - 2 - 2 * t, lambda e, n: cells.electric(e, n, moved_now))


def prepare(moves, moved, own, beside):
    planes, width, depth = own[0].shape
    tall = width + TILE
    vmem = lambda *shape: pltpu.VMEM(shape, jnp.float32)
    shapes = [vmem(planes + 4, tall, depth)] * 9
    shapes += [vmem(7, tall, depth)]
    return pl.pallas_call(
        functools.partial(prepare_kernel, moves, len(beside)),
        out_shape=shapes,
        in_specs=[SMEM] + [VMEM] * (8 + len(beside)),
        out_specs=[VMEM] * len(shapes),
        compiler_params=pltpu.CompilerParams(vmem_limit_bytes=32 * 2**20),
        cost_estimate=pl.CostEstimate(flops=27 * 10**8, bytes_accessed=10**7, transcendentals=0),
        name="prepare",
    )(moved, *own, *beside)


def steps_kernel(case, n_sides, planes, width, moved, *refs):
    rows, down, up, on, off = refs[9:14]
    outs = refs[14:20]
    cells = Cells((*refs[20:29], rows), width)
    sems = refs[29]
    ext = cells.ext
    moves = case[0]
    base = 3 - moves
    top = base + planes - 1
    far = planes + 3
    first = lax.axis_index("gz") == 0
    last = lax.axis_index("gz") == lax.axis_size("gz") - 1
    even = lax.axis_index("gz") % 2 == 0
    downs, ups = down_counts(case), up_counts(case)
    traces, _ = up_traces(case)
    at, up_at = offsets(downs[:6]), [traces + n for n in offsets(ups)]
    far_at = at[-1]
    at = at[:6] + [far_at + 4, far_at + 4 + downs[CODES]]
    tiles_at = at[BUNCH] + downs[BUNCH]
    copies = []

    def send(a, start, end):
        if end > start:
            item = pltpu.make_async_copy(
                ext[a].at[pl.ds(start, end - start), pl.ds(0, width)],
                outs[a].at[pl.ds(start - 3, end - start)],
                sems.at[len(copies)],
            )
            item.start()
            copies.append(item)

    for a in range(6):
        send(a, base + (2 if a >= BX else 3), top - 2)

    def corner(a, plane, count, stack, above):
        tiles = []
        for n in range(n_sides):
            span = pl.ds((n * 4 + a % 4) * stack + plane, count)
            tiles.append(jnp.where(even, on[span], off[span]) if above else jnp.where(even, off[span], on[span]))
        return spread_tiles(tiles, a >= 4)

    from_above = lambda a, plane, count: corner(a, plane, count, moves + 2, True)
    for a in range(8):
        if downs[a]:
            cells.put(a, top + 1, downs[a], down[pl.ds(at[a], downs[a])], False)
            cells.put(a, top + 1, downs[a], from_above(a, 0, downs[a]), True)
        if ups[a]:
            cells.put(a, base - ups[a], ups[a], up[pl.ds(up_at[a], ups[a])], False)
            cells.put(a, base - ups[a], ups[a], corner(a, base - ups[a], ups[a], base, False), True)

    low = low_half(cells.depth)
    left, right, ghost = pl.ds(0, TILE), pl.ds(width - TILE, TILE), pl.ds(width, TILE)

    def blocks(right_tile, ghost_tile, left_tile):
        return jnp.where(low, right_tile, ghost_tile), jnp.where(low, ghost_tile, left_tile)

    def kept_blocks(ref, *plane):
        return blocks(*(turned(ref[(*plane, where)]) for where in (right, ghost, left)))

    def sent_blocks(a, n, plane, above=True):
        message, start = (down, tiles_at) if above else (up, up_at[-1])
        where, here = tile_of(message, start, n, width)
        ghosts = corner(a, plane, 1, moves + 2 if above else base, above)[0]
        return message[where, here], jnp.where(cells.ghost_in[0], ghosts, 0.0)

    def both(tiles):
        return blocks(tiles[0], turned(tiles[1]), tiles[0])

    const = [kept_blocks(rows, n) for n in range(7)]

    def block_magnetic(fields, next_e, b):
        ex, ey, es, bx, by, bs = fields
        row = [v[b] for v in const]
        weighted = row[0] * es
        above_x, above_y = next_e if next_e else (0.0, 0.0)
        bx = bx - row[4] * (next_y(es) - es) + row[5] * (above_y - ey)
        by = by - row[6] * ((above_x - ex) - (next_x(weighted) - weighted))
        bs = bs - row[4] * ((next_x(ey) - ey) - (next_y(ex) - ex))
        return ex, ey, es, bx, by, bs

    def block_electric(fields, below, factors, b):
        ex, ey, _, bx, by, bs = fields
        row = [v[b] for v in const]
        kept, gained = factors
        weighted = row[1] * bs
        ex = kept * ex + gained * ((bs - last_y(bs)) - row[3] * (by - below[1]))
        ey = kept * ey + gained * (row[2] * ((bx - below[0]) - (weighted - last_x(weighted))))
        return ex, ey

    def block_electric_s(fields, bunch, factors):
        bx, by = fields[3:5]
        return factors[0] * fields[2] + factors[1] * (
            (by - last_x(by)) - (bx - last_y(bx)) - CURRENT_SCALE * bunch
        )

    tile_row = lax.broadcasted_iota(jnp.int32, (TILE, cells.depth), 0)

    def with_edges(value, right_block, left_block):
        at_right = jnp.where(tile_row >= TILE - 2, turned(right_block), value[width - TILE :])
        at_left = jnp.where(tile_row < 2, turned(left_block), value[:TILE])
        beyond = turned(jnp.where(low, left_block, right_block))
        return jnp.concatenate([at_left, value[TILE : width - TILE], at_right, beyond], 0)

    def set_far(values, found):
        for a in (EX, EY):
            value = with_edges(values[a], found[0][a], found[1][a])
            ext[a][far] = jnp.where(last, 0.0, value)

    def below_first(moved_now):
        es_under, bx_under, by_under = (
            both(sent_blocks(a, n, 0, False)) for n, a in enumerate((ES, BX, BY))
        )
        raw = [both(sent_blocks(a, 3 + a, 1, False)) for a in range(6)]
        bunch = both(sent_blocks(BUNCH, 9, 1 - case[1], False))
        own = [kept_blocks(ref, 1 - moved_now) for ref in (cells.keep, cells.gain)]
        found = []
        for b in range(2):
            fields, factors = [v[b] for v in raw], [v[b] for v in own]
            zero = jnp.zeros_like(fields[0])
            under = (zero, zero, es_under[b], bx_under[b], by_under[b], zero)
            under = block_magnetic(under, fields[:2], b)[3:5]
            fields = block_magnetic(fields, None, b)
            first_b = fields[3:5]
            es = block_electric_s(fields, bunch[b], factors)
            ex, ey = block_electric(fields, under, factors, b)
            found.append((first_b, block_magnetic((ex, ey, es, *fields[3:]), None, b)[3:5]))
        once = [with_edges(up[n], found[0][0][n], found[1][0][n]) for n in range(2)]
        twice = [with_edges(up[2 + n], found[0][1][n], found[1][1][n]) for n in range(2)]

        bx, by = rows[5] * ext[EY][base], -rows[6] * ext[EX][base]
        gained = cells.gain[1 - moved_now]
        ex, ey = -gained * (rows[3] * by), gained * (rows[2] * bx)
        es = gained * ((by - last_x(by)) - (bx - last_y(bx)))
        weighted = rows[0] * es
        ext[BX][1], ext[BY][1] = once[0] + bx, once[1] + by
        bx = bx - rows[4] * (next_y(es) - es) - rows[5] * ey
        by = by + rows[6] * (ex + next_x(weighted) - weighted)
        return twice[0] + bx, twice[1] + by

    def below_second(state):
        ext[BX][1] = state[0] + rows[5] * ext[EY][base]
        ext[BY][1] = state[1] - rows[6] * ext[EX][base]

    def far_first(moved_now):
        planes_raw = [[both(sent_blocks(a, n * 7 + a, moves + n)) for a in range(6)] for n in range(2)]
        bunch = both(sent_blocks(BUNCH, 6, moves - case[1]))
        tile, beyond = sent_blocks(CODES, 13, moves + 1 - case[1])
        over = [both(pair) for pair in zip(coefficients(tile), coefficients(beyond))]
        own = [kept_blocks(ref, far - moved_now) for ref in (cells.keep, cells.gain)]
        below = [kept_blocks(ext[a], far - 1) for a in (BX, BY)]
        state = []
        for b in range(2):
            raw, raw_over = ([v[b] for v in plane] for plane in planes_raw)
            mine = block_magnetic(raw, raw_over[:2], b)
            theirs = block_magnetic(raw_over, None, b)
            factors = [v[b] for v in own]
            ex, ey = block_electric(mine, [v[b] for v in below], factors, b)
            ex_over, ey_over = block_electric(theirs, mine[3:5], [v[b] for v in over], b)
            es = block_electric_s(mine, bunch[b], factors)
            state.append(((ex, ey, es, *mine[3:]), (ex_over, ey_over)))
        set_far([down[far_at], down[far_at + 1]], [fields[:2] for fields, _ in state])
        return state

    def far_second(state, moved_now):
        own = [kept_blocks(ref, far - moved_now) for ref in (cells.keep, cells.gain)]
        below = [kept_blocks(ext[a], far - 1) for a in (BX, BY)]
        found = []
        for b in range(2):
            fields = block_magnetic(*state[b], b)
            found.append(block_electric(fields, [v[b] for v in below], [v[b] for v in own], b))
        gained = cells.gain[far - moved_now, mine]
        ex = down[far_at + 2] + gained * (rows[3, mine] * ext[BY][far - 1, mine])
        ey = down[far_at + 3] - gained * (rows[2, mine] * ext[BX][far - 1, mine])
        set_far([ex, ey], found)

    mine = pl.ds(0, width)
    moved_now = 0
    for t in range(STEPS):
        moved_now = moved_now + moved[t]
        above = moves + 1 + t
        if moves == 1:
            count, lowest = min(t, 2), 2
            count_e, lowest_e = min(t + 1, 2), max(t + 1, 2)
        else:
            count, lowest, count_e, lowest_e = base, t, base, t + 1
        if moves == 1 and t == 0:
            below_state = below_first(moved_now)
        if count:
            cells.magnetic(lowest, count)
        cells.magnetic(top - t, above)
        if moves == 1 and t == 1:
            below_second(below_state)

        @pl.when(first)
        def _():
            cells.leave(base + moved_now - 1)

        if t == STEPS - 1:
            for a in (BX, BY, BS):
                send(a, 3, base + 2)
                send(a, top - 2, planes + 3)
        cells.electric(lowest_e, count_e, moved_now)
        if t < STEPS - 1:
            cells.electric(top - t, above, moved_now)
        else:
            for a in (EX, EY, ES):
                send(a, 3, base + 3)
            cut = above // 2
            for start, end in ((top - 2, top - 2 + cut), (top - 2 + cut, planes + 3)):
                cells.electric(start, end - start, moved_now)
                for a in (EX, EY, ES):
                    send(a, start, end)
        if t == 0:
            edge_state = far_first(moved_now)
        elif t == 1:
            far_second(edge_state, moved_now)
        if t < STEPS - 1:

            @pl.when(last)
            def _():
                for a in (EX, EY, ES):
                    ext[a][top + 1 + moved_now] = jnp.zeros((cells.tall, cells.depth), jnp.float32)

    for item in copies:
        item.wait()


def advance(case, n_sides, moved, shape, ready, ghosts):
    planes, width, depth = shape
    block = jax.ShapeDtypeStruct(shape, jnp.float32)
    n_in = 11 + len(ghosts)
    found = pl.pallas_call(
        functools.partial(steps_kernel, case, n_sides, planes, width),
        out_shape=[block] * 6 + [pltpu.VMEM(x.shape, x.dtype) for x in ready[:9]],
        in_specs=[SMEM] + [VMEM] * (n_in - 1),
        out_specs=[ANY] * 6 + [VMEM] * 9,
        input_output_aliases={1 + n: 6 + n for n in range(9)},
        scratch_shapes=[pltpu.SemaphoreType.DMA((21,))],
        compiler_params=pltpu.CompilerParams(vmem_limit_bytes=32 * 2**20),
        name="steps",
    )(moved, *ready, *ghosts)
    return tuple(found[:6])


def passed(block, to, sides=(0,)):
    size_z, size_x = lax.axis_size("gz"), lax.axis_size("gx")
    route = [
        (z * size_x + x, to(z) * size_x + x + dx)
        for z in range(size_z)
        for x in range(size_x)
        for dx in sides
        if 0 <= to(z) < size_z and 0 <= x + dx < size_x
    ]
    return lax.ppermute(block, ("gz", "gx"), route)


def on_device(*args):
    arrays, moved = args[:8], args[8]
    arrays = arrays[:6] + (arrays[7], arrays[6])
    sides = ("swap",) if lax.axis_size("gx") == 2 else ("right", "left")
    which, moved, sent = pack(arrays, moved)

    def run(c, own, sent, moved):
        case = CASES[c]
        down = passed(sent[c], lambda z: z - 1)
        across = edges(sides, own)
        ways = {"swap": (1, -1), "right": (1,), "left": (-1,)}
        beside = [passed(block, lambda z: z, ways[side]) for block, side in zip(across, sides)]
        up = passed(lift(case, own, across), lambda z: z + 1)
        on, off = relay(case, own[0].shape, beside)
        on, off = passed(on, lambda z: z ^ 1), passed(off, lambda z: z + 1 if z % 2 else z - 1)
        ready = prepare(case[0], moved, own, beside)
        return advance(case, len(sides), moved, own[0].shape, ready, [down, up, on, off])

    return lax.switch(
        which[0],
        [functools.partial(run, c) for c in range(len(CASES))],
        arrays,
        sent,
        moved,
    )


def solution(mesh):
    block = P("gz", "gx", None)
    return jax.shard_map(
        on_device,
        mesh=mesh,
        in_specs=(block,) * 8 + (P(),),
        out_specs=(block,) * 6,
        check_vma=False,
    )
```

```python
import functools

import jax
import jax.numpy as jnp
from jax import lax
from jax.experimental import pallas as pl
from jax.experimental.pallas import tpu as pltpu
from jax.sharding import PartitionSpec as P

STEPS = 3
TILE = 8
HALF = 4
GROUP = 4
TIME_STEP = 0.5
CURRENT_SCALE = 0.1
VMEM = pl.BlockSpec(memory_space=pltpu.VMEM)
SMEM = pl.BlockSpec(memory_space=pltpu.SMEM)
ANY = pl.BlockSpec(memory_space=pl.ANY)
EX, EY, ES, BX, BY, BS, CODES, BUNCH = range(8)
CASES = ((1, 1), (1, 0), (2, 1), (2, 0))


def down_counts(case):
    moves, now = case
    later = moves - now
    return (moves,) * 6 + (later + 1, later)


def up_counts(case):
    moves, now = case
    later = moves - now
    return (0,) * 6 + (2 - later, 1 if moves == 1 else 2 - later)


def up_traces(case):
    return 4 if case[0] == 1 else 2


def offsets(counts):
    starts = [0]
    for count in counts:
        starts.append(starts[-1] + count)
    return starts


def column_scales(place, total):
    place = place.astype(jnp.float32)
    whole = 1.0 + (place - total / 2) / (2 * total)
    half = 1.0 + (place + 0.5 - total / 2) / (2 * total)
    return whole, half


def turned(tiles):
    return pltpu.roll(tiles, HALF, tiles.ndim - 2)


def next_y(v):
    depth = v.shape[-1]
    lane = lax.broadcasted_iota(jnp.int32, v.shape[-2:], 1)
    return jnp.where(lane < depth - 1, pltpu.roll(v, depth - 1, v.ndim - 1), 0.0)


def last_y(v):
    lane = lax.broadcasted_iota(jnp.int32, v.shape[-2:], 1)
    return jnp.where(lane > 0, pltpu.roll(v, 1, v.ndim - 1), 0.0)


def next_x(v):
    return pltpu.roll(v, v.shape[-2] - 1, v.ndim - 2)


def last_x(v):
    return pltpu.roll(v, 1, v.ndim - 2)


def low_half(depth):
    return lax.broadcasted_iota(jnp.int32, (TILE, depth), 0) < HALF


class Plane:
    def __init__(self, start, width, depth, total, masked=False):
        column = start + lax.broadcasted_iota(jnp.int32, (width, depth), 0)
        self.inside = (column >= 0) & (column < total) if masked else None
        self.whole, self.half = column_scales(column, total)
        self.one_whole, self.one_half = 1.0 / self.whole, 1.0 / self.half
        self.step_whole, self.step_half = TIME_STEP * self.one_whole, TIME_STEP * self.one_half

    def kept(self, *values):
        if self.inside is None:
            return values
        return tuple(jnp.where(self.inside, v, 0.0) for v in values)

    def add_above(self, bx, by, ex, ey):
        return bx + self.step_whole * ey, by - self.step_half * ex

    def radial_vertical(self, bx, by, ex, ey, es):
        weighted = self.whole * es
        bx = bx - TIME_STEP * (next_y(es) - es) - self.step_whole * ey
        by = by + self.step_half * (ex + next_x(weighted) - weighted)
        return self.kept(bx, by)

    def longitudinal(self, bs, ex, ey):
        return self.kept(bs - TIME_STEP * ((next_x(ey) - ey) - (next_y(ex) - ex)))[0]

    def electric(self, ex, ey, bs, over_x, over_y, factors):
        kept, gained = factors
        weighted = self.half * bs
        ex = kept * ex + gained * ((bs - last_y(bs)) - self.one_half * over_y)
        ey = kept * ey + gained * (self.one_whole * (over_x - (weighted - last_x(weighted))))
        return self.kept(ex, ey)

    def electric_s(self, es, bx, by, bunch, factors):
        current = CURRENT_SCALE * bunch.astype(jnp.float32)
        es = factors[0] * es + factors[1] * ((by - last_x(by)) - (bx - last_y(bx)) - current)
        return self.kept(es)[0]


def far_traces(flat, case, second_move, field, code, bunch, codes_ready=lambda: None):
    far, first_move = case
    folded, now_b = {}, {}
    for plane in range(far - 1, far + 2):
        above = field(EX, plane + 1), field(EY, plane + 1)
        folded[plane] = flat.add_above(field(BX, plane), field(BY, plane), *above)
        fields = field(EX, plane), field(EY, plane), field(ES, plane)
        now_b[plane] = flat.radial_vertical(*folded[plane], *fields)
    codes_ready()
    now_e, now_s = {}, {}
    for plane in (far, far + 1):
        ex, ey = field(EX, plane), field(EY, plane)
        now_s[plane] = flat.longitudinal(field(BS, plane), ex, ey)
        factors = coefficients(code(plane - first_move))
        over = [up - under for up, under in zip(now_b[plane], now_b[plane - 1])]
        now_e[plane] = flat.electric(ex, ey, now_s[plane], *over, factors)
        if plane == far:
            es = flat.electric_s(field(ES, far), *now_b[far], bunch(far - first_move), factors)
    bx, by = flat.add_above(*now_b[far], *now_e[far + 1])
    bx, by = flat.radial_vertical(bx, by, *now_e[far], es)
    bs = flat.longitudinal(now_s[far], *now_e[far])
    factors = coefficients(code(far - first_move - second_move))
    return folded[far - 1], (*now_e[far], *flat.electric(*now_e[far], bs, bx, by, factors))


def near_traces(flat, case, planes, field, code, bunch):
    top = planes - 1
    ex, ey, es, bx, by, bs = (field(a, top) for a in range(6))
    first = flat.radial_vertical(bx, by, ex, ey, es)
    if case[0] == 2:
        return first
    under = flat.add_above(field(BX, top - 1), field(BY, top - 1), ex, ey)
    under = flat.radial_vertical(*under, *(field(a, top - 1) for a in (EX, EY, ES)))
    bs = flat.longitudinal(bs, ex, ey)
    factors = coefficients(code(top - case[1]))
    ex, ey = flat.electric(ex, ey, bs, first[0] - under[0], first[1] - under[1], factors)
    es = flat.electric_s(es, *first, bunch(top - case[1]), factors)
    return (*first, *flat.radial_vertical(*first, ex, ey, es))


def pack_kernel(*refs):
    sources, moved = refs[:8], refs[8]
    which, moved_here = refs[9:11]
    sent = refs[11 : 11 + len(CASES)]
    near, near_int, sems, moved_sem = refs[11 + len(CASES) :]
    _, _, width, depth = near.shape
    most = max(case[0] for case in CASES)
    fetched = (most + 3,) * 2 + (most + 2,) * 5 + (most + 1,)
    gx = lax.axis_index("gx")
    total = width * lax.axis_size("gx")

    get_moved = pltpu.make_async_copy(moved, moved_here, moved_sem)
    get_moved.start()
    copies = []
    for a in range(8):
        span = pl.ds(0, fetched[a])
        goal = near.at[a, span] if a < 6 else near_int.at[a - 6, span]
        copies.append(pltpu.make_async_copy(sources[a].at[span], goal, sems.at[a]))
        copies[-1].start()
    get_moved.wait()
    now = moved_here[0]
    later = moved_here[1] + moved_here[2]
    case_index = jnp.where(now + later == 1, 1 - now, 3 - now)
    which[0] = case_index

    flat = Plane(gx * width, width, depth, total)
    for item in copies[:6]:
        item.wait()

    for c, case in enumerate(CASES):
        down = sent[c]
        downs = down_counts(case)
        at = offsets(downs[:6])
        far = case[0]

        @pl.when(case_index == c)
        def _():
            field = lambda a, plane: near[a, plane]
            for a in range(6):
                down[pl.ds(at[a], far)] = near[a, :far]

            folded, traces = far_traces(
                flat,
                case,
                moved_here[1],
                field,
                lambda plane: near_int[0, plane],
                lambda plane: near_int[1, plane],
                lambda: [item.wait() for item in copies[6:]],
            )
            down[at[BX] + far - 1], down[at[BY] + far - 1] = folded
            place = at[-1]
            for v in traces:
                down[place] = v
                place += 1
            for n, a in enumerate((CODES, BUNCH)):
                if downs[a]:
                    down[pl.ds(place, downs[a])] = near_int[n, : downs[a]].astype(jnp.float32)
                place += downs[a]


def pack(arrays, moved):
    planes, width, depth = arrays[0].shape
    near = max(case[0] for case in CASES) + 3
    shapes = [pltpu.SMEM((1,), jnp.int32), pltpu.SMEM((STEPS,), jnp.int32)]
    for case in CASES:
        count = sum(down_counts(case)) + 4
        shapes.append(pltpu.VMEM((count, width, depth), jnp.float32))
    found = pl.pallas_call(
        pack_kernel,
        out_shape=shapes,
        in_specs=[ANY] * 9,
        out_specs=[SMEM] * 2 + [VMEM] * len(CASES),
        scratch_shapes=[
            pltpu.VMEM((6, near, width, depth), jnp.float32),
            pltpu.VMEM((2, near, width, depth), jnp.int32),
            pltpu.SemaphoreType.DMA((8,)),
            pltpu.SemaphoreType.DMA,
        ],
        compiler_params=pltpu.CompilerParams(vmem_limit_bytes=32 * 2**20),
        name="pack",
    )(*(pltpu.with_memory_space_constraint(a, pltpu.HBM) for a in (*arrays, moved)))
    return found[0], found[1], found[2:]


def edges_kernel(sides, *refs):
    own, across = refs[:8], refs[8:]
    planes, width, depth = own[0].shape
    gx = lax.axis_index("gx")
    low = low_half(depth)
    for n, side in enumerate(sides):
        if side == "swap":
            at, high = pl.multiple_of(jnp.where(gx == 0, width - TILE, 0), TILE), gx == 0
        else:
            at, high = (width - TILE, True) if side == "right" else (0, False)
        for a in range(4):
            first = own[a][:, pl.ds(at, TILE)]
            second = own[a + 4][:, pl.ds(at, TILE)].astype(jnp.float32)
            if side == "swap":
                first = jnp.where(high, turned(first), first)
                second = jnp.where(high, second, turned(second))
            elif high:
                first = turned(first)
            else:
                second = turned(second)
            across[n][pl.ds(a * planes, planes)] = jnp.where(low, first, second)


def edges(sides, own):
    planes, width, depth = own[0].shape
    return pl.pallas_call(
        functools.partial(edges_kernel, sides),
        out_shape=[pltpu.VMEM((4 * planes, TILE, depth), jnp.float32)] * len(sides),
        in_specs=[VMEM] * 8,
        out_specs=[VMEM] * len(sides),
        compiler_params=pltpu.CompilerParams(vmem_limit_bytes=32 * 2**20),
        name="edges",
    )(*own)


def lift_kernel(case, *refs):
    own, up = refs[:8], refs[-1]
    planes, width, depth = own[0].shape
    ups = up_counts(case)
    at = [up_traces(case) + n for n in offsets(ups)]
    flat = Plane(lax.axis_index("gx") * width, width, depth, width * lax.axis_size("gx"))
    for a in (CODES, BUNCH):
        if ups[a]:
            up[pl.ds(at[a], ups[a])] = own[a][planes - ups[a] :].astype(jnp.float32)
    values = near_traces(
        flat,
        case,
        planes,
        lambda a, plane: own[a][plane],
        lambda plane: own[CODES][plane],
        lambda plane: own[BUNCH][plane],
    )
    for n, v in enumerate(values):
        up[n] = v


def lift(case, own, after):
    planes, width, depth = own[0].shape
    count = sum(up_counts(case)) + up_traces(case)
    return pl.pallas_call(
        functools.partial(lift_kernel, case),
        out_shape=pltpu.VMEM((count, width, depth), jnp.float32),
        in_specs=[VMEM] * 8 + [ANY] * len(after),
        out_specs=VMEM,
        compiler_params=pltpu.CompilerParams(vmem_limit_bytes=32 * 2**20),
        cost_estimate=pl.CostEstimate(flops=10**7, bytes_accessed=10**7, transcendentals=0),
        name="lift",
    )(*own, *after)


def edge_blocks(right_tile, ghost_tile, left_tile):
    right_tile, ghost_tile, left_tile = turned(right_tile), turned(ghost_tile), turned(left_tile)
    low = low_half(right_tile.shape[-1])
    return jnp.where(low, right_tile, ghost_tile), jnp.where(low, ghost_tile, left_tile)


def corner_starts(case):
    moves = case[0]
    return offsets((moves, moves, moves + 1, moves))


def relay_kernel(case, n_sides, moved, *refs):
    own, beside, (on, off) = refs[:8], refs[8 : 8 + n_sides], refs[8 + n_sides :]
    planes, width, depth = own[0].shape
    moves = case[0]
    gx = lax.axis_index("gx")
    even = lax.axis_index("gz") % 2 == 0
    start = gx * width
    total = width * lax.axis_size("gx")
    low = low_half(depth)
    row = lax.broadcasted_iota(jnp.int32, (TILE, depth), 0)
    ghost_in = ghost_inside(width, depth)[0]

    def block_traces(b):
        flat = Plane(start - HALF if b else start + width - HALF, TILE, depth, total, True)

        def value(a, plane):
            ghost_tile = spread_tiles([side[a % 4 * planes + plane] for side in beside], a >= 4)
            ghost_tile = jnp.where(ghost_in, ghost_tile, 0.0)
            first = own[a][plane, pl.ds(0, TILE)].astype(jnp.float32)
            last = own[a][plane, pl.ds(width - TILE, TILE)].astype(jnp.float32)
            return edge_blocks(last, ghost_tile, first)[b]

        code, bunch = functools.partial(value, CODES), functools.partial(value, BUNCH)
        above = far_traces(flat, case, moved[1], value, code, bunch)[1]
        return above, near_traces(flat, case, planes, value, code, bunch)

    blocks = [block_traces(b) for b in range(2)]
    before = [v for pair in zip(blocks[0][0], blocks[1][0]) for v in pair]
    after = [v for pair in zip(blocks[0][1], blocks[1][1]) for v in pair]

    def fill(to_before, to_after):
        for n, v in enumerate(before):
            to_before[n] = v
        for n, v in enumerate(after):
            to_after[n] = v
        starts = corner_starts(case)
        for n in range(n_sides):
            if n_sides == 1:
                left_column = jnp.where(gx == 0, start + width, start - HALF)
            else:
                left_column = start - HALF if n == 0 else start + width
            whole, half = column_scales(left_column + jnp.where(row < HALF, row, row - HALF), total)
            at = len(before) + n * starts[-1]
            for a in range(4):
                count = starts[a + 1] - starts[a]
                to_before[pl.ds(at + starts[a], count)] = beside[n][pl.ds(a * planes, count)]
            plane = moves - 1
            tile = lambda a, plane: beside[n][a * planes + plane]
            to_before[at + starts[BX] + plane] = tile(BX, plane) + jnp.where(
                low, (TIME_STEP / whole) * tile(EY, moves), 0.0
            )
            to_before[at + plane] = tile(BY - 4, plane) - jnp.where(
                low, 0.0, turned((TIME_STEP / half) * tile(EX, moves))
            )
            base = 3 - moves
            for a in (2, 3):
                to = len(after) + (2 * n + a - 2) * base
                to_after[pl.ds(to, base)] = beside[n][pl.ds((a + 1) * planes - base, base)]

    @pl.when(even)
    def _():
        fill(off, on)

    @pl.when(jnp.logical_not(even))
    def _():
        fill(on, off)


def relay(case, moved, own, beside):
    planes, width, depth = own[0].shape
    count = 8 + len(beside) * corner_starts(case)[-1]
    return pl.pallas_call(
        functools.partial(relay_kernel, case, len(beside)),
        out_shape=[pltpu.VMEM((n, TILE, depth), jnp.float32) for n in (count + 1, count)],
        in_specs=[SMEM] + [VMEM] * (8 + len(beside)),
        out_specs=[VMEM] * 2,
        compiler_params=pltpu.CompilerParams(vmem_limit_bytes=32 * 2**20),
        name="relay",
    )(moved, *own, *beside)


def coefficients(code):
    kind = code.dtype.type
    five, six, seven = code == kind(5), code == kind(6), code == kind(7)
    keep = jnp.where(five, 0.0, jnp.where(six, 0.8 / 1.2, jnp.where(seven, 0.4 / 1.6, 1.0)))
    gain = jnp.where(
        five,
        0.0,
        jnp.where(six, TIME_STEP / 1.2, jnp.where(seven, TIME_STEP / 1.6, TIME_STEP)),
    )
    return keep, gain


def ghost_inside(width, depth):
    gx = lax.axis_index("gx")
    row = lax.broadcasted_iota(jnp.int32, (1, TILE, depth), 1)
    right = gx < lax.axis_size("gx") - 1
    return jnp.where(row < HALF, right.astype(jnp.int32), (gx > 0).astype(jnp.int32)) == 1


def spread_tiles(beside, upper):
    gx = lax.axis_index("gx")
    if len(beside) == 1:
        same = (gx > 0) if upper else (gx == 0)
        return jnp.where(same, beside[0], turned(beside[0]))
    from_left, from_right = beside
    if upper:
        from_right = turned(from_right)
    else:
        from_left = turned(from_left)
    return jnp.where(low_half(from_left.shape[-1]), from_right, from_left)


class Cells:
    def __init__(self, refs, width):
        self.ext, (self.keep, self.gain, self.current, self.rows) = refs[:6], refs[6:]
        self.width = width
        self.tall, self.depth = self.keep.shape[1:]
        self.ghost_in = ghost_inside(width, self.depth)

    def put(self, a, at, count, value, ghost):
        here = pl.ds(at, count)
        where = pl.ds(self.width, TILE) if ghost else pl.ds(0, self.width)
        mask = (lambda v: jnp.where(self.ghost_in, v, 0.0)) if ghost else (lambda v: v)
        if a < 6:
            self.ext[a][here, where] = mask(value)
        elif a == CODES:
            kept, gained = coefficients(value)
            self.keep[here, where], self.gain[here, where] = mask(kept), mask(gained)
        else:
            self.current[here, where] = CURRENT_SCALE * mask(value.astype(jnp.float32))

    def magnetic(self, e, count):
        ext, rows = self.ext, self.rows
        here, above = pl.ds(e, count), pl.ds(e + 1, count)
        ex, ey, es = ext[EX][here], ext[EY][here], ext[ES][here]
        bx = ext[BX][here] - (rows[4] * (next_y(es) - es) - rows[5] * (ext[EY][above] - ey))
        by = ext[BY][here] - rows[6] * ((ext[EX][above] - ex) - (next_x(rows[0] * es) - rows[0] * es))
        bs = ext[BS][here] - rows[4] * ((next_x(ey) - ey) - (next_y(ex) - ex))
        ext[BX][here], ext[BY][here], ext[BS][here] = bx, by, bs

    def electric(self, e, count, moved_now):
        ext, rows = self.ext, self.rows
        here, below, cells = pl.ds(e, count), pl.ds(e - 1, count), pl.ds(e - moved_now, count)
        bx, by, bs = ext[BX][here], ext[BY][here], ext[BS][here]
        kept, gained = self.keep[cells], self.gain[cells]
        ex = kept * ext[EX][here] + gained * ((bs - last_y(bs)) - rows[3] * (by - ext[BY][below]))
        ey = kept * ext[EY][here] + gained * (
            rows[2] * ((bx - ext[BX][below]) - (rows[1] * bs - last_x(rows[1] * bs)))
        )
        es = kept * ext[ES][here] + gained * (
            (by - last_x(by)) - (bx - last_y(bx)) - self.current[cells]
        )
        ext[EX][here], ext[EY][here], ext[ES][here] = ex, ey, es

    def leave(self, plane):
        for a in (BX, BY):
            self.ext[a][plane] = jnp.zeros((self.tall, self.depth), jnp.float32)


def in_groups(start, count, body):
    whole = max(count, 0) // GROUP
    if whole:

        @pl.loop(0, whole)
        def _(i):
            body(start + i * GROUP, GROUP)

    if count > 0 and count % GROUP:
        body(start + whole * GROUP, count % GROUP)


def prepare_kernel(moves, n_sides, moved, *refs):
    own, beside = refs[:8], refs[8 : 8 + n_sides]
    planes, width, depth = own[0].shape
    cells = Cells(refs[8 + n_sides :], width)
    tall, rows = cells.tall, cells.rows
    base = 3 - moves
    top = base + planes - 1
    total = width * lax.axis_size("gx")

    row = lax.broadcasted_iota(jnp.int32, (tall, depth), 0)
    place = lax.axis_index("gx") * width + jnp.where(row < width + HALF, row, row - tall)
    inside = (place >= 0) & (place < total)
    whole, half = column_scales(place, total)
    step = jnp.where(inside, TIME_STEP, 0.0)
    for n, value in enumerate((whole, half, 1.0 / whole, 1.0 / half, step, step / whole, step / half)):
        rows[n] = value
    for a in range(8):
        cells.put(a, base, planes, own[a][...], False)
        tiles = [side[pl.ds(a % 4 * planes, planes)] for side in beside]
        cells.put(a, base, planes, spread_tiles(tiles, a >= 4), True)
    for a in (EX, EY):
        cells.ext[a][0] = jnp.zeros((tall, depth), jnp.float32)
        cells.ext[a][planes + 3] = jnp.zeros((tall, depth), jnp.float32)

    moved_now = 0
    for t in range(STEPS):
        moved_now = moved_now + moved[t]
        in_groups(base + t, planes - 1 - 2 * t, cells.magnetic)

        @pl.when((lax.axis_index("gz") == 0) & (moved_now == t + 1))
        def _():
            cells.leave(base + t)

        in_groups(base + t + 1, planes - 2 - 2 * t, lambda e, n: cells.electric(e, n, moved_now))


def prepare(moves, moved, own, beside):
    planes, width, depth = own[0].shape
    tall = width + TILE
    vmem = lambda *shape: pltpu.VMEM(shape, jnp.float32)
    shapes = [vmem(planes + 4, tall, depth)] * 9
    shapes += [vmem(7, tall, depth)]
    return pl.pallas_call(
        functools.partial(prepare_kernel, moves, len(beside)),
        out_shape=shapes,
        in_specs=[SMEM] + [VMEM] * (8 + len(beside)),
        out_specs=[VMEM] * len(shapes),
        compiler_params=pltpu.CompilerParams(vmem_limit_bytes=32 * 2**20),
        cost_estimate=pl.CostEstimate(flops=22 * 10**8, bytes_accessed=10**7, transcendentals=0),
        name="prepare",
    )(moved, *own, *beside)


def steps_kernel(case, n_sides, planes, width, moved, *refs):
    rows, down, up, on, off = refs[9:14]
    outs = refs[14:20]
    cells = Cells((*refs[20:29], rows), width)
    sems = refs[29]
    ext = cells.ext
    moves = case[0]
    base = 3 - moves
    top = base + planes - 1
    far = planes + 3
    first = lax.axis_index("gz") == 0
    last = lax.axis_index("gz") == lax.axis_size("gz") - 1
    even = lax.axis_index("gz") % 2 == 0
    downs, ups = down_counts(case), up_counts(case)
    at, up_at = offsets(downs[:6]), [up_traces(case) + n for n in offsets(ups)]
    far_at = at[-1]
    at = at[:6] + [far_at + 4, far_at + 4 + downs[CODES]]
    copies = []

    def send(a, start, end):
        if end > start:
            item = pltpu.make_async_copy(
                ext[a].at[pl.ds(start, end - start), pl.ds(0, width)],
                outs[a].at[pl.ds(start - 3, end - start)],
                sems.at[len(copies)],
            )
            item.start()
            copies.append(item)

    for a in range(6):
        send(a, base + (2 if a >= BX else 3), top - 2)

    starts = corner_starts(case)

    def came(span, above):
        if above:
            return jnp.where(even, on[span], off[span])
        return jnp.where(even, off[span], on[span])

    def corner_above(a, count):
        at = [8 + n * starts[-1] + starts[a % 4] for n in range(n_sides)]
        return spread_tiles([came(pl.ds(n, count), True) for n in at], a >= 4)

    def corner_below(a, count):
        at = [2 * up_traces(case) + (2 * n + a % 4 - 1) * base - count for n in range(n_sides)]
        return spread_tiles([came(pl.ds(n, count), False) for n in at], a >= 4)

    for a in range(8):
        if downs[a]:
            cells.put(a, top + 1, downs[a], down[pl.ds(at[a], downs[a])], False)
            cells.put(a, top + 1, downs[a], corner_above(a, downs[a]), True)
        if ups[a]:
            cells.put(a, base - ups[a], ups[a], up[pl.ds(up_at[a], ups[a])], False)
            cells.put(a, base - ups[a], ups[a], corner_below(a, ups[a]), True)

    low = low_half(cells.depth)
    tile_row = lax.broadcasted_iota(jnp.int32, (TILE, cells.depth), 0)

    def trace(value, n, above):
        right_block, left_block = came(2 * n, above), came(2 * n + 1, above)
        at_right = jnp.where(tile_row >= TILE - 2, turned(right_block), value[width - TILE :])
        at_left = jnp.where(tile_row < 2, turned(left_block), value[:TILE])
        beyond = turned(jnp.where(low, left_block, right_block))
        return jnp.concatenate([at_left, value[TILE : width - TILE], at_right, beyond], 0)

    def far_first():
        for a in (EX, EY):
            ext[a][far] = jnp.where(last, 0.0, trace(down[far_at + a], a, True))

    def far_second(moved_now):
        gained = cells.gain[far - moved_now]
        ex = trace(down[far_at + 2], 2, True) + gained * (rows[3] * ext[BY][far - 1])
        ey = trace(down[far_at + 3], 3, True) - gained * (rows[2] * ext[BX][far - 1])
        ext[EX][far], ext[EY][far] = jnp.where(last, 0.0, ex), jnp.where(last, 0.0, ey)

    def below_first(moved_now):
        bx, by = rows[5] * ext[EY][base], -rows[6] * ext[EX][base]
        ext[BX][base - 1] = trace(up[0], 0, False) + bx
        ext[BY][base - 1] = trace(up[1], 1, False) + by
        if moves == 2:
            return None
        gained = cells.gain[1 - moved_now]
        ex, ey = -gained * (rows[3] * by), gained * (rows[2] * bx)
        es = gained * ((by - last_x(by)) - (bx - last_y(bx)))
        weighted = rows[0] * es
        bx = bx - rows[4] * (next_y(es) - es) - rows[5] * ey
        by = by + rows[6] * (ex + next_x(weighted) - weighted)
        return trace(up[2], 2, False) + bx, trace(up[3], 3, False) + by

    def below_second(state):
        ext[BX][1] = state[0] + rows[5] * ext[EY][base]
        ext[BY][1] = state[1] - rows[6] * ext[EX][base]

    moved_now = 0
    for t in range(STEPS):
        moved_now = moved_now + moved[t]
        above = moves + 1 + t
        lowest, lowest_e = max(t, base), max(t + 1, base)
        if t == 0:
            below_state = below_first(moved_now)
        if base + t > lowest:
            cells.magnetic(lowest, base + t - lowest)
        cells.magnetic(top - t, above)
        if moves == 1 and t == 1:
            below_second(below_state)

        @pl.when(first)
        def _():
            cells.leave(base + moved_now - 1)

        if t == STEPS - 1:
            for a in (BX, BY, BS):
                send(a, 3, base + 2)
                send(a, top - 2, planes + 3)
        low_part = lowest_e, base + t + 1 - lowest_e
        if t < STEPS - 1:
            cells.electric(*low_part, moved_now)
            cells.electric(top - t, above, moved_now)
        else:
            cut = above // 2
            for start, count in ((top - 2, cut), (top - 2 + cut, above - cut), low_part):
                cells.electric(start, count, moved_now)
                for a in (EX, EY, ES):
                    send(a, start, start + count)
        if t == 0:
            far_first()
        elif t == 1:
            far_second(moved_now)
        if t < STEPS - 1:

            @pl.when(last)
            def _():
                for a in (EX, EY, ES):
                    ext[a][top + 1 + moved_now] = jnp.zeros((cells.tall, cells.depth), jnp.float32)

    for item in copies:
        item.wait()


def advance(case, n_sides, moved, shape, ready, ghosts):
    planes, width, depth = shape
    block = jax.ShapeDtypeStruct(shape, jnp.float32)
    n_in = 11 + len(ghosts)
    found = pl.pallas_call(
        functools.partial(steps_kernel, case, n_sides, planes, width),
        out_shape=[block] * 6 + [pltpu.VMEM(x.shape, x.dtype) for x in ready[:9]],
        in_specs=[SMEM] + [VMEM] * (n_in - 1),
        out_specs=[ANY] * 6 + [VMEM] * 9,
        input_output_aliases={1 + n: 6 + n for n in range(9)},
        scratch_shapes=[pltpu.SemaphoreType.DMA((21,))],
        compiler_params=pltpu.CompilerParams(vmem_limit_bytes=32 * 2**20),
        name="steps",
    )(moved, *ready, *ghosts)
    return tuple(found[:6])


def passed(block, to, sides=(0,)):
    size_z, size_x = lax.axis_size("gz"), lax.axis_size("gx")
    route = [
        (z * size_x + x, to(z) * size_x + x + dx)
        for z in range(size_z)
        for x in range(size_x)
        for dx in sides
        if 0 <= to(z) < size_z and 0 <= x + dx < size_x
    ]
    return lax.ppermute(block, ("gz", "gx"), route)


def on_device(*args):
    arrays, moved = args[:8], args[8]
    arrays = arrays[:6] + (arrays[7], arrays[6])
    sides = ("swap",) if lax.axis_size("gx") == 2 else ("right", "left")
    which, moved, sent = pack(arrays, moved)

    def run(c, own, sent, moved):
        case = CASES[c]
        down = passed(sent[c], lambda z: z - 1)
        across = edges(sides, own)
        ways = {"swap": (1, -1), "right": (1,), "left": (-1,)}
        beside = [passed(block, lambda z: z, ways[side]) for block, side in zip(across, sides)]
        up = passed(lift(case, own, across), lambda z: z + 1)
        on, off = relay(case, moved, own, beside)
        off = passed(off, lambda z: z + 1 if z % 2 else z - 1)
        on = passed(on, lambda z: z ^ 1)
        ready = prepare(case[0], moved, own, beside)
        return advance(case, len(sides), moved, own[0].shape, ready, [down, up, on, off])

    return lax.switch(
        which[0],
        [functools.partial(run, c) for c in range(len(CASES))],
        arrays,
        sent,
        moved,
    )


def solution(mesh):
    block = P("gz", "gx", None)
    return jax.shard_map(
        on_device,
        mesh=mesh,
        in_specs=(block,) * 8 + (P(),),
        out_specs=(block,) * 6,
        check_vma=False,
    )
```

```python
import functools

import jax
import jax.numpy as jnp
from jax import lax
from jax.experimental import pallas as pl
from jax.experimental.pallas import tpu as pltpu
from jax.sharding import PartitionSpec as P

STEPS = 3
TILE = 8
HALF = 4
GROUP = 4
TIME_STEP = 0.5
CURRENT_SCALE = 0.1
VMEM = pl.BlockSpec(memory_space=pltpu.VMEM)
SMEM = pl.BlockSpec(memory_space=pltpu.SMEM)
ANY = pl.BlockSpec(memory_space=pl.ANY)
EX, EY, ES, BX, BY, BS, CODES, BUNCH = range(8)
CASES = ((1, 1), (1, 0), (2, 1), (2, 0))


def down_counts(case):
    moves, now = case
    later = moves - now
    return (moves,) * 6 + (later + (moves == 1), later)


def up_counts(case):
    moves, now = case
    later = moves - now
    return (0,) * 6 + (2 - later, 1 if moves == 1 else 2 - later)


def up_traces(case):
    return 4 if case[0] == 1 else 2


def offsets(counts):
    starts = [0]
    for count in counts:
        starts.append(starts[-1] + count)
    return starts


def column_scales(place, total):
    place = place.astype(jnp.float32)
    whole = 1.0 + (place - total / 2) / (2 * total)
    half = 1.0 + (place + 0.5 - total / 2) / (2 * total)
    return whole, half


def turned(tiles):
    return pltpu.roll(tiles, HALF, tiles.ndim - 2)


def next_y(v):
    depth = v.shape[-1]
    lane = lax.broadcasted_iota(jnp.int32, v.shape[-2:], 1)
    return jnp.where(lane < depth - 1, pltpu.roll(v, depth - 1, v.ndim - 1), 0.0)


def last_y(v):
    lane = lax.broadcasted_iota(jnp.int32, v.shape[-2:], 1)
    return jnp.where(lane > 0, pltpu.roll(v, 1, v.ndim - 1), 0.0)


def next_x(v):
    return pltpu.roll(v, v.shape[-2] - 1, v.ndim - 2)


def last_x(v):
    return pltpu.roll(v, 1, v.ndim - 2)


def low_half(depth):
    return lax.broadcasted_iota(jnp.int32, (TILE, depth), 0) < HALF


class Plane:
    def __init__(self, start, width, depth, total, masked=False):
        column = start + lax.broadcasted_iota(jnp.int32, (width, depth), 0)
        self.inside = (column >= 0) & (column < total) if masked else None
        self.whole, self.half = column_scales(column, total)
        self.one_whole, self.one_half = 1.0 / self.whole, 1.0 / self.half
        self.step_whole, self.step_half = TIME_STEP * self.one_whole, TIME_STEP * self.one_half

    def kept(self, *values):
        if self.inside is None:
            return values
        return tuple(jnp.where(self.inside, v, 0.0) for v in values)

    def add_above(self, bx, by, ex, ey):
        return bx + self.step_whole * ey, by - self.step_half * ex

    def radial_vertical(self, bx, by, ex, ey, es):
        weighted = self.whole * es
        bx = bx - TIME_STEP * (next_y(es) - es) - self.step_whole * ey
        by = by + self.step_half * (ex + next_x(weighted) - weighted)
        return self.kept(bx, by)

    def longitudinal(self, bs, ex, ey):
        return self.kept(bs - TIME_STEP * ((next_x(ey) - ey) - (next_y(ex) - ex)))[0]

    def electric(self, ex, ey, bs, over_x, over_y, factors):
        kept, gained = factors
        weighted = self.half * bs
        ex = kept * ex + gained * ((bs - last_y(bs)) - self.one_half * over_y)
        ey = kept * ey + gained * (self.one_whole * (over_x - (weighted - last_x(weighted))))
        return self.kept(ex, ey)

    def electric_s(self, es, bx, by, bunch, factors):
        current = CURRENT_SCALE * bunch.astype(jnp.float32)
        es = factors[0] * es + factors[1] * ((by - last_x(by)) - (bx - last_y(bx)) - current)
        return self.kept(es)[0]


def far_traces(flat, case, second_move, field, code, bunch, codes_ready=lambda: None):
    far, first_move = case
    lowest = far - 1 if far == 1 else far - 2
    folded, now_b = {}, {}
    for plane in range(lowest, far + 2):
        above = field(EX, plane + 1), field(EY, plane + 1)
        folded[plane] = flat.add_above(field(BX, plane), field(BY, plane), *above)
        fields = field(EX, plane), field(EY, plane), field(ES, plane)
        now_b[plane] = flat.radial_vertical(*folded[plane], *fields)
    codes_ready()
    now_e, now_es, now_bs = {}, {}, {}
    for plane in range(lowest + 1, far + 2):
        ex, ey = field(EX, plane), field(EY, plane)
        now_bs[plane] = flat.longitudinal(field(BS, plane), ex, ey)
        factors = coefficients(code(plane - first_move))
        over = [up - under for up, under in zip(now_b[plane], now_b[plane - 1])]
        now_e[plane] = flat.electric(ex, ey, now_bs[plane], *over, factors)
        if plane <= far:
            now_es[plane] = flat.electric_s(
                field(ES, plane), *now_b[plane], bunch(plane - first_move), factors
            )

    def second(plane):
        next_b = flat.add_above(*now_b[plane], *now_e[plane + 1])
        return flat.radial_vertical(*next_b, *now_e[plane], now_es[plane])

    over = second(far)
    if far == 2:
        over = [up - under for up, under in zip(over, second(far - 1))]
    bs = flat.longitudinal(now_bs[far], *now_e[far])
    factors = coefficients(code(far - first_move - second_move))
    return folded[far - 1], (*now_e[far], *flat.electric(*now_e[far], bs, *over, factors))


def near_traces(flat, case, planes, field, code, bunch):
    top = planes - 1
    ex, ey, es, bx, by, bs = (field(a, top) for a in range(6))
    first = flat.radial_vertical(bx, by, ex, ey, es)
    if case[0] == 2:
        return first
    under = flat.add_above(field(BX, top - 1), field(BY, top - 1), ex, ey)
    under = flat.radial_vertical(*under, *(field(a, top - 1) for a in (EX, EY, ES)))
    bs = flat.longitudinal(bs, ex, ey)
    factors = coefficients(code(top - case[1]))
    ex, ey = flat.electric(ex, ey, bs, first[0] - under[0], first[1] - under[1], factors)
    es = flat.electric_s(es, *first, bunch(top - case[1]), factors)
    return (*first, *flat.radial_vertical(*first, ex, ey, es))


def pack_kernel(*refs):
    sources, moved = refs[:8], refs[8]
    which, moved_here = refs[9:11]
    sent = refs[11 : 11 + len(CASES)]
    near, near_int, sems, moved_sem = refs[11 + len(CASES) :]
    _, _, width, depth = near.shape
    most = max(case[0] for case in CASES)
    fetched = (most + 3,) * 2 + (most + 2,) * 5 + (most + 1,)
    gx = lax.axis_index("gx")
    total = width * lax.axis_size("gx")

    get_moved = pltpu.make_async_copy(moved, moved_here, moved_sem)
    get_moved.start()
    copies = []
    for a in range(8):
        span = pl.ds(0, fetched[a])
        goal = near.at[a, span] if a < 6 else near_int.at[a - 6, span]
        copies.append(pltpu.make_async_copy(sources[a].at[span], goal, sems.at[a]))
        copies[-1].start()
    get_moved.wait()
    now = moved_here[0]
    later = moved_here[1] + moved_here[2]
    case_index = jnp.where(now + later == 1, 1 - now, 3 - now)
    which[0] = case_index

    flat = Plane(gx * width, width, depth, total)
    for item in copies[:6]:
        item.wait()

    for c, case in enumerate(CASES):
        down = sent[c]
        downs = down_counts(case)
        at = offsets(downs[:6])
        far = case[0]

        @pl.when(case_index == c)
        def _():
            field = lambda a, plane: near[a, plane]
            for a in range(6):
                down[pl.ds(at[a], far)] = near[a, :far]

            folded, traces = far_traces(
                flat,
                case,
                moved_here[1],
                field,
                lambda plane: near_int[0, plane],
                lambda plane: near_int[1, plane],
                lambda: [item.wait() for item in copies[6:]],
            )
            down[at[BX] + far - 1], down[at[BY] + far - 1] = folded
            place = at[-1]
            for v in traces:
                down[place] = v
                place += 1
            for n, a in enumerate((CODES, BUNCH)):
                if downs[a]:
                    down[pl.ds(place, downs[a])] = near_int[n, : downs[a]].astype(jnp.float32)
                place += downs[a]


def pack(arrays, moved):
    planes, width, depth = arrays[0].shape
    near = max(case[0] for case in CASES) + 3
    shapes = [pltpu.SMEM((1,), jnp.int32), pltpu.SMEM((STEPS,), jnp.int32)]
    for case in CASES:
        count = sum(down_counts(case)) + 4
        shapes.append(pltpu.VMEM((count, width, depth), jnp.float32))
    found = pl.pallas_call(
        pack_kernel,
        out_shape=shapes,
        in_specs=[ANY] * 9,
        out_specs=[SMEM] * 2 + [VMEM] * len(CASES),
        scratch_shapes=[
            pltpu.VMEM((6, near, width, depth), jnp.float32),
            pltpu.VMEM((2, near, width, depth), jnp.int32),
            pltpu.SemaphoreType.DMA((8,)),
            pltpu.SemaphoreType.DMA,
        ],
        compiler_params=pltpu.CompilerParams(vmem_limit_bytes=32 * 2**20),
        name="pack",
    )(*(pltpu.with_memory_space_constraint(a, pltpu.HBM) for a in (*arrays, moved)))
    return found[0], found[1], found[2:]


def edges_kernel(sides, *refs):
    own, across = refs[:8], refs[8:]
    planes, width, depth = own[0].shape
    gx = lax.axis_index("gx")
    low = low_half(depth)
    for n, side in enumerate(sides):
        if side == "swap":
            at, high = pl.multiple_of(jnp.where(gx == 0, width - TILE, 0), TILE), gx == 0
        else:
            at, high = (width - TILE, True) if side == "right" else (0, False)
        for a in range(4):
            first = own[a][:, pl.ds(at, TILE)]
            second = own[a + 4][:, pl.ds(at, TILE)].astype(jnp.float32)
            if side == "swap":
                first = jnp.where(high, turned(first), first)
                second = jnp.where(high, second, turned(second))
            elif high:
                first = turned(first)
            else:
                second = turned(second)
            across[n][pl.ds(a * planes, planes)] = jnp.where(low, first, second)


def edges(sides, own):
    planes, width, depth = own[0].shape
    return pl.pallas_call(
        functools.partial(edges_kernel, sides),
        out_shape=[pltpu.VMEM((4 * planes, TILE, depth), jnp.float32)] * len(sides),
        in_specs=[VMEM] * 8,
        out_specs=[VMEM] * len(sides),
        compiler_params=pltpu.CompilerParams(vmem_limit_bytes=32 * 2**20),
        name="edges",
    )(*own)


def lift_kernel(case, *refs):
    own, up = refs[:8], refs[-1]
    planes, width, depth = own[0].shape
    ups = up_counts(case)
    at = [up_traces(case) + n for n in offsets(ups)]
    flat = Plane(lax.axis_index("gx") * width, width, depth, width * lax.axis_size("gx"))
    for a in (CODES, BUNCH):
        if ups[a]:
            up[pl.ds(at[a], ups[a])] = own[a][planes - ups[a] :].astype(jnp.float32)
    values = near_traces(
        flat,
        case,
        planes,
        lambda a, plane: own[a][plane],
        lambda plane: own[CODES][plane],
        lambda plane: own[BUNCH][plane],
    )
    for n, v in enumerate(values):
        up[n] = v


def lift(case, own, after):
    planes, width, depth = own[0].shape
    count = sum(up_counts(case)) + up_traces(case)
    return pl.pallas_call(
        functools.partial(lift_kernel, case),
        out_shape=pltpu.VMEM((count, width, depth), jnp.float32),
        in_specs=[VMEM] * 8 + [ANY] * len(after),
        out_specs=VMEM,
        compiler_params=pltpu.CompilerParams(vmem_limit_bytes=32 * 2**20),
        cost_estimate=pl.CostEstimate(flops=10**7, bytes_accessed=10**7, transcendentals=0),
        name="lift",
    )(*own, *after)


def edge_blocks(right_tile, ghost_tile, left_tile):
    right_tile, ghost_tile, left_tile = turned(right_tile), turned(ghost_tile), turned(left_tile)
    low = low_half(right_tile.shape[-1])
    return jnp.where(low, right_tile, ghost_tile), jnp.where(low, ghost_tile, left_tile)


def corner_starts(case):
    moves = case[0]
    return offsets((moves, moves, moves + (moves == 1), moves))


def relay_kernel(case, n_sides, moved, *refs):
    own, beside, (on, off) = refs[:8], refs[8 : 8 + n_sides], refs[8 + n_sides :]
    planes, width, depth = own[0].shape
    moves = case[0]
    gx = lax.axis_index("gx")
    even = lax.axis_index("gz") % 2 == 0
    start = gx * width
    total = width * lax.axis_size("gx")
    low = low_half(depth)
    row = lax.broadcasted_iota(jnp.int32, (TILE, depth), 0)
    ghost_in = ghost_inside(width, depth)[0]

    def block_traces(b):
        flat = Plane(start - HALF if b else start + width - HALF, TILE, depth, total, True)

        def value(a, plane):
            ghost_tile = spread_tiles([side[a % 4 * planes + plane] for side in beside], a >= 4)
            ghost_tile = jnp.where(ghost_in, ghost_tile, 0.0)
            first = own[a][plane, pl.ds(0, TILE)].astype(jnp.float32)
            last = own[a][plane, pl.ds(width - TILE, TILE)].astype(jnp.float32)
            return edge_blocks(last, ghost_tile, first)[b]

        code, bunch = functools.partial(value, CODES), functools.partial(value, BUNCH)
        above = far_traces(flat, case, moved[1], value, code, bunch)[1]
        return above, near_traces(flat, case, planes, value, code, bunch)

    blocks = [block_traces(b) for b in range(2)]
    before = [v for pair in zip(blocks[0][0], blocks[1][0]) for v in pair]
    after = [v for pair in zip(blocks[0][1], blocks[1][1]) for v in pair]

    def fill(to_before, to_after):
        for n, v in enumerate(before):
            to_before[n] = v
        for n, v in enumerate(after):
            to_after[n] = v
        starts = corner_starts(case)
        for n in range(n_sides):
            if n_sides == 1:
                left_column = jnp.where(gx == 0, start + width, start - HALF)
            else:
                left_column = start - HALF if n == 0 else start + width
            whole, half = column_scales(left_column + jnp.where(row < HALF, row, row - HALF), total)
            at = len(before) + n * starts[-1]
            for a in range(4):
                count = starts[a + 1] - starts[a]
                to_before[pl.ds(at + starts[a], count)] = beside[n][pl.ds(a * planes, count)]
            plane = moves - 1
            tile = lambda a, plane: beside[n][a * planes + plane]
            to_before[at + starts[BX] + plane] = tile(BX, plane) + jnp.where(
                low, (TIME_STEP / whole) * tile(EY, moves), 0.0
            )
            to_before[at + plane] = tile(BY - 4, plane) - jnp.where(
                low, 0.0, turned((TIME_STEP / half) * tile(EX, moves))
            )
            base = 3 - moves
            for a in (2, 3):
                to = len(after) + (2 * n + a - 2) * base
                to_after[pl.ds(to, base)] = beside[n][pl.ds((a + 1) * planes - base, base)]

    @pl.when(even)
    def _():
        fill(off, on)

    @pl.when(jnp.logical_not(even))
    def _():
        fill(on, off)


def relay(case, moved, own, beside):
    planes, width, depth = own[0].shape
    count = 8 + len(beside) * corner_starts(case)[-1]
    return pl.pallas_call(
        functools.partial(relay_kernel, case, len(beside)),
        out_shape=[pltpu.VMEM((n, TILE, depth), jnp.float32) for n in (count + 1, count)],
        in_specs=[SMEM] + [VMEM] * (8 + len(beside)),
        out_specs=[VMEM] * 2,
        compiler_params=pltpu.CompilerParams(vmem_limit_bytes=32 * 2**20),
        name="relay",
    )(moved, *own, *beside)


def coefficients(code):
    kind = code.dtype.type
    five, six, seven = code == kind(5), code == kind(6), code == kind(7)
    keep = jnp.where(five, 0.0, jnp.where(six, 0.8 / 1.2, jnp.where(seven, 0.4 / 1.6, 1.0)))
    gain = jnp.where(
        five,
        0.0,
        jnp.where(six, TIME_STEP / 1.2, jnp.where(seven, TIME_STEP / 1.6, TIME_STEP)),
    )
    return keep, gain


def ghost_inside(width, depth):
    gx = lax.axis_index("gx")
    row = lax.broadcasted_iota(jnp.int32, (1, TILE, depth), 1)
    right = gx < lax.axis_size("gx") - 1
    return jnp.where(row < HALF, right.astype(jnp.int32), (gx > 0).astype(jnp.int32)) == 1


def spread_tiles(beside, upper):
    gx = lax.axis_index("gx")
    if len(beside) == 1:
        same = (gx > 0) if upper else (gx == 0)
        return jnp.where(same, beside[0], turned(beside[0]))
    from_left, from_right = beside
    if upper:
        from_right = turned(from_right)
    else:
        from_left = turned(from_left)
    return jnp.where(low_half(from_left.shape[-1]), from_right, from_left)


class Cells:
    def __init__(self, refs, width):
        self.ext, (self.keep, self.gain, self.current, self.rows) = refs[:6], refs[6:]
        self.width = width
        self.tall, self.depth = self.keep.shape[1:]
        self.ghost_in = ghost_inside(width, self.depth)

    def put(self, a, at, count, value, ghost):
        here = pl.ds(at, count)
        where = pl.ds(self.width, TILE) if ghost else pl.ds(0, self.width)
        mask = (lambda v: jnp.where(self.ghost_in, v, 0.0)) if ghost else (lambda v: v)
        if a < 6:
            self.ext[a][here, where] = mask(value)
        elif a == CODES:
            kept, gained = coefficients(value)
            self.keep[here, where], self.gain[here, where] = mask(kept), mask(gained)
        else:
            self.current[here, where] = CURRENT_SCALE * mask(value.astype(jnp.float32))

    def magnetic(self, e, count):
        ext, rows = self.ext, self.rows
        here, above = pl.ds(e, count), pl.ds(e + 1, count)
        ex, ey, es = ext[EX][here], ext[EY][here], ext[ES][here]
        bx = ext[BX][here] - (rows[4] * (next_y(es) - es) - rows[5] * (ext[EY][above] - ey))
        by = ext[BY][here] - rows[6] * ((ext[EX][above] - ex) - (next_x(rows[0] * es) - rows[0] * es))
        bs = ext[BS][here] - rows[4] * ((next_x(ey) - ey) - (next_y(ex) - ex))
        ext[BX][here], ext[BY][here], ext[BS][here] = bx, by, bs

    def electric(self, e, count, moved_now):
        ext, rows = self.ext, self.rows
        here, below, cells = pl.ds(e, count), pl.ds(e - 1, count), pl.ds(e - moved_now, count)
        bx, by, bs = ext[BX][here], ext[BY][here], ext[BS][here]
        kept, gained = self.keep[cells], self.gain[cells]
        ex = kept * ext[EX][here] + gained * ((bs - last_y(bs)) - rows[3] * (by - ext[BY][below]))
        ey = kept * ext[EY][here] + gained * (
            rows[2] * ((bx - ext[BX][below]) - (rows[1] * bs - last_x(rows[1] * bs)))
        )
        es = kept * ext[ES][here] + gained * (
            (by - last_x(by)) - (bx - last_y(bx)) - self.current[cells]
        )
        ext[EX][here], ext[EY][here], ext[ES][here] = ex, ey, es

    def leave(self, plane):
        for a in (BX, BY):
            self.ext[a][plane] = jnp.zeros((self.tall, self.depth), jnp.float32)


def in_groups(start, count, body):
    whole = max(count, 0) // GROUP
    if whole:

        @pl.loop(0, whole)
        def _(i):
            body(start + i * GROUP, GROUP)

    if count > 0 and count % GROUP:
        body(start + whole * GROUP, count % GROUP)


def prepare_kernel(moves, n_sides, moved, *refs):
    own, beside = refs[:8], refs[8 : 8 + n_sides]
    planes, width, depth = own[0].shape
    cells = Cells(refs[8 + n_sides :], width)
    tall, rows = cells.tall, cells.rows
    base = 3 - moves
    top = base + planes - 1
    total = width * lax.axis_size("gx")

    row = lax.broadcasted_iota(jnp.int32, (tall, depth), 0)
    place = lax.axis_index("gx") * width + jnp.where(row < width + HALF, row, row - tall)
    inside = (place >= 0) & (place < total)
    whole, half = column_scales(place, total)
    step = jnp.where(inside, TIME_STEP, 0.0)
    for n, value in enumerate((whole, half, 1.0 / whole, 1.0 / half, step, step / whole, step / half)):
        rows[n] = value
    for a in range(8):
        cells.put(a, base, planes, own[a][...], False)
        tiles = [side[pl.ds(a % 4 * planes, planes)] for side in beside]
        cells.put(a, base, planes, spread_tiles(tiles, a >= 4), True)
    for a in (EX, EY):
        cells.ext[a][0] = jnp.zeros((tall, depth), jnp.float32)
        cells.ext[a][planes + 3] = jnp.zeros((tall, depth), jnp.float32)

    moved_now = 0
    for t in range(STEPS):
        moved_now = moved_now + moved[t]
        in_groups(base + t, planes - 1 - 2 * t, cells.magnetic)

        @pl.when((lax.axis_index("gz") == 0) & (moved_now == t + 1))
        def _():
            cells.leave(base + t)

        in_groups(base + t + 1, planes - 2 - 2 * t, lambda e, n: cells.electric(e, n, moved_now))


def prepare(moves, moved, own, beside):
    planes, width, depth = own[0].shape
    tall = width + TILE
    vmem = lambda *shape: pltpu.VMEM(shape, jnp.float32)
    shapes = [vmem(planes + 4, tall, depth)] * 9
    shapes += [vmem(7, tall, depth)]
    return pl.pallas_call(
        functools.partial(prepare_kernel, moves, len(beside)),
        out_shape=shapes,
        in_specs=[SMEM] + [VMEM] * (8 + len(beside)),
        out_specs=[VMEM] * len(shapes),
        compiler_params=pltpu.CompilerParams(vmem_limit_bytes=32 * 2**20),
        cost_estimate=pl.CostEstimate(flops=22 * 10**8, bytes_accessed=10**7, transcendentals=0),
        name="prepare",
    )(moved, *own, *beside)


def steps_kernel(case, n_sides, planes, width, moved, *refs):
    rows, down, up, on, off = refs[9:14]
    outs = refs[14:20]
    cells = Cells((*refs[20:29], rows), width)
    sems = refs[29]
    ext = cells.ext
    moves = case[0]
    base = 3 - moves
    top = base + planes - 1
    far = planes + 3
    first = lax.axis_index("gz") == 0
    last = lax.axis_index("gz") == lax.axis_size("gz") - 1
    even = lax.axis_index("gz") % 2 == 0
    downs, ups = down_counts(case), up_counts(case)
    at, up_at = offsets(downs[:6]), [up_traces(case) + n for n in offsets(ups)]
    far_at = at[-1]
    at = at[:6] + [far_at + 4, far_at + 4 + downs[CODES]]
    copies = []

    def send(a, start, end):
        if end > start:
            item = pltpu.make_async_copy(
                ext[a].at[pl.ds(start, end - start), pl.ds(0, width)],
                outs[a].at[pl.ds(start - 3, end - start)],
                sems.at[len(copies)],
            )
            item.start()
            copies.append(item)

    for a in range(6):
        send(a, base + (2 if a >= BX else 3), top - 2)

    starts = corner_starts(case)

    def came(span, above):
        if above:
            return jnp.where(even, on[span], off[span])
        return jnp.where(even, off[span], on[span])

    def corner_above(a, count):
        at = [8 + n * starts[-1] + starts[a % 4] for n in range(n_sides)]
        return spread_tiles([came(pl.ds(n, count), True) for n in at], a >= 4)

    def corner_below(a, count):
        at = [2 * up_traces(case) + (2 * n + a % 4 - 1) * base - count for n in range(n_sides)]
        return spread_tiles([came(pl.ds(n, count), False) for n in at], a >= 4)

    for a in range(8):
        if downs[a]:
            cells.put(a, top + 1, downs[a], down[pl.ds(at[a], downs[a])], False)
            cells.put(a, top + 1, downs[a], corner_above(a, downs[a]), True)
        if ups[a]:
            cells.put(a, base - ups[a], ups[a], up[pl.ds(up_at[a], ups[a])], False)
            cells.put(a, base - ups[a], ups[a], corner_below(a, ups[a]), True)

    low = low_half(cells.depth)
    tile_row = lax.broadcasted_iota(jnp.int32, (TILE, cells.depth), 0)

    def trace(value, n, above):
        right_block, left_block = came(2 * n, above), came(2 * n + 1, above)
        at_right = jnp.where(tile_row >= TILE - 2, turned(right_block), value[width - TILE :])
        at_left = jnp.where(tile_row < 2, turned(left_block), value[:TILE])
        beyond = turned(jnp.where(low, left_block, right_block))
        return jnp.concatenate([at_left, value[TILE : width - TILE], at_right, beyond], 0)

    def far_first():
        for a in (EX, EY):
            ext[a][far] = jnp.where(last, 0.0, trace(down[far_at + a], a, True))

    def far_second(moved_now):
        ex, ey = trace(down[far_at + 2], 2, True), trace(down[far_at + 3], 3, True)
        if moves == 1:
            gained = cells.gain[far - moved_now]
            ex = ex + gained * (rows[3] * ext[BY][far - 1])
            ey = ey - gained * (rows[2] * ext[BX][far - 1])
        ext[EX][far], ext[EY][far] = jnp.where(last, 0.0, ex), jnp.where(last, 0.0, ey)

    def below_first(moved_now):
        bx, by = rows[5] * ext[EY][base], -rows[6] * ext[EX][base]
        ext[BX][base - 1] = trace(up[0], 0, False) + bx
        ext[BY][base - 1] = trace(up[1], 1, False) + by
        if moves == 2:
            return None
        gained = cells.gain[1 - moved_now]
        ex, ey = -gained * (rows[3] * by), gained * (rows[2] * bx)
        es = gained * ((by - last_x(by)) - (bx - last_y(bx)))
        weighted = rows[0] * es
        bx = bx - rows[4] * (next_y(es) - es) - rows[5] * ey
        by = by + rows[6] * (ex + next_x(weighted) - weighted)
        return trace(up[2], 2, False) + bx, trace(up[3], 3, False) + by

    def below_second(state):
        ext[BX][1] = state[0] + rows[5] * ext[EY][base]
        ext[BY][1] = state[1] - rows[6] * ext[EX][base]

    moved_now = 0
    for t in range(STEPS):
        moved_now = moved_now + moved[t]
        above = moves + 1 + t
        lowest, lowest_e = max(t, base), max(t + 1, base)
        if t == 0:
            below_state = below_first(moved_now)
        if base + t > lowest:
            cells.magnetic(lowest, base + t - lowest)
        cells.magnetic(top - t, above)
        if moves == 1 and t == 1:
            below_second(below_state)

        @pl.when(first)
        def _():
            cells.leave(base + moved_now - 1)

        if t == STEPS - 1:
            for a in (BX, BY, BS):
                send(a, 3, base + 2)
                send(a, top - 2, planes + 3)
        low_part = lowest_e, base + t + 1 - lowest_e
        if t < STEPS - 1:
            cells.electric(*low_part, moved_now)
            cells.electric(top - t, above, moved_now)
        else:
            cut = above // 2
            for start, count in ((top - 2, cut), (top - 2 + cut, above - cut), low_part):
                cells.electric(start, count, moved_now)
                for a in (EX, EY, ES):
                    send(a, start, start + count)
        if t == 0:
            far_first()
        elif t == 1:
            far_second(moved_now)
        if t < STEPS - 1:

            @pl.when(last)
            def _():
                for a in (EX, EY, ES):
                    ext[a][top + 1 + moved_now] = jnp.zeros((cells.tall, cells.depth), jnp.float32)

    for item in copies:
        item.wait()


def advance(case, n_sides, moved, shape, ready, ghosts):
    planes, width, depth = shape
    block = jax.ShapeDtypeStruct(shape, jnp.float32)
    n_in = 11 + len(ghosts)
    found = pl.pallas_call(
        functools.partial(steps_kernel, case, n_sides, planes, width),
        out_shape=[block] * 6 + [pltpu.VMEM(x.shape, x.dtype) for x in ready[:9]],
        in_specs=[SMEM] + [VMEM] * (n_in - 1),
        out_specs=[ANY] * 6 + [VMEM] * 9,
        input_output_aliases={1 + n: 6 + n for n in range(9)},
        scratch_shapes=[pltpu.SemaphoreType.DMA((21,))],
        compiler_params=pltpu.CompilerParams(vmem_limit_bytes=32 * 2**20),
        name="steps",
    )(moved, *ready, *ghosts)
    return tuple(found[:6])


def passed(block, to, sides=(0,)):
    size_z, size_x = lax.axis_size("gz"), lax.axis_size("gx")
    route = [
        (z * size_x + x, to(z) * size_x + x + dx)
        for z in range(size_z)
        for x in range(size_x)
        for dx in sides
        if 0 <= to(z) < size_z and 0 <= x + dx < size_x
    ]
    return lax.ppermute(block, ("gz", "gx"), route)


def on_device(*args):
    arrays, moved = args[:8], args[8]
    arrays = arrays[:6] + (arrays[7], arrays[6])
    sides = ("swap",) if lax.axis_size("gx") == 2 else ("right", "left")
    which, moved, sent = pack(arrays, moved)

    def run(c, own, sent, moved):
        case = CASES[c]
        down = passed(sent[c], lambda z: z - 1)
        across = edges(sides, own)
        ways = {"swap": (1, -1), "right": (1,), "left": (-1,)}
        beside = [passed(block, lambda z: z, ways[side]) for block, side in zip(across, sides)]
        up = passed(lift(case, own, across), lambda z: z + 1)
        on, off = relay(case, moved, own, beside)
        off = passed(off, lambda z: z + 1 if z % 2 else z - 1)
        on = passed(on, lambda z: z ^ 1)
        ready = prepare(case[0], moved, own, beside)
        return advance(case, len(sides), moved, own[0].shape, ready, [down, up, on, off])

    return lax.switch(
        which[0],
        [functools.partial(run, c) for c in range(len(CASES))],
        arrays,
        sent,
        moved,
    )


def solution(mesh):
    block = P("gz", "gx", None)
    return jax.shard_map(
        on_device,
        mesh=mesh,
        in_specs=(block,) * 8 + (P(),),
        out_specs=(block,) * 6,
        check_vma=False,
    )
```

```python
import functools

import jax
import jax.numpy as jnp
from jax import lax
from jax.experimental import pallas as pl
from jax.experimental.pallas import tpu as pltpu
from jax.sharding import PartitionSpec as P

STEPS = 3
TILE = 8
HALF = 4
GROUP = 4
TIME_STEP = 0.5
CURRENT_SCALE = 0.1
VMEM = pl.BlockSpec(memory_space=pltpu.VMEM)
SMEM = pl.BlockSpec(memory_space=pltpu.SMEM)
ANY = pl.BlockSpec(memory_space=pl.ANY)
EX, EY, ES, BX, BY, BS, CODES, BUNCH = range(8)
CASES = ((1, 1), (1, 0), (2, 1), (2, 0))


def down_counts(case):
    moves, now = case
    later = moves - now
    return (moves,) * 6 + (later + (moves == 1), later)


def up_counts(case):
    moves, now = case
    later = moves - now
    return (0,) * 6 + (2 - later, 1 if moves == 1 else 2 - later)


def up_traces(case):
    return 4 if case[0] == 1 else 2


def offsets(counts):
    starts = [0]
    for count in counts:
        starts.append(starts[-1] + count)
    return starts


def column_scales(place, total):
    place = place.astype(jnp.float32)
    whole = 1.0 + (place - total / 2) / (2 * total)
    half = 1.0 + (place + 0.5 - total / 2) / (2 * total)
    return whole, half


def turned(tiles):
    return pltpu.roll(tiles, HALF, tiles.ndim - 2)


def next_y(v):
    depth = v.shape[-1]
    lane = lax.broadcasted_iota(jnp.int32, v.shape[-2:], 1)
    return jnp.where(lane < depth - 1, pltpu.roll(v, depth - 1, v.ndim - 1), 0.0)


def last_y(v):
    lane = lax.broadcasted_iota(jnp.int32, v.shape[-2:], 1)
    return jnp.where(lane > 0, pltpu.roll(v, 1, v.ndim - 1), 0.0)


def next_x(v):
    return pltpu.roll(v, v.shape[-2] - 1, v.ndim - 2)


def last_x(v):
    return pltpu.roll(v, 1, v.ndim - 2)


def low_half(depth):
    return lax.broadcasted_iota(jnp.int32, (TILE, depth), 0) < HALF


class Plane:
    def __init__(self, start, width, depth, total, masked=False):
        column = start + lax.broadcasted_iota(jnp.int32, (width, depth), 0)
        self.inside = (column >= 0) & (column < total) if masked else None
        self.whole, self.half = column_scales(column, total)
        self.one_whole, self.one_half = 1.0 / self.whole, 1.0 / self.half
        self.step_whole, self.step_half = TIME_STEP * self.one_whole, TIME_STEP * self.one_half

    def kept(self, *values):
        if self.inside is None:
            return values
        return tuple(jnp.where(self.inside, v, 0.0) for v in values)

    def add_above(self, bx, by, ex, ey):
        return bx + self.step_whole * ey, by - self.step_half * ex

    def radial_vertical(self, bx, by, ex, ey, es):
        weighted = self.whole * es
        bx = bx - TIME_STEP * (next_y(es) - es) - self.step_whole * ey
        by = by + self.step_half * (ex + next_x(weighted) - weighted)
        return self.kept(bx, by)

    def longitudinal(self, bs, ex, ey):
        return self.kept(bs - TIME_STEP * ((next_x(ey) - ey) - (next_y(ex) - ex)))[0]

    def electric(self, ex, ey, bs, over_x, over_y, factors):
        kept, gained = factors
        weighted = self.half * bs
        ex = kept * ex + gained * ((bs - last_y(bs)) - self.one_half * over_y)
        ey = kept * ey + gained * (self.one_whole * (over_x - (weighted - last_x(weighted))))
        return self.kept(ex, ey)

    def electric_s(self, es, bx, by, bunch, factors):
        current = CURRENT_SCALE * bunch.astype(jnp.float32)
        es = factors[0] * es + factors[1] * ((by - last_x(by)) - (bx - last_y(bx)) - current)
        return self.kept(es)[0]


def far_traces(flat, case, second_move, field, code, bunch, ready=lambda arrays: None):
    far, first_move = case
    lowest = far - 1 if far == 1 else far - 2
    ready((EX, EY, ES))
    zeros, above_terms, own_terms, spin = (0.0, 0.0), {}, {}, {}
    for plane in range(lowest, far + 2):
        ex, ey = field(EX, plane), field(EY, plane)
        above_terms[plane] = flat.add_above(*zeros, field(EX, plane + 1), field(EY, plane + 1))
        own_terms[plane] = flat.radial_vertical(*above_terms[plane], ex, ey, field(ES, plane))
        if plane > lowest:
            spin[plane] = flat.longitudinal(0.0, ex, ey)
    ready((BX, BY, BS))
    now_b = {}
    for plane in range(lowest, far + 2):
        now_b[plane] = [field(a, plane) + v for a, v in zip((BX, BY), own_terms[plane])]
    folded = [field(a, far - 1) + v for a, v in zip((BX, BY), above_terms[far - 1])]
    ready((CODES, BUNCH))
    now_e, now_es, now_bs = {}, {}, {}
    for plane in range(lowest + 1, far + 2):
        ex, ey = field(EX, plane), field(EY, plane)
        now_bs[plane] = field(BS, plane) + spin[plane]
        factors = coefficients(code(plane - first_move))
        over = [up - under for up, under in zip(now_b[plane], now_b[plane - 1])]
        now_e[plane] = flat.electric(ex, ey, now_bs[plane], *over, factors)
        if plane <= far:
            now_es[plane] = flat.electric_s(
                field(ES, plane), *now_b[plane], bunch(plane - first_move), factors
            )

    def second(plane):
        next_b = flat.add_above(*now_b[plane], *now_e[plane + 1])
        return flat.radial_vertical(*next_b, *now_e[plane], now_es[plane])

    over = second(far)
    if far == 2:
        over = [up - under for up, under in zip(over, second(far - 1))]
    bs = flat.longitudinal(now_bs[far], *now_e[far])
    factors = coefficients(code(far - first_move - second_move))
    return folded, (*now_e[far], *flat.electric(*now_e[far], bs, *over, factors))


def near_traces(flat, case, planes, field, code, bunch):
    top = planes - 1
    ex, ey, es, bx, by, bs = (field(a, top) for a in range(6))
    first = flat.radial_vertical(bx, by, ex, ey, es)
    if case[0] == 2:
        return first
    under = flat.add_above(field(BX, top - 1), field(BY, top - 1), ex, ey)
    under = flat.radial_vertical(*under, *(field(a, top - 1) for a in (EX, EY, ES)))
    bs = flat.longitudinal(bs, ex, ey)
    factors = coefficients(code(top - case[1]))
    ex, ey = flat.electric(ex, ey, bs, first[0] - under[0], first[1] - under[1], factors)
    es = flat.electric_s(es, *first, bunch(top - case[1]), factors)
    return (*first, *flat.radial_vertical(*first, ex, ey, es))


def pack_kernel(*refs):
    sources, moved = refs[:8], refs[8]
    which, moved_here = refs[9:11]
    sent = refs[11 : 11 + len(CASES)]
    near, near_int, sems, moved_sem = refs[11 + len(CASES) :]
    _, _, width, depth = near.shape
    most = max(case[0] for case in CASES)
    fetched = (most + 3,) * 2 + (most + 2,) * 5 + (most + 1,)
    gx = lax.axis_index("gx")
    total = width * lax.axis_size("gx")

    get_moved = pltpu.make_async_copy(moved, moved_here, moved_sem)
    get_moved.start()
    copies = []
    for a in range(8):
        span = pl.ds(0, fetched[a])
        goal = near.at[a, span] if a < 6 else near_int.at[a - 6, span]
        copies.append(pltpu.make_async_copy(sources[a].at[span], goal, sems.at[a]))
        copies[-1].start()
    get_moved.wait()
    now = moved_here[0]
    later = moved_here[1] + moved_here[2]
    case_index = jnp.where(now + later == 1, 1 - now, 3 - now)
    which[0] = case_index

    flat = Plane(gx * width, width, depth, total)
    for c, case in enumerate(CASES):
        down = sent[c]
        downs = down_counts(case)
        at = offsets(downs[:6])
        far = case[0]

        @pl.when(case_index == c)
        def _():
            field = lambda a, plane: near[a, plane]

            folded, traces = far_traces(
                flat,
                case,
                moved_here[1],
                field,
                lambda plane: near_int[0, plane],
                lambda plane: near_int[1, plane],
                lambda arrays: [copies[a].wait() for a in arrays],
            )
            for a in range(6):
                down[pl.ds(at[a], far)] = near[a, :far]
            down[at[BX] + far - 1], down[at[BY] + far - 1] = folded
            place = at[-1]
            for v in traces:
                down[place] = v
                place += 1
            for n, a in enumerate((CODES, BUNCH)):
                if downs[a]:
                    down[pl.ds(place, downs[a])] = near_int[n, : downs[a]].astype(jnp.float32)
                place += downs[a]


def pack(arrays, moved):
    planes, width, depth = arrays[0].shape
    near = max(case[0] for case in CASES) + 3
    shapes = [pltpu.SMEM((1,), jnp.int32), pltpu.SMEM((STEPS,), jnp.int32)]
    for case in CASES:
        count = sum(down_counts(case)) + 4
        shapes.append(pltpu.VMEM((count, width, depth), jnp.float32))
    found = pl.pallas_call(
        pack_kernel,
        out_shape=shapes,
        in_specs=[ANY] * 9,
        out_specs=[SMEM] * 2 + [VMEM] * len(CASES),
        scratch_shapes=[
            pltpu.VMEM((6, near, width, depth), jnp.float32),
            pltpu.VMEM((2, near, width, depth), jnp.int32),
            pltpu.SemaphoreType.DMA((8,)),
            pltpu.SemaphoreType.DMA,
        ],
        compiler_params=pltpu.CompilerParams(vmem_limit_bytes=32 * 2**20),
        name="pack",
    )(*(pltpu.with_memory_space_constraint(a, pltpu.HBM) for a in (*arrays, moved)))
    return found[0], found[1], found[2:]


def edges_kernel(sides, *refs):
    own, across = refs[:8], refs[8:]
    planes, width, depth = own[0].shape
    gx = lax.axis_index("gx")
    low = low_half(depth)
    for n, side in enumerate(sides):
        if side == "swap":
            at, high = pl.multiple_of(jnp.where(gx == 0, width - TILE, 0), TILE), gx == 0
        else:
            at, high = (width - TILE, True) if side == "right" else (0, False)
        for a in range(4):
            first = own[a][:, pl.ds(at, TILE)]
            second = own[a + 4][:, pl.ds(at, TILE)].astype(jnp.float32)
            if side == "swap":
                first = jnp.where(high, turned(first), first)
                second = jnp.where(high, second, turned(second))
            elif high:
                first = turned(first)
            else:
                second = turned(second)
            across[n][pl.ds(a * planes, planes)] = jnp.where(low, first, second)


def edges(sides, own):
    planes, width, depth = own[0].shape
    return pl.pallas_call(
        functools.partial(edges_kernel, sides),
        out_shape=[pltpu.VMEM((4 * planes, TILE, depth), jnp.float32)] * len(sides),
        in_specs=[VMEM] * 8,
        out_specs=[VMEM] * len(sides),
        compiler_params=pltpu.CompilerParams(vmem_limit_bytes=32 * 2**20),
        name="edges",
    )(*own)


def lift_kernel(case, *refs):
    own, up = refs[:8], refs[-1]
    planes, width, depth = own[0].shape
    ups = up_counts(case)
    at = [up_traces(case) + n for n in offsets(ups)]
    flat = Plane(lax.axis_index("gx") * width, width, depth, width * lax.axis_size("gx"))
    for a in (CODES, BUNCH):
        if ups[a]:
            up[pl.ds(at[a], ups[a])] = own[a][planes - ups[a] :].astype(jnp.float32)
    values = near_traces(
        flat,
        case,
        planes,
        lambda a, plane: own[a][plane],
        lambda plane: own[CODES][plane],
        lambda plane: own[BUNCH][plane],
    )
    for n, v in enumerate(values):
        up[n] = v


def lift(case, own, after):
    planes, width, depth = own[0].shape
    count = sum(up_counts(case)) + up_traces(case)
    return pl.pallas_call(
        functools.partial(lift_kernel, case),
        out_shape=pltpu.VMEM((count, width, depth), jnp.float32),
        in_specs=[VMEM] * 8 + [ANY] * len(after),
        out_specs=VMEM,
        compiler_params=pltpu.CompilerParams(vmem_limit_bytes=32 * 2**20),
        cost_estimate=pl.CostEstimate(flops=10**7, bytes_accessed=10**7, transcendentals=0),
        name="lift",
    )(*own, *after)


def edge_blocks(right_tile, ghost_tile, left_tile):
    right_tile, ghost_tile, left_tile = turned(right_tile), turned(ghost_tile), turned(left_tile)
    low = low_half(right_tile.shape[-1])
    return jnp.where(low, right_tile, ghost_tile), jnp.where(low, ghost_tile, left_tile)


def corner_starts(case):
    moves = case[0]
    return offsets((moves, moves, moves + (moves == 1), moves))


def relay_kernel(case, n_sides, moved, *refs):
    own, beside, (on, off) = refs[:8], refs[8 : 8 + n_sides], refs[8 + n_sides :]
    planes, width, depth = own[0].shape
    moves = case[0]
    gx = lax.axis_index("gx")
    even = lax.axis_index("gz") % 2 == 0
    start = gx * width
    total = width * lax.axis_size("gx")
    low = low_half(depth)
    row = lax.broadcasted_iota(jnp.int32, (TILE, depth), 0)
    ghost_in = ghost_inside(width, depth)[0]

    def block_traces(b):
        flat = Plane(start - HALF if b else start + width - HALF, TILE, depth, total, True)

        def value(a, plane):
            ghost_tile = spread_tiles([side[a % 4 * planes + plane] for side in beside], a >= 4)
            ghost_tile = jnp.where(ghost_in, ghost_tile, 0.0)
            first = own[a][plane, pl.ds(0, TILE)].astype(jnp.float32)
            last = own[a][plane, pl.ds(width - TILE, TILE)].astype(jnp.float32)
            return edge_blocks(last, ghost_tile, first)[b]

        code, bunch = functools.partial(value, CODES), functools.partial(value, BUNCH)
        above = far_traces(flat, case, moved[1], value, code, bunch)[1]
        return above, near_traces(flat, case, planes, value, code, bunch)

    blocks = [block_traces(b) for b in range(2)]
    before = [v for pair in zip(blocks[0][0], blocks[1][0]) for v in pair]
    after = [v for pair in zip(blocks[0][1], blocks[1][1]) for v in pair]

    def fill(to_before, to_after):
        for n, v in enumerate(before):
            to_before[n] = v
        for n, v in enumerate(after):
            to_after[n] = v
        starts = corner_starts(case)
        for n in range(n_sides):
            if n_sides == 1:
                left_column = jnp.where(gx == 0, start + width, start - HALF)
            else:
                left_column = start - HALF if n == 0 else start + width
            whole, half = column_scales(left_column + jnp.where(row < HALF, row, row - HALF), total)
            at = len(before) + n * starts[-1]
            for a in range(4):
                count = starts[a + 1] - starts[a]
                to_before[pl.ds(at + starts[a], count)] = beside[n][pl.ds(a * planes, count)]
            plane = moves - 1
            tile = lambda a, plane: beside[n][a * planes + plane]
            to_before[at + starts[BX] + plane] = tile(BX, plane) + jnp.where(
                low, (TIME_STEP / whole) * tile(EY, moves), 0.0
            )
            to_before[at + plane] = tile(BY - 4, plane) - jnp.where(
                low, 0.0, turned((TIME_STEP / half) * tile(EX, moves))
            )
            base = 3 - moves
            for a in (2, 3):
                to = len(after) + (2 * n + a - 2) * base
                to_after[pl.ds(to, base)] = beside[n][pl.ds((a + 1) * planes - base, base)]

    @pl.when(even)
    def _():
        fill(off, on)

    @pl.when(jnp.logical_not(even))
    def _():
        fill(on, off)


def relay(case, moved, own, beside):
    planes, width, depth = own[0].shape
    count = 8 + len(beside) * corner_starts(case)[-1]
    return pl.pallas_call(
        functools.partial(relay_kernel, case, len(beside)),
        out_shape=[pltpu.VMEM((n, TILE, depth), jnp.float32) for n in (count + 1, count)],
        in_specs=[SMEM] + [VMEM] * (8 + len(beside)),
        out_specs=[VMEM] * 2,
        compiler_params=pltpu.CompilerParams(vmem_limit_bytes=32 * 2**20),
        name="relay",
    )(moved, *own, *beside)


def coefficients(code):
    kind = code.dtype.type
    five, six, seven = code == kind(5), code == kind(6), code == kind(7)
    keep = jnp.where(five, 0.0, jnp.where(six, 0.8 / 1.2, jnp.where(seven, 0.4 / 1.6, 1.0)))
    gain = jnp.where(
        five,
        0.0,
        jnp.where(six, TIME_STEP / 1.2, jnp.where(seven, TIME_STEP / 1.6, TIME_STEP)),
    )
    return keep, gain


def ghost_inside(width, depth):
    gx = lax.axis_index("gx")
    row = lax.broadcasted_iota(jnp.int32, (1, TILE, depth), 1)
    right = gx < lax.axis_size("gx") - 1
    return jnp.where(row < HALF, right.astype(jnp.int32), (gx > 0).astype(jnp.int32)) == 1


def spread_tiles(beside, upper):
    gx = lax.axis_index("gx")
    if len(beside) == 1:
        same = (gx > 0) if upper else (gx == 0)
        return jnp.where(same, beside[0], turned(beside[0]))
    from_left, from_right = beside
    if upper:
        from_right = turned(from_right)
    else:
        from_left = turned(from_left)
    return jnp.where(low_half(from_left.shape[-1]), from_right, from_left)


class Cells:
    def __init__(self, refs, width):
        self.ext, (self.keep, self.gain, self.current, self.rows) = refs[:6], refs[6:]
        self.width = width
        self.tall, self.depth = self.keep.shape[1:]
        self.ghost_in = ghost_inside(width, self.depth)

    def put(self, a, at, count, value, ghost):
        here = pl.ds(at, count)
        where = pl.ds(self.width, TILE) if ghost else pl.ds(0, self.width)
        mask = (lambda v: jnp.where(self.ghost_in, v, 0.0)) if ghost else (lambda v: v)
        if a < 6:
            self.ext[a][here, where] = mask(value)
        elif a == CODES:
            kept, gained = coefficients(value)
            self.keep[here, where], self.gain[here, where] = mask(kept), mask(gained)
        else:
            self.current[here, where] = CURRENT_SCALE * mask(value.astype(jnp.float32))

    def magnetic(self, e, count):
        ext, rows = self.ext, self.rows
        here, above = pl.ds(e, count), pl.ds(e + 1, count)
        ex, ey, es = ext[EX][here], ext[EY][here], ext[ES][here]
        bx = ext[BX][here] - (rows[4] * (next_y(es) - es) - rows[5] * (ext[EY][above] - ey))
        by = ext[BY][here] - rows[6] * ((ext[EX][above] - ex) - (next_x(rows[0] * es) - rows[0] * es))
        bs = ext[BS][here] - rows[4] * ((next_x(ey) - ey) - (next_y(ex) - ex))
        ext[BX][here], ext[BY][here], ext[BS][here] = bx, by, bs

    def electric(self, e, count, moved_now):
        ext, rows = self.ext, self.rows
        here, below, cells = pl.ds(e, count), pl.ds(e - 1, count), pl.ds(e - moved_now, count)
        bx, by, bs = ext[BX][here], ext[BY][here], ext[BS][here]
        kept, gained = self.keep[cells], self.gain[cells]
        ex = kept * ext[EX][here] + gained * ((bs - last_y(bs)) - rows[3] * (by - ext[BY][below]))
        ey = kept * ext[EY][here] + gained * (
            rows[2] * ((bx - ext[BX][below]) - (rows[1] * bs - last_x(rows[1] * bs)))
        )
        es = kept * ext[ES][here] + gained * (
            (by - last_x(by)) - (bx - last_y(bx)) - self.current[cells]
        )
        ext[EX][here], ext[EY][here], ext[ES][here] = ex, ey, es

    def leave(self, plane):
        for a in (BX, BY):
            self.ext[a][plane] = jnp.zeros((self.tall, self.depth), jnp.float32)


def in_groups(start, count, body):
    whole = max(count, 0) // GROUP
    if whole:

        @pl.loop(0, whole)
        def _(i):
            body(start + i * GROUP, GROUP)

    if count > 0 and count % GROUP:
        body(start + whole * GROUP, count % GROUP)


def prepare_kernel(moves, n_sides, moved, *refs):
    own, beside = refs[:8], refs[8 : 8 + n_sides]
    planes, width, depth = own[0].shape
    cells = Cells(refs[8 + n_sides :], width)
    tall, rows = cells.tall, cells.rows
    base = 3 - moves
    top = base + planes - 1
    total = width * lax.axis_size("gx")

    row = lax.broadcasted_iota(jnp.int32, (tall, depth), 0)
    place = lax.axis_index("gx") * width + jnp.where(row < width + HALF, row, row - tall)
    inside = (place >= 0) & (place < total)
    whole, half = column_scales(place, total)
    step = jnp.where(inside, TIME_STEP, 0.0)
    for n, value in enumerate((whole, half, 1.0 / whole, 1.0 / half, step, step / whole, step / half)):
        rows[n] = value
    for a in range(8):
        cells.put(a, base, planes, own[a][...], False)
        tiles = [side[pl.ds(a % 4 * planes, planes)] for side in beside]
        cells.put(a, base, planes, spread_tiles(tiles, a >= 4), True)
    for a in (EX, EY):
        cells.ext[a][0] = jnp.zeros((tall, depth), jnp.float32)
        cells.ext[a][planes + 3] = jnp.zeros((tall, depth), jnp.float32)

    moved_now = 0
    for t in range(STEPS):
        moved_now = moved_now + moved[t]
        in_groups(base + t, planes - 1 - 2 * t, cells.magnetic)

        @pl.when((lax.axis_index("gz") == 0) & (moved_now == t + 1))
        def _():
            cells.leave(base + t)

        in_groups(base + t + 1, planes - 2 - 2 * t, lambda e, n: cells.electric(e, n, moved_now))


def prepare(moves, moved, own, beside):
    planes, width, depth = own[0].shape
    tall = width + TILE
    vmem = lambda *shape: pltpu.VMEM(shape, jnp.float32)
    shapes = [vmem(planes + 4, tall, depth)] * 9
    shapes += [vmem(7, tall, depth)]
    return pl.pallas_call(
        functools.partial(prepare_kernel, moves, len(beside)),
        out_shape=shapes,
        in_specs=[SMEM] + [VMEM] * (8 + len(beside)),
        out_specs=[VMEM] * len(shapes),
        compiler_params=pltpu.CompilerParams(vmem_limit_bytes=32 * 2**20),
        cost_estimate=pl.CostEstimate(flops=22 * 10**8, bytes_accessed=10**7, transcendentals=0),
        name="prepare",
    )(moved, *own, *beside)


def steps_kernel(case, n_sides, planes, width, moved, *refs):
    rows, down, up, on, off = refs[9:14]
    outs = refs[14:20]
    cells = Cells((*refs[20:29], rows), width)
    sems = refs[29]
    ext = cells.ext
    moves = case[0]
    base = 3 - moves
    top = base + planes - 1
    far = planes + 3
    first = lax.axis_index("gz") == 0
    last = lax.axis_index("gz") == lax.axis_size("gz") - 1
    even = lax.axis_index("gz") % 2 == 0
    downs, ups = down_counts(case), up_counts(case)
    at, up_at = offsets(downs[:6]), [up_traces(case) + n for n in offsets(ups)]
    far_at = at[-1]
    at = at[:6] + [far_at + 4, far_at + 4 + downs[CODES]]
    copies = []

    def send(a, start, end):
        if end > start:
            item = pltpu.make_async_copy(
                ext[a].at[pl.ds(start, end - start), pl.ds(0, width)],
                outs[a].at[pl.ds(start - 3, end - start)],
                sems.at[len(copies)],
            )
            item.start()
            copies.append(item)

    for a in range(6):
        send(a, base + (2 if a >= BX else 3), top - 2)

    starts = corner_starts(case)

    def came(span, above):
        if above:
            return jnp.where(even, on[span], off[span])
        return jnp.where(even, off[span], on[span])

    def corner_above(a, count):
        at = [8 + n * starts[-1] + starts[a % 4] for n in range(n_sides)]
        return spread_tiles([came(pl.ds(n, count), True) for n in at], a >= 4)

    def corner_below(a, count):
        at = [2 * up_traces(case) + (2 * n + a % 4 - 1) * base - count for n in range(n_sides)]
        return spread_tiles([came(pl.ds(n, count), False) for n in at], a >= 4)

    for a in range(8):
        if downs[a]:
            cells.put(a, top + 1, downs[a], down[pl.ds(at[a], downs[a])], False)
            cells.put(a, top + 1, downs[a], corner_above(a, downs[a]), True)
        if ups[a]:
            cells.put(a, base - ups[a], ups[a], up[pl.ds(up_at[a], ups[a])], False)
            cells.put(a, base - ups[a], ups[a], corner_below(a, ups[a]), True)

    low = low_half(cells.depth)
    tile_row = lax.broadcasted_iota(jnp.int32, (TILE, cells.depth), 0)

    def trace(value, n, above):
        right_block, left_block = came(2 * n, above), came(2 * n + 1, above)
        at_right = jnp.where(tile_row >= TILE - 2, turned(right_block), value[width - TILE :])
        at_left = jnp.where(tile_row < 2, turned(left_block), value[:TILE])
        beyond = turned(jnp.where(low, left_block, right_block))
        return jnp.concatenate([at_left, value[TILE : width - TILE], at_right, beyond], 0)

    def far_first():
        for a in (EX, EY):
            ext[a][far] = jnp.where(last, 0.0, trace(down[far_at + a], a, True))

    def far_second(moved_now):
        ex, ey = trace(down[far_at + 2], 2, True), trace(down[far_at + 3], 3, True)
        if moves == 1:
            gained = cells.gain[far - moved_now]
            ex = ex + gained * (rows[3] * ext[BY][far - 1])
            ey = ey - gained * (rows[2] * ext[BX][far - 1])
        ext[EX][far], ext[EY][far] = jnp.where(last, 0.0, ex), jnp.where(last, 0.0, ey)

    def below_first(moved_now):
        bx, by = rows[5] * ext[EY][base], -rows[6] * ext[EX][base]
        ext[BX][base - 1] = trace(up[0], 0, False) + bx
        ext[BY][base - 1] = trace(up[1], 1, False) + by
        if moves == 2:
            return None
        gained = cells.gain[1 - moved_now]
        ex, ey = -gained * (rows[3] * by), gained * (rows[2] * bx)
        es = gained * ((by - last_x(by)) - (bx - last_y(bx)))
        weighted = rows[0] * es
        bx = bx - rows[4] * (next_y(es) - es) - rows[5] * ey
        by = by + rows[6] * (ex + next_x(weighted) - weighted)
        return trace(up[2], 2, False) + bx, trace(up[3], 3, False) + by

    def below_second(state):
        ext[BX][1] = state[0] + rows[5] * ext[EY][base]
        ext[BY][1] = state[1] - rows[6] * ext[EX][base]

    moved_now = 0
    for t in range(STEPS):
        moved_now = moved_now + moved[t]
        above = moves + 1 + t
        lowest, lowest_e = max(t, base), max(t + 1, base)
        if t == 0:
            below_state = below_first(moved_now)
        if base + t > lowest:
            cells.magnetic(lowest, base + t - lowest)
        cells.magnetic(top - t, above)
        if moves == 1 and t == 1:
            below_second(below_state)

        @pl.when(first)
        def _():
            cells.leave(base + moved_now - 1)

        if t == STEPS - 1:
            for a in (BX, BY, BS):
                send(a, 3, base + 2)
                send(a, top - 2, planes + 3)
        low_part = lowest_e, base + t + 1 - lowest_e
        if t < STEPS - 1:
            cells.electric(*low_part, moved_now)
            cells.electric(top - t, above, moved_now)
        else:
            cut = above // 2
            for start, count in ((top - 2, cut), (top - 2 + cut, above - cut), low_part):
                cells.electric(start, count, moved_now)
                for a in (EX, EY, ES):
                    send(a, start, start + count)
        if t == 0:
            far_first()
        elif t == 1:
            far_second(moved_now)
        if t < STEPS - 1:

            @pl.when(last)
            def _():
                for a in (EX, EY, ES):
                    ext[a][top + 1 + moved_now] = jnp.zeros((cells.tall, cells.depth), jnp.float32)

    for item in copies:
        item.wait()


def advance(case, n_sides, moved, shape, ready, ghosts):
    planes, width, depth = shape
    block = jax.ShapeDtypeStruct(shape, jnp.float32)
    n_in = 11 + len(ghosts)
    found = pl.pallas_call(
        functools.partial(steps_kernel, case, n_sides, planes, width),
        out_shape=[block] * 6 + [pltpu.VMEM(x.shape, x.dtype) for x in ready[:9]],
        in_specs=[SMEM] + [VMEM] * (n_in - 1),
        out_specs=[ANY] * 6 + [VMEM] * 9,
        input_output_aliases={1 + n: 6 + n for n in range(9)},
        scratch_shapes=[pltpu.SemaphoreType.DMA((21,))],
        compiler_params=pltpu.CompilerParams(vmem_limit_bytes=32 * 2**20),
        name="steps",
    )(moved, *ready, *ghosts)
    return tuple(found[:6])


def passed(block, to, sides=(0,)):
    size_z, size_x = lax.axis_size("gz"), lax.axis_size("gx")
    route = [
        (z * size_x + x, to(z) * size_x + x + dx)
        for z in range(size_z)
        for x in range(size_x)
        for dx in sides
        if 0 <= to(z) < size_z and 0 <= x + dx < size_x
    ]
    return lax.ppermute(block, ("gz", "gx"), route)


def on_device(*args):
    arrays, moved = args[:8], args[8]
    arrays = arrays[:6] + (arrays[7], arrays[6])
    sides = ("swap",) if lax.axis_size("gx") == 2 else ("right", "left")
    which, moved, sent = pack(arrays, moved)

    def run(c, own, sent, moved):
        case = CASES[c]
        down = passed(sent[c], lambda z: z - 1)
        across = edges(sides, own)
        ways = {"swap": (1, -1), "right": (1,), "left": (-1,)}
        beside = [passed(block, lambda z: z, ways[side]) for block, side in zip(across, sides)]
        up = passed(lift(case, own, across), lambda z: z + 1)
        on, off = relay(case, moved, own, beside)
        off = passed(off, lambda z: z + 1 if z % 2 else z - 1)
        on = passed(on, lambda z: z ^ 1)
        ready = prepare(case[0], moved, own, beside)
        return advance(case, len(sides), moved, own[0].shape, ready, [down, up, on, off])

    return lax.switch(
        which[0],
        [functools.partial(run, c) for c in range(len(CASES))],
        arrays,
        sent,
        moved,
    )


def solution(mesh):
    block = P("gz", "gx", None)
    return jax.shard_map(
        on_device,
        mesh=mesh,
        in_specs=(block,) * 8 + (P(),),
        out_specs=(block,) * 6,
        check_vma=False,
    )
```

```python
import functools

import jax
import jax.numpy as jnp
from jax import lax
from jax.experimental import pallas as pl
from jax.experimental.pallas import tpu as pltpu
from jax.sharding import PartitionSpec as P

STEPS = 3
TILE = 8
HALF = 4
GROUP = 4
TIME_STEP = 0.5
CURRENT_SCALE = 0.1
VMEM = pl.BlockSpec(memory_space=pltpu.VMEM)
SMEM = pl.BlockSpec(memory_space=pltpu.SMEM)
ANY = pl.BlockSpec(memory_space=pl.ANY)
EX, EY, ES, BX, BY, BS, CODES, BUNCH = range(8)
CASES = ((1, 1), (1, 0), (2, 1), (2, 0))


def down_counts(case):
    moves, now = case
    later = moves - now
    return (moves,) * 6 + (later + (moves == 1), later)


def up_counts(case):
    moves, now = case
    later = moves - now
    return (0,) * 6 + (2 - later, 1 if moves == 1 else 2 - later)


def up_traces(case):
    return 4 if case[0] == 1 else 2


def offsets(counts):
    starts = [0]
    for count in counts:
        starts.append(starts[-1] + count)
    return starts


def column_scales(place, total):
    place = place.astype(jnp.float32)
    whole = 1.0 + (place - total / 2) / (2 * total)
    half = 1.0 + (place + 0.5 - total / 2) / (2 * total)
    return whole, half


def turned(tiles):
    return pltpu.roll(tiles, HALF, tiles.ndim - 2)


def next_y(v):
    depth = v.shape[-1]
    lane = lax.broadcasted_iota(jnp.int32, v.shape[-2:], 1)
    return jnp.where(lane < depth - 1, pltpu.roll(v, depth - 1, v.ndim - 1), 0.0)


def last_y(v):
    lane = lax.broadcasted_iota(jnp.int32, v.shape[-2:], 1)
    return jnp.where(lane > 0, pltpu.roll(v, 1, v.ndim - 1), 0.0)


def next_x(v):
    return pltpu.roll(v, v.shape[-2] - 1, v.ndim - 2)


def last_x(v):
    return pltpu.roll(v, 1, v.ndim - 2)


def low_half(depth):
    return lax.broadcasted_iota(jnp.int32, (TILE, depth), 0) < HALF


class Plane:
    def __init__(self, start, width, depth, total, masked=False):
        column = start + lax.broadcasted_iota(jnp.int32, (width, depth), 0)
        self.inside = (column >= 0) & (column < total) if masked else None
        self.whole, self.half = column_scales(column, total)
        self.one_whole, self.one_half = 1.0 / self.whole, 1.0 / self.half
        self.step_whole, self.step_half = TIME_STEP * self.one_whole, TIME_STEP * self.one_half

    def kept(self, *values):
        if self.inside is None:
            return values
        return tuple(jnp.where(self.inside, v, 0.0) for v in values)

    def add_above(self, bx, by, ex, ey):
        return bx + self.step_whole * ey, by - self.step_half * ex

    def radial_vertical(self, bx, by, ex, ey, es):
        weighted = self.whole * es
        bx = bx - TIME_STEP * (next_y(es) - es) - self.step_whole * ey
        by = by + self.step_half * (ex + next_x(weighted) - weighted)
        return self.kept(bx, by)

    def longitudinal(self, bs, ex, ey):
        return self.kept(bs - TIME_STEP * ((next_x(ey) - ey) - (next_y(ex) - ex)))[0]

    def electric(self, ex, ey, bs, over_x, over_y, factors):
        kept, gained = factors
        weighted = self.half * bs
        ex = kept * ex + gained * ((bs - last_y(bs)) - self.one_half * over_y)
        ey = kept * ey + gained * (self.one_whole * (over_x - (weighted - last_x(weighted))))
        return self.kept(ex, ey)

    def electric_s(self, es, bx, by, bunch, factors):
        current = CURRENT_SCALE * bunch.astype(jnp.float32)
        es = factors[0] * es + factors[1] * ((by - last_x(by)) - (bx - last_y(bx)) - current)
        return self.kept(es)[0]


def far_traces(flat, case, second_move, field, code, bunch, ready=lambda arrays: None):
    far, first_move = case
    lowest = far - 1 if far == 1 else far - 2
    ready((EX, EY, ES))
    zeros, above_terms, own_terms, spin = (0.0, 0.0), {}, {}, {}
    for plane in range(lowest, far + 2):
        ex, ey = field(EX, plane), field(EY, plane)
        above_terms[plane] = flat.add_above(*zeros, field(EX, plane + 1), field(EY, plane + 1))
        own_terms[plane] = flat.radial_vertical(*above_terms[plane], ex, ey, field(ES, plane))
        if plane > lowest:
            spin[plane] = flat.longitudinal(0.0, ex, ey)
    ready((BX, BY, BS))
    now_b = {}
    for plane in range(lowest, far + 2):
        now_b[plane] = [field(a, plane) + v for a, v in zip((BX, BY), own_terms[plane])]
    folded = [field(a, far - 1) + v for a, v in zip((BX, BY), above_terms[far - 1])]
    ready((CODES, BUNCH))
    now_e, now_es, now_bs = {}, {}, {}
    for plane in range(lowest + 1, far + 2):
        ex, ey = field(EX, plane), field(EY, plane)
        now_bs[plane] = field(BS, plane) + spin[plane]
        factors = coefficients(code(plane - first_move))
        over = [up - under for up, under in zip(now_b[plane], now_b[plane - 1])]
        now_e[plane] = flat.electric(ex, ey, now_bs[plane], *over, factors)
        if plane <= far:
            now_es[plane] = flat.electric_s(
                field(ES, plane), *now_b[plane], bunch(plane - first_move), factors
            )

    def second(plane):
        next_b = flat.add_above(*now_b[plane], *now_e[plane + 1])
        return flat.radial_vertical(*next_b, *now_e[plane], now_es[plane])

    over = second(far)
    if far == 2:
        over = [up - under for up, under in zip(over, second(far - 1))]
    bs = flat.longitudinal(now_bs[far], *now_e[far])
    factors = coefficients(code(far - first_move - second_move))
    return folded, (*now_e[far], *flat.electric(*now_e[far], bs, *over, factors))


def near_traces(flat, case, planes, field, code, bunch):
    top = planes - 1
    ex, ey, es, bx, by, bs = (field(a, top) for a in range(6))
    first = flat.radial_vertical(bx, by, ex, ey, es)
    if case[0] == 2:
        return first
    under = flat.add_above(field(BX, top - 1), field(BY, top - 1), ex, ey)
    under = flat.radial_vertical(*under, *(field(a, top - 1) for a in (EX, EY, ES)))
    bs = flat.longitudinal(bs, ex, ey)
    factors = coefficients(code(top - case[1]))
    ex, ey = flat.electric(ex, ey, bs, first[0] - under[0], first[1] - under[1], factors)
    es = flat.electric_s(es, *first, bunch(top - case[1]), factors)
    return (*first, *flat.radial_vertical(*first, ex, ey, es))


def pack_kernel(*refs):
    sources, moved = refs[:8], refs[8]
    which, moved_here = refs[9:11]
    sent = refs[11 : 11 + len(CASES)]
    near, near_int, sems, moved_sem = refs[11 + len(CASES) :]
    _, _, width, depth = near.shape
    most = max(case[0] for case in CASES)
    fetched = (most + 3,) * 2 + (most + 2,) * 5 + (most + 1,)
    gx = lax.axis_index("gx")
    total = width * lax.axis_size("gx")

    get_moved = pltpu.make_async_copy(moved, moved_here, moved_sem)
    get_moved.start()
    copies = []
    for a in range(8):
        span = pl.ds(0, fetched[a])
        goal = near.at[a, span] if a < 6 else near_int.at[a - 6, span]
        copies.append(pltpu.make_async_copy(sources[a].at[span], goal, sems.at[a]))
        copies[-1].start()
    get_moved.wait()
    now = moved_here[0]
    later = moved_here[1] + moved_here[2]
    case_index = jnp.where(now + later == 1, 1 - now, 3 - now)
    which[0] = case_index

    flat = Plane(gx * width, width, depth, total)
    for c, case in enumerate(CASES):
        down = sent[c]
        downs = down_counts(case)
        at = offsets(downs[:6])
        far = case[0]

        @pl.when(case_index == c)
        def _():
            field = lambda a, plane: near[a, plane]

            folded, traces = far_traces(
                flat,
                case,
                moved_here[1],
                field,
                lambda plane: near_int[0, plane],
                lambda plane: near_int[1, plane],
                lambda arrays: [copies[a].wait() for a in arrays],
            )
            for a in range(6):
                down[pl.ds(at[a], far)] = near[a, :far]
            down[at[BX] + far - 1], down[at[BY] + far - 1] = folded
            place = at[-1]
            for v in traces:
                down[place] = v
                place += 1
            for n, a in enumerate((CODES, BUNCH)):
                if downs[a]:
                    down[pl.ds(place, downs[a])] = near_int[n, : downs[a]].astype(jnp.float32)
                place += downs[a]


def pack(arrays, moved):
    planes, width, depth = arrays[0].shape
    near = max(case[0] for case in CASES) + 3
    shapes = [pltpu.SMEM((1,), jnp.int32), pltpu.SMEM((STEPS,), jnp.int32)]
    for case in CASES:
        count = sum(down_counts(case)) + 4
        shapes.append(pltpu.VMEM((count, width, depth), jnp.float32))
    found = pl.pallas_call(
        pack_kernel,
        out_shape=shapes,
        in_specs=[ANY] * 9,
        out_specs=[SMEM] * 2 + [VMEM] * len(CASES),
        scratch_shapes=[
            pltpu.VMEM((6, near, width, depth), jnp.float32),
            pltpu.VMEM((2, near, width, depth), jnp.int32),
            pltpu.SemaphoreType.DMA((8,)),
            pltpu.SemaphoreType.DMA,
        ],
        compiler_params=pltpu.CompilerParams(vmem_limit_bytes=32 * 2**20),
        name="pack",
    )(*(pltpu.with_memory_space_constraint(a, pltpu.HBM) for a in (*arrays, moved)))
    return found[0], found[1], found[2:]


def edges_kernel(sides, *refs):
    own, across = refs[:8], refs[8:]
    planes, width, depth = own[0].shape
    gx = lax.axis_index("gx")
    low = low_half(depth)
    for n, side in enumerate(sides):
        if side == "swap":
            at, high = pl.multiple_of(jnp.where(gx == 0, width - TILE, 0), TILE), gx == 0
        else:
            at, high = (width - TILE, True) if side == "right" else (0, False)
        for a in range(4):
            first = own[a][:, pl.ds(at, TILE)]
            second = own[a + 4][:, pl.ds(at, TILE)].astype(jnp.float32)
            if side == "swap":
                first = jnp.where(high, turned(first), first)
                second = jnp.where(high, second, turned(second))
            elif high:
                first = turned(first)
            else:
                second = turned(second)
            across[n][pl.ds(a * planes, planes)] = jnp.where(low, first, second)


def edges(sides, own):
    planes, width, depth = own[0].shape
    return pl.pallas_call(
        functools.partial(edges_kernel, sides),
        out_shape=[pltpu.VMEM((4 * planes, TILE, depth), jnp.float32)] * len(sides),
        in_specs=[VMEM] * 8,
        out_specs=[VMEM] * len(sides),
        compiler_params=pltpu.CompilerParams(vmem_limit_bytes=32 * 2**20),
        name="edges",
    )(*own)


def lift_kernel(case, *refs):
    own, up = refs[:8], refs[-1]
    planes, width, depth = own[0].shape
    ups = up_counts(case)
    at = [up_traces(case) + n for n in offsets(ups)]
    flat = Plane(lax.axis_index("gx") * width, width, depth, width * lax.axis_size("gx"))
    for a in (CODES, BUNCH):
        if ups[a]:
            up[pl.ds(at[a], ups[a])] = own[a][planes - ups[a] :].astype(jnp.float32)
    values = near_traces(
        flat,
        case,
        planes,
        lambda a, plane: own[a][plane],
        lambda plane: own[CODES][plane],
        lambda plane: own[BUNCH][plane],
    )
    for n, v in enumerate(values):
        up[n] = v


def lift(case, own, after):
    planes, width, depth = own[0].shape
    count = sum(up_counts(case)) + up_traces(case)
    return pl.pallas_call(
        functools.partial(lift_kernel, case),
        out_shape=pltpu.VMEM((count, width, depth), jnp.float32),
        in_specs=[VMEM] * 8 + [ANY] * len(after),
        out_specs=VMEM,
        compiler_params=pltpu.CompilerParams(vmem_limit_bytes=32 * 2**20),
        cost_estimate=pl.CostEstimate(flops=10**7, bytes_accessed=10**7, transcendentals=0),
        name="lift",
    )(*own, *after)


def edge_blocks(right_tile, ghost_tile, left_tile):
    right_tile, ghost_tile, left_tile = turned(right_tile), turned(ghost_tile), turned(left_tile)
    low = low_half(right_tile.shape[-1])
    return jnp.where(low, right_tile, ghost_tile), jnp.where(low, ghost_tile, left_tile)


def corner_starts(case):
    moves = case[0]
    return offsets((moves, moves, moves + (moves == 1), moves))


def relay_kernel(case, n_sides, moved, *refs):
    own, beside, (on, off) = refs[:8], refs[8 : 8 + n_sides], refs[8 + n_sides :]
    planes, width, depth = own[0].shape
    moves = case[0]
    gx = lax.axis_index("gx")
    even = lax.axis_index("gz") % 2 == 0
    start = gx * width
    total = width * lax.axis_size("gx")
    low = low_half(depth)
    row = lax.broadcasted_iota(jnp.int32, (TILE, depth), 0)
    ghost_in = ghost_inside(width, depth)[0]

    def block_traces(b):
        flat = Plane(start - HALF if b else start + width - HALF, TILE, depth, total, True)

        def value(a, plane):
            ghost_tile = spread_tiles([side[a % 4 * planes + plane] for side in beside], a >= 4)
            ghost_tile = jnp.where(ghost_in, ghost_tile, 0.0)
            first = own[a][plane, pl.ds(0, TILE)].astype(jnp.float32)
            last = own[a][plane, pl.ds(width - TILE, TILE)].astype(jnp.float32)
            return edge_blocks(last, ghost_tile, first)[b]

        code, bunch = functools.partial(value, CODES), functools.partial(value, BUNCH)
        above = far_traces(flat, case, moved[1], value, code, bunch)[1]
        return above, near_traces(flat, case, planes, value, code, bunch)

    blocks = [block_traces(b) for b in range(2)]
    before = [v for pair in zip(blocks[0][0], blocks[1][0]) for v in pair]
    after = [v for pair in zip(blocks[0][1], blocks[1][1]) for v in pair]

    def fill(to_before, to_after):
        for n, v in enumerate(before):
            to_before[n] = v
        for n, v in enumerate(after):
            to_after[n] = v
        starts = corner_starts(case)
        for n in range(n_sides):
            if n_sides == 1:
                left_column = jnp.where(gx == 0, start + width, start - HALF)
            else:
                left_column = start - HALF if n == 0 else start + width
            whole, half = column_scales(left_column + jnp.where(row < HALF, row, row - HALF), total)
            at = len(before) + n * starts[-1]
            for a in range(4):
                count = starts[a + 1] - starts[a]
                to_before[pl.ds(at + starts[a], count)] = beside[n][pl.ds(a * planes, count)]
            plane = moves - 1
            tile = lambda a, plane: beside[n][a * planes + plane]
            to_before[at + starts[BX] + plane] = tile(BX, plane) + jnp.where(
                low, (TIME_STEP / whole) * tile(EY, moves), 0.0
            )
            to_before[at + plane] = tile(BY - 4, plane) - jnp.where(
                low, 0.0, turned((TIME_STEP / half) * tile(EX, moves))
            )
            base = 3 - moves
            for a in (2, 3):
                to = len(after) + (2 * n + a - 2) * base
                to_after[pl.ds(to, base)] = beside[n][pl.ds((a + 1) * planes - base, base)]

    @pl.when(even)
    def _():
        fill(off, on)

    @pl.when(jnp.logical_not(even))
    def _():
        fill(on, off)


def relay(case, moved, own, beside):
    planes, width, depth = own[0].shape
    count = 8 + len(beside) * corner_starts(case)[-1]
    return pl.pallas_call(
        functools.partial(relay_kernel, case, len(beside)),
        out_shape=[pltpu.VMEM((n, TILE, depth), jnp.float32) for n in (count + 1, count)],
        in_specs=[SMEM] + [VMEM] * (8 + len(beside)),
        out_specs=[VMEM] * 2,
        compiler_params=pltpu.CompilerParams(vmem_limit_bytes=32 * 2**20),
        name="relay",
    )(moved, *own, *beside)


def coefficients(code):
    kind = code.dtype.type
    five, six, seven = code == kind(5), code == kind(6), code == kind(7)
    keep = jnp.where(five, 0.0, jnp.where(six, 0.8 / 1.2, jnp.where(seven, 0.4 / 1.6, 1.0)))
    gain = jnp.where(
        five,
        0.0,
        jnp.where(six, TIME_STEP / 1.2, jnp.where(seven, TIME_STEP / 1.6, TIME_STEP)),
    )
    return keep, gain


def ghost_inside(width, depth):
    gx = lax.axis_index("gx")
    row = lax.broadcasted_iota(jnp.int32, (1, TILE, depth), 1)
    right = gx < lax.axis_size("gx") - 1
    return jnp.where(row < HALF, right.astype(jnp.int32), (gx > 0).astype(jnp.int32)) == 1


def spread_tiles(beside, upper):
    gx = lax.axis_index("gx")
    if len(beside) == 1:
        same = (gx > 0) if upper else (gx == 0)
        return jnp.where(same, beside[0], turned(beside[0]))
    from_left, from_right = beside
    if upper:
        from_right = turned(from_right)
    else:
        from_left = turned(from_left)
    return jnp.where(low_half(from_left.shape[-1]), from_right, from_left)


class Cells:
    def __init__(self, refs, width):
        self.ext, (self.keep, self.gain, self.current, self.rows) = refs[:6], refs[6:]
        self.width = width
        self.tall, self.depth = self.keep.shape[1:]
        self.ghost_in = ghost_inside(width, self.depth)

    def put(self, a, at, count, value, ghost):
        here = pl.ds(at, count)
        where = pl.ds(self.width, TILE) if ghost else pl.ds(0, self.width)
        mask = (lambda v: jnp.where(self.ghost_in, v, 0.0)) if ghost else (lambda v: v)
        if a < 6:
            self.ext[a][here, where] = mask(value)
        elif a == CODES:
            kept, gained = coefficients(value)
            self.keep[here, where], self.gain[here, where] = mask(kept), mask(gained)
        else:
            self.current[here, where] = CURRENT_SCALE * mask(value.astype(jnp.float32))

    def magnetic(self, e, count):
        ext, rows = self.ext, self.rows
        here, above = pl.ds(e, count), pl.ds(e + 1, count)
        ex, ey, es = ext[EX][here], ext[EY][here], ext[ES][here]
        bx = ext[BX][here] - (rows[4] * (next_y(es) - es) - rows[5] * (ext[EY][above] - ey))
        by = ext[BY][here] - rows[6] * ((ext[EX][above] - ex) - (next_x(rows[0] * es) - rows[0] * es))
        bs = ext[BS][here] - rows[4] * ((next_x(ey) - ey) - (next_y(ex) - ex))
        ext[BX][here], ext[BY][here], ext[BS][here] = bx, by, bs

    def electric(self, e, count, moved_now):
        ext, rows = self.ext, self.rows
        here, below, cells = pl.ds(e, count), pl.ds(e - 1, count), pl.ds(e - moved_now, count)
        bx, by, bs = ext[BX][here], ext[BY][here], ext[BS][here]
        kept, gained = self.keep[cells], self.gain[cells]
        ex = kept * ext[EX][here] + gained * ((bs - last_y(bs)) - rows[3] * (by - ext[BY][below]))
        ey = kept * ext[EY][here] + gained * (
            rows[2] * ((bx - ext[BX][below]) - (rows[1] * bs - last_x(rows[1] * bs)))
        )
        es = kept * ext[ES][here] + gained * (
            (by - last_x(by)) - (bx - last_y(bx)) - self.current[cells]
        )
        ext[EX][here], ext[EY][here], ext[ES][here] = ex, ey, es

    def leave(self, plane):
        for a in (BX, BY):
            self.ext[a][plane] = jnp.zeros((self.tall, self.depth), jnp.float32)


def in_groups(start, count, body):
    whole = max(count, 0) // GROUP
    if whole:

        @pl.loop(0, whole)
        def _(i):
            body(start + i * GROUP, GROUP)

    if count > 0 and count % GROUP:
        body(start + whole * GROUP, count % GROUP)


def prepare_kernel(moves, n_sides, moved, *refs):
    own, beside = refs[:8], refs[8 : 8 + n_sides]
    planes, width, depth = own[0].shape
    cells = Cells(refs[8 + n_sides :], width)
    tall, rows = cells.tall, cells.rows
    base = 3 - moves
    top = base + planes - 1
    total = width * lax.axis_size("gx")

    row = lax.broadcasted_iota(jnp.int32, (tall, depth), 0)
    place = lax.axis_index("gx") * width + jnp.where(row < width + HALF, row, row - tall)
    inside = (place >= 0) & (place < total)
    whole, half = column_scales(place, total)
    step = jnp.where(inside, TIME_STEP, 0.0)
    for n, value in enumerate((whole, half, 1.0 / whole, 1.0 / half, step, step / whole, step / half)):
        rows[n] = value
    for a in range(8):
        cells.put(a, base, planes, own[a][...], False)
        tiles = [side[pl.ds(a % 4 * planes, planes)] for side in beside]
        cells.put(a, base, planes, spread_tiles(tiles, a >= 4), True)
    for a in (EX, EY):
        cells.ext[a][0] = jnp.zeros((tall, depth), jnp.float32)
        cells.ext[a][planes + 3] = jnp.zeros((tall, depth), jnp.float32)

    moved_now = 0
    for t in range(STEPS):
        moved_now = moved_now + moved[t]
        in_groups(base + t, planes - 1 - 2 * t, cells.magnetic)

        @pl.when((lax.axis_index("gz") == 0) & (moved_now == t + 1))
        def _():
            cells.leave(base + t)

        in_groups(base + t + 1, planes - 2 - 2 * t, lambda e, n: cells.electric(e, n, moved_now))


def prepare(moves, moved, own, beside):
    planes, width, depth = own[0].shape
    tall = width + TILE
    vmem = lambda *shape: pltpu.VMEM(shape, jnp.float32)
    shapes = [vmem(planes + 4, tall, depth)] * 9
    shapes += [vmem(7, tall, depth)]
    return pl.pallas_call(
        functools.partial(prepare_kernel, moves, len(beside)),
        out_shape=shapes,
        in_specs=[SMEM] + [VMEM] * (8 + len(beside)),
        out_specs=[VMEM] * len(shapes),
        compiler_params=pltpu.CompilerParams(vmem_limit_bytes=32 * 2**20),
        cost_estimate=pl.CostEstimate(flops=22 * 10**8, bytes_accessed=10**7, transcendentals=0),
        name="prepare",
    )(moved, *own, *beside)


def steps_kernel(case, n_sides, planes, width, moved, *refs):
    rows, down, up, on, off = refs[9:14]
    outs = refs[14:20]
    cells = Cells((*refs[20:29], rows), width)
    sems = refs[29]
    ext = cells.ext
    moves = case[0]
    base = 3 - moves
    top = base + planes - 1
    far = planes + 3
    first = lax.axis_index("gz") == 0
    last = lax.axis_index("gz") == lax.axis_size("gz") - 1
    even = lax.axis_index("gz") % 2 == 0
    downs, ups = down_counts(case), up_counts(case)
    at, up_at = offsets(downs[:6]), [up_traces(case) + n for n in offsets(ups)]
    far_at = at[-1]
    at = at[:6] + [far_at + 4, far_at + 4 + downs[CODES]]
    copies = []

    def send(a, start, end):
        if end > start:
            item = pltpu.make_async_copy(
                ext[a].at[pl.ds(start, end - start), pl.ds(0, width)],
                outs[a].at[pl.ds(start - 3, end - start)],
                sems.at[len(copies)],
            )
            item.start()
            copies.append(item)

    for a in range(6):
        send(a, base + (2 if a >= BX else 3), top - 2)

    starts = corner_starts(case)

    def came(span, above):
        if above:
            return jnp.where(even, on[span], off[span])
        return jnp.where(even, off[span], on[span])

    def corner_above(a, count):
        at = [8 + n * starts[-1] + starts[a % 4] for n in range(n_sides)]
        return spread_tiles([came(pl.ds(n, count), True) for n in at], a >= 4)

    def corner_below(a, count):
        at = [2 * up_traces(case) + (2 * n + a % 4 - 1) * base - count for n in range(n_sides)]
        return spread_tiles([came(pl.ds(n, count), False) for n in at], a >= 4)

    for a in range(8):
        if downs[a]:
            cells.put(a, top + 1, downs[a], down[pl.ds(at[a], downs[a])], False)
            cells.put(a, top + 1, downs[a], corner_above(a, downs[a]), True)
        if ups[a]:
            cells.put(a, base - ups[a], ups[a], up[pl.ds(up_at[a], ups[a])], False)
            cells.put(a, base - ups[a], ups[a], corner_below(a, ups[a]), True)

    low = low_half(cells.depth)
    tile_row = lax.broadcasted_iota(jnp.int32, (TILE, cells.depth), 0)

    def trace(value, n, above):
        right_block, left_block = came(2 * n, above), came(2 * n + 1, above)
        at_right = jnp.where(tile_row >= TILE - 2, turned(right_block), value[width - TILE :])
        at_left = jnp.where(tile_row < 2, turned(left_block), value[:TILE])
        beyond = turned(jnp.where(low, left_block, right_block))
        return jnp.concatenate([at_left, value[TILE : width - TILE], at_right, beyond], 0)

    def far_first():
        for a in (EX, EY):
            ext[a][far] = jnp.where(last, 0.0, trace(down[far_at + a], a, True))

    def far_second(moved_now):
        ex, ey = trace(down[far_at + 2], 2, True), trace(down[far_at + 3], 3, True)
        if moves == 1:
            gained = cells.gain[far - moved_now]
            ex = ex + gained * (rows[3] * ext[BY][far - 1])
            ey = ey - gained * (rows[2] * ext[BX][far - 1])
        ext[EX][far], ext[EY][far] = jnp.where(last, 0.0, ex), jnp.where(last, 0.0, ey)

    def below_first(moved_now):
        bx, by = rows[5] * ext[EY][base], -rows[6] * ext[EX][base]
        ext[BX][base - 1] = trace(up[0], 0, False) + bx
        ext[BY][base - 1] = trace(up[1], 1, False) + by
        if moves == 2:
            return None
        gained = cells.gain[1 - moved_now]
        ex, ey = -gained * (rows[3] * by), gained * (rows[2] * bx)
        es = gained * ((by - last_x(by)) - (bx - last_y(bx)))
        weighted = rows[0] * es
        bx = bx - rows[4] * (next_y(es) - es) - rows[5] * ey
        by = by + rows[6] * (ex + next_x(weighted) - weighted)
        return trace(up[2], 2, False) + bx, trace(up[3], 3, False) + by

    def below_second(state):
        ext[BX][1] = state[0] + rows[5] * ext[EY][base]
        ext[BY][1] = state[1] - rows[6] * ext[EX][base]

    moved_now = 0
    for t in range(STEPS):
        moved_now = moved_now + moved[t]
        above = moves + 1 + t
        lowest, lowest_e = max(t, base), max(t + 1, base)
        if t == 0:
            below_state = below_first(moved_now)
        if base + t > lowest:
            cells.magnetic(lowest, base + t - lowest)
        cells.magnetic(top - t, above)
        if moves == 1 and t == 1:
            below_second(below_state)

        @pl.when(first)
        def _():
            cells.leave(base + moved_now - 1)

        if t == STEPS - 1:
            for a in (BX, BY, BS):
                send(a, 3, base + 2)
                send(a, top - 2, planes + 3)
        low_part = lowest_e, base + t + 1 - lowest_e
        if t < STEPS - 1:
            cells.electric(*low_part, moved_now)
            cells.electric(top - t, above, moved_now)
        else:
            cut = (2 * above + 2) // 3
            for start, count in ((top - 2, cut), (top - 2 + cut, above - cut), low_part):
                cells.electric(start, count, moved_now)
                for a in (EX, EY, ES):
                    send(a, start, start + count)
        if t == 0:
            far_first()
        elif t == 1:
            far_second(moved_now)
        if t < STEPS - 1:

            @pl.when(last)
            def _():
                for a in (EX, EY, ES):
                    ext[a][top + 1 + moved_now] = jnp.zeros((cells.tall, cells.depth), jnp.float32)

    for item in copies:
        item.wait()


def advance(case, n_sides, moved, shape, ready, ghosts):
    planes, width, depth = shape
    block = jax.ShapeDtypeStruct(shape, jnp.float32)
    n_in = 11 + len(ghosts)
    found = pl.pallas_call(
        functools.partial(steps_kernel, case, n_sides, planes, width),
        out_shape=[block] * 6 + [pltpu.VMEM(x.shape, x.dtype) for x in ready[:9]],
        in_specs=[SMEM] + [VMEM] * (n_in - 1),
        out_specs=[ANY] * 6 + [VMEM] * 9,
        input_output_aliases={1 + n: 6 + n for n in range(9)},
        scratch_shapes=[pltpu.SemaphoreType.DMA((21,))],
        compiler_params=pltpu.CompilerParams(vmem_limit_bytes=32 * 2**20),
        name="steps",
    )(moved, *ready, *ghosts)
    return tuple(found[:6])


def passed(block, to, sides=(0,)):
    size_z, size_x = lax.axis_size("gz"), lax.axis_size("gx")
    route = [
        (z * size_x + x, to(z) * size_x + x + dx)
        for z in range(size_z)
        for x in range(size_x)
        for dx in sides
        if 0 <= to(z) < size_z and 0 <= x + dx < size_x
    ]
    return lax.ppermute(block, ("gz", "gx"), route)


def on_device(*args):
    arrays, moved = args[:8], args[8]
    arrays = arrays[:6] + (arrays[7], arrays[6])
    sides = ("swap",) if lax.axis_size("gx") == 2 else ("right", "left")
    which, moved, sent = pack(arrays, moved)

    def run(c, own, sent, moved):
        case = CASES[c]
        down = passed(sent[c], lambda z: z - 1)
        across = edges(sides, own)
        ways = {"swap": (1, -1), "right": (1,), "left": (-1,)}
        beside = [passed(block, lambda z: z, ways[side]) for block, side in zip(across, sides)]
        up = passed(lift(case, own, across), lambda z: z + 1)
        on, off = relay(case, moved, own, beside)
        off = passed(off, lambda z: z + 1 if z % 2 else z - 1)
        on = passed(on, lambda z: z ^ 1)
        ready = prepare(case[0], moved, own, beside)
        return advance(case, len(sides), moved, own[0].shape, ready, [down, up, on, off])

    return lax.switch(
        which[0],
        [functools.partial(run, c) for c in range(len(CASES))],
        arrays,
        sent,
        moved,
    )


def solution(mesh):
    block = P("gz", "gx", None)
    return jax.shard_map(
        on_device,
        mesh=mesh,
        in_specs=(block,) * 8 + (P(),),
        out_specs=(block,) * 6,
        check_vma=False,
    )
```
